32 devices in a mesh: dp: 8 (over z, y), mp: 4 (over x, core).
Axes of the slice: x: 2, y: 2, z: 4, core: 2. Of those that a mesh axis runs over, the one named last changes fastest.
Arguments:
- inputs: bfloat16 [4, 512, 1024], P(None, 'dp'), may hold values from -8 to 8
- depth_counts: int32 [512], P('dp'), may hold values from 2 to 4, as said below
- out_grad: bfloat16 [4, 512, 1024], P(None, 'dp'), may hold values from -8 to 8
- attn_weight: float32 [1024, 4, 4, 1024], P('dp', None, None, 'mp'), may hold values from -0.26516504 to 0.26516504
- attn_first: float32 [1024, 4, 4, 1024], P('dp', None, None, 'mp'), may hold values from -0.0007324219 to 0.0007324219
- attn_second: float32 [1024, 4, 4, 1024], P('dp', None, None, 'mp'), may hold values from 1.4901161e-08 to 5.9604645e-08
- ffn_weight: float32 [1024, 3, 4, 4096], P('dp', None, None, 'mp'), may hold values from -0.125 to 0.125
- ffn_first: float32 [1024, 3, 4, 4096], P('dp', None, None, 'mp'), may hold values from -0.0007324219 to 0.0007324219
- ffn_second: float32 [1024, 3, 4, 4096], P('dp', None, None, 'mp'), may hold values from 1.4901161e-08 to 5.9604645e-08
- norm_gains: float32 [2, 1024], replicated, may hold values from 0.25 to 1.75
- gain_first: float32 [2, 1024], replicated, may hold values from -0.00390625 to 0.00390625
- gain_second: float32 [2, 1024], replicated, may hold values from 3.7252903e-07 to 1.4901161e-06
Outputs:
- output: bfloat16 [4, 512, 1024], P(None, 'dp')
- input_grad: bfloat16 [4, 512, 1024], P(None, 'dp')
- grad_norm: float32 [], replicated
- attn_weight_new: float32 [1024, 4, 4, 1024], P('dp', None, None, 'mp')
- attn_first_new: float32 [1024, 4, 4, 1024], P('dp', None, None, 'mp')
- attn_second_new: float32 [1024, 4, 4, 1024], P('dp', None, None, 'mp')
- ffn_weight_new: float32 [1024, 3, 4, 4096], P('dp', None, None, 'mp')
- ffn_first_new: float32 [1024, 3, 4, 4096], P('dp', None, None, 'mp')
- ffn_second_new: float32 [1024, 3, 4, 4096], P('dp', None, None, 'mp')
- gains_new: float32 [2, 1024], replicated
- gain_first_new: float32 [2, 1024], replicated
- gain_second_new: float32 [2, 1024], replicated
The draws below stay inside these ranges and needn't reach their ends.
Inputs may be any that keep to these rules, and one draw needn't show every extreme that they name: `depth_counts`: every count is 2 or 4; among the 64 frames of one device at most 48 have count 4, and in every draw some device has exactly 48.
All inputs are finite; a program needn't handle non-finite values.
Results may differ from the reference program's by a relative error of at most 0.012.
Values may be sent and summed in bfloat16 or wider, within the bound.
No kernel may reach another device: no remote copies, remote signals or barrier semaphores. Data moves between devices by JAX's collectives and lax.ppermute only.
A program may use at most 384 MiB of HBM per device.

```python
import math
import jax
import jax.numpy as jnp
from jax import lax

D = 1024
HEADS = 16
HD = 64
FF = 4096
DEPTH = 4
STEP = 5
FR_DEV = 64
CAP = 48
FRAMES = 512


def draw_depth_counts(key, part):
    key = jax.random.fold_in(key, 7)
    blocks = FRAMES // FR_DEV
    key_count, key_full, key_rank = jax.random.split(key, 3)
    deep_total = jax.random.randint(key_count, (blocks,), FR_DEV // 8, CAP + 1)
    full_block = jax.random.randint(key_full, (), 0, blocks)
    deep_total = jnp.where(jnp.arange(blocks) == full_block, CAP, deep_total)
    ranking = jax.vmap(lambda subkey: jax.random.permutation(subkey, FR_DEV))(jax.random.split(key_rank, blocks))
    deep_rows = ranking < deep_total[:, None]
    return jnp.where(deep_rows, DEPTH, DEPTH // 2).reshape(FRAMES).astype(jnp.int32)


def draw_attn_weight(key, part):
    key = jax.random.fold_in(key, 11)
    columns = HEADS * HD
    array_shape = (D, 4, DEPTH, columns)
    entries = jax.random.truncated_normal(key, -4.0, 4.0, array_shape, jnp.float32)
    low_end = 0.5
    rising = low_end + jnp.arange(columns, dtype=jnp.float32) / columns
    inner = jnp.full((columns,), D ** (-0.5), jnp.float32)
    factor = jnp.stack([inner, inner, inner, rising * (columns // 2) ** (-0.5)])
    return entries * factor[None, :, None, :]


def draw_ffn_weight(key, part):
    key = jax.random.fold_in(key, 13)
    array_shape = (D, 3, DEPTH, FF)
    entries = jax.random.truncated_normal(key, -4.0, 4.0, array_shape, jnp.float32)
    low_end = 0.5
    rising = low_end + jnp.arange(FF, dtype=jnp.float32) / FF
    inner = jnp.full((FF,), D ** (-0.5), jnp.float32)
    factor = jnp.stack([inner, inner, rising * FF ** (-0.5)])
    return entries * factor[None, :, None, :]


def draw_norm_gains(key, part):
    key = jax.random.fold_in(key, 17)
    entries = jax.random.uniform(key, (2, D), jnp.float32, 0.85, 1.15)
    low_end = 0.5
    rising = low_end + jnp.arange(D, dtype=jnp.float32) / D
    return entries * rising[None, :]


def strengthened(drawn, key, source, target, shards_of, factor):
    def block_of(position):
        return (jnp.arange(drawn.shape[position]) // (drawn.shape[position] // shards_of)).reshape((-1,) + (1,) * (drawn.ndim - 1 - position))

    first = jax.random.permutation(key, shards_of)[block_of(target)]
    far = (block_of(target) + shards_of // 2) % shards_of
    return jnp.where((block_of(source) == first) | (block_of(source) == far), factor * drawn, drawn)


def levels(stream_key, extent, pieces, least, high):
    def one(axis_at, blocks):
        steps = jax.random.uniform(jax.random.fold_in(jax.random.fold_in(stream_key, 6), axis_at), (blocks,), jnp.float32, least / len(pieces), high / len(pieces))
        return jnp.repeat(jnp.exp(steps), extent[axis_at] // blocks).reshape((-1,) + (1,) * (len(extent) - axis_at - 1))

    loudness = one(*pieces[0])
    for cut in pieces[1:]:
        loudness = loudness * one(*cut)
    return loudness


def scatter_about(key, dims, width, bound, pieces=(), held_as=jnp.bfloat16):
    drawn = width * jax.random.normal(key, dims, jnp.float32)
    if pieces:
        drawn = drawn * levels(key, dims, pieces, -0.22, 0.18)
    return jnp.clip(drawn, -bound, bound).astype(held_as)


def noise_with(rng, shape, spread, reach, cuts, heavy, kind=jnp.bfloat16):
    result = spread * jax.random.normal(rng, shape, jnp.float32)
    if cuts:
        result = result * levels(rng, shape, cuts, -0.22, 0.18)
    return jnp.clip(strengthened(result, jax.random.fold_in(rng, 3), *heavy), -reach, reach).astype(kind)


def setup_inputs(seed: int = 0) -> dict:
    keys = jax.random.split(jax.random.key(seed), 13)
    inputs = noise_with(keys[0], (DEPTH, FRAMES, D), 1.0, 8.0, ((1, 8),), (1, 2, 8, 2.0))
    depth_counts = draw_depth_counts(jax.random.fold_in(keys[12], 71), 0)
    out_grad = noise_with(keys[2], (DEPTH, FRAMES, D), 1.0, 8.0, ((1, 8),), (1, 2, 8, 2.0))
    attn_weight = draw_attn_weight(jax.random.fold_in(keys[12], 71), 0)
    attn_first = scatter_about(keys[4], (D, 4, DEPTH, HEADS * HD), ((D * DEPTH * (4 * HEADS * HD + 3 * FF)) ** -0.5), 0.0007324219, ((0, 8), (3, 4)), jnp.float32)
    attn_second = jnp.clip(jnp.exp(math.log(5.960464477539063e-08) - 1.3862944 * jax.random.uniform(keys[5], (D, 4, DEPTH, HEADS * HD), jnp.float32) ** levels(keys[5], (D, 4, DEPTH, HEADS * HD), ((0, 8), (3, 4)), -0.2, 0.2)), 1.4901161193847656e-08, 5.960464477539063e-08)
    ffn_weight = draw_ffn_weight(jax.random.fold_in(keys[12], 71), 0)
    ffn_first = scatter_about(keys[7], (D, 3, DEPTH, FF), ((D * DEPTH * (4 * HEADS * HD + 3 * FF)) ** -0.5), 0.0007324219, ((0, 8), (3, 4)), jnp.float32)
    ffn_second = jnp.clip(jnp.exp(math.log(5.960464477539063e-08) - 1.3862944 * jax.random.uniform(keys[8], (D, 3, DEPTH, FF), jnp.float32) ** levels(keys[8], (D, 3, DEPTH, FF), ((0, 8), (3, 4)), -0.2, 0.2)), 1.4901161193847656e-08, 5.960464477539063e-08)
    norm_gains = draw_norm_gains(jax.random.fold_in(keys[12], 71), 0)
    gain_first = scatter_about(keys[10], (2, D), (5 * (D * DEPTH * (4 * HEADS * HD + 3 * FF)) ** -0.5), 0.00390625, (), jnp.float32)
    gain_second = jnp.clip(jnp.exp(jax.random.uniform(keys[11], (2, D), jnp.float32, math.log(3.725290298461914e-07), math.log(1.4901161193847656e-06))), 3.725290298461914e-07, 1.4901161193847656e-06)
    return {"inputs": inputs, "depth_counts": depth_counts, "out_grad": out_grad, "attn_weight": attn_weight, "attn_first": attn_first, "attn_second": attn_second, "ffn_weight": ffn_weight, "ffn_first": ffn_first, "ffn_second": ffn_second, "norm_gains": norm_gains, "gain_first": gain_first, "gain_second": gain_second}


NORM_EPS = 1e-05
BETA_ONE = 0.5
BETA_TWO = 0.5
LEARN_RATE = 0.02
GAIN_RATE = 0.4
WEIGHT_DECAY = 0.1
ADAM_EPS = 1e-08
CLIP_NORM = 1.0
MAXIMAL_ACCURACY = lax.Precision.HIGHEST

@jax.custom_vjp
def low(v):
    return lax.optimization_barrier(v.astype(jnp.bfloat16)).astype(jnp.float32)

@jax.custom_vjp
def lower_part_backward(v):
    return v

def low_keep(v):
    return (low(v), None)

def low_pass(kept, grad):
    return (grad,)

def back_keep(v):
    return (v, None)

def back_low(kept, grad):
    return (low(grad),)
low.defvjp(low_keep, low_pass)
lower_part_backward.defvjp(back_keep, back_low)

def rms_norm(values, gain):
    unit_rows = values * lax.rsqrt(lax.optimization_barrier(jnp.mean(values * values, axis=-1, keepdims=True)) + NORM_EPS)
    return low(unit_rows * gain)

def split_heads(values):
    return values.reshape(values.shape[0], values.shape[1], -1, HD)

def layer_forward(frames_in, counts_block, attn_weight, ffn_weight, norm_gains):
    depth_mask = (jnp.arange(DEPTH)[:, None] < counts_block[None, :]).astype(jnp.float32)[:, :, None]
    attention_lower_part = low(attn_weight)
    feedforward_lower_part = low(ffn_weight)
    normed_attn = rms_norm(frames_in, norm_gains[0])
    projected = low(jnp.einsum('pfd,dkpc->kpfc', normed_attn, attention_lower_part[:, 0:3], precision=MAXIMAL_ACCURACY))
    queries = lower_part_backward(projected[0])
    key_rows = lower_part_backward(projected[1])
    value_rows = lower_part_backward(projected[2])
    scores = jnp.einsum('pfhe,jfhe->fhpj', split_heads(queries), split_heads(key_rows), precision=MAXIMAL_ACCURACY)
    scores = lower_part_backward(scores * HD ** (-0.5))
    causal = jnp.arange(DEPTH)[:, None] >= jnp.arange(DEPTH)[None, :]
    masked = jnp.where(causal, scores, -1e+30)
    row_top = lax.optimization_barrier(jnp.max(masked, axis=-1, keepdims=True))
    expo_terms = jnp.exp(masked - row_top)
    soft_probs = low(expo_terms / lax.optimization_barrier(jnp.sum(expo_terms, axis=-1, keepdims=True)))
    context_values = jnp.einsum('fhpj,jfhe->pfhe', soft_probs, split_heads(value_rows), precision=MAXIMAL_ACCURACY)
    context_values = lower_part_backward(low(context_values.reshape(queries.shape)))
    attention_output = lower_part_backward(jnp.einsum('vzi,kvi->vzk', context_values, attention_lower_part[:, 3], precision=MAXIMAL_ACCURACY))
    hidden_in = frames_in + depth_mask * attention_output
    normed_ffn = rms_norm(hidden_in, norm_gains[1])
    gate_up = jnp.einsum('pfd,dkpc->kpfc', normed_ffn, feedforward_lower_part[:, 0:2], precision=MAXIMAL_ACCURACY)
    gate_pre = lower_part_backward(gate_up[0])
    up_proj = lower_part_backward(gate_up[1])
    saved_activations = low(jax.nn.silu(gate_pre) * up_proj)
    feedforward_output = lower_part_backward(jnp.einsum('vzi,kvi->vzk', saved_activations, feedforward_lower_part[:, 2], precision=MAXIMAL_ACCURACY))
    return hidden_in + depth_mask * feedforward_output

def adamw_update(weights, first, second, grads, clip_factor, decay_rate, step_rate):
    clipped = clip_factor * grads
    first_new = BETA_ONE * first + (1.0 - BETA_ONE) * clipped
    second_new = BETA_TWO * second + (1.0 - BETA_TWO) * clipped * clipped
    first_hat = first_new / (1.0 - BETA_ONE ** STEP)
    second_hat = second_new / (1.0 - BETA_TWO ** STEP)
    new_weights = weights - step_rate * (first_hat / (jnp.sqrt(second_hat) + ADAM_EPS) + decay_rate * weights)
    return (new_weights, first_new, second_new)

def reference(inputs, depth_counts, out_grad, attn_weight, attn_first, attn_second, ffn_weight, ffn_first, ffn_second, norm_gains, gain_first, gain_second):
    blocks = FRAMES // FR_DEV

    def to_blocks(values):
        return jnp.swapaxes(values.reshape(DEPTH, blocks, FR_DEV, D), 0, 1)

    def from_blocks(values):
        return jnp.swapaxes(values, 0, 1).reshape(DEPTH, FRAMES, D)

    def block_step(totals, block_items):
        block_in, block_grad, block_counts = block_items

        def closed(frames_in, attn_w, ffn_w, gains_w):
            return layer_forward(frames_in, block_counts, attn_w, ffn_w, gains_w)
        block_out, pullback = jax.vjp(closed, block_in.astype(jnp.float32), attn_weight, ffn_weight, norm_gains)
        grad_in, grad_attn, grad_ffn, grad_gain = pullback(block_grad.astype(jnp.float32))
        totals = (totals[0] + grad_attn, totals[1] + grad_ffn, totals[2] + grad_gain)
        return (totals, (block_out.astype(jnp.bfloat16), grad_in.astype(jnp.bfloat16)))
    zero_grads = (jnp.zeros_like(attn_weight), jnp.zeros_like(ffn_weight), jnp.zeros_like(norm_gains))
    block_inputs = (to_blocks(inputs), to_blocks(out_grad), depth_counts.reshape(blocks, FR_DEV))
    (attn_grad, ffn_grad, gain_grad), (out_blocks, grad_blocks) = lax.scan(block_step, zero_grads, block_inputs)
    grad_norm = jnp.sqrt(jnp.sum(attn_grad * attn_grad) + jnp.sum(ffn_grad * ffn_grad) + jnp.sum(gain_grad * gain_grad))
    clip_factor = CLIP_NORM / jnp.maximum(grad_norm, CLIP_NORM)
    attn_new = adamw_update(attn_weight, attn_first, attn_second, attn_grad, clip_factor, WEIGHT_DECAY, LEARN_RATE)
    ffn_new = adamw_update(ffn_weight, ffn_first, ffn_second, ffn_grad, clip_factor, WEIGHT_DECAY, LEARN_RATE)
    gain_new = adamw_update(norm_gains, gain_first, gain_second, gain_grad, clip_factor, 0.0, GAIN_RATE)
    return (from_blocks(out_blocks), from_blocks(grad_blocks), grad_norm, attn_new[0], attn_new[1], attn_new[2], ffn_new[0], ffn_new[1], ffn_new[2], gain_new[0], gain_new[1], gain_new[2])
```

```python
import math

import jax
import jax.numpy as jnp
from jax import lax
from jax.sharding import Mesh, PartitionSpec as P

HD = 64
STEP = 5
NORM_EPS = 1e-05
BETA_ONE = 0.5
BETA_TWO = 0.5
LEARN_RATE = 0.02
GAIN_RATE = 0.4
WEIGHT_DECAY = 0.1
ADAM_EPS = 1e-08
CLIP_NORM = 1.0

BF = jnp.bfloat16
F32 = jnp.float32


def axis_total(axes):
    return math.prod(lax.axis_size(a) for a in axes)


def linear_index(axes):
    index = 0
    for a in axes:
        index = index * lax.axis_size(a) + lax.axis_index(a)
    return index


def hop(value, axes, step):
    n = axis_total(axes)
    return lax.ppermute(value, axes, [(i, i ^ step) for i in range(n)])


def take(stack, index):
    return lax.dynamic_index_in_dim(stack, index, 0, keepdims=False)


def put(stack, value, index):
    return lax.dynamic_update_index_in_dim(stack, value, index, 0)


def gather_parts(parts, me):
    full = jnp.zeros((len(parts),) + parts[0].shape, parts[0].dtype)
    for s, part in enumerate(parts):
        full = put(full, part, me ^ s)
    return full


def all_to_all(stack, axes):
    n = axis_total(axes)
    me = linear_index(axes)
    parts = [take(stack, me)]
    for s in range(1, n):
        parts.append(hop(take(stack, me ^ s), axes, s))
    return gather_parts(parts, me)


def all_gather(value, axes):
    n = axis_total(axes)
    me = linear_index(axes)
    return gather_parts([value] + [hop(value, axes, s) for s in range(1, n)], me)


def tree_sum(parts):
    while len(parts) > 1:
        parts = [a + b for a, b in zip(parts[::2], parts[1::2])]
    return parts[0]


def all_sum(value, axes):
    n = axis_total(axes)
    return tree_sum([value] + [hop(value, axes, s) for s in range(1, n)])


CHIPS = ("rs", "mx")
CORES = ("mc",)


def plane_gather(rows):
    wide = all_gather(rows, CHIPS)
    both = all_gather(wide, CORES)
    both = jnp.swapaxes(both, 0, 1)
    return both.reshape((-1,) + rows.shape[1:])


def plane_scatter(partial):
    cores = axis_total(CORES)
    chips = axis_total(CHIPS)
    width = partial.shape[-1]
    parts = partial.astype(BF).reshape(chips, cores, -1, width)
    parts = jnp.swapaxes(parts, 0, 1)
    me = linear_index(CORES)
    pair = take(parts, me).astype(F32) + hop(take(parts, me ^ 1), CORES, 1).astype(F32)
    pair = pair.astype(BF)
    me = linear_index(CHIPS)
    return tree_sum(
        [take(pair, me).astype(F32)]
        + [hop(take(pair, me ^ s), CHIPS, s).astype(F32) for s in range(1, chips)]
    )


def rms_forward(values, gain):
    inv_rms = lax.rsqrt(jnp.mean(values * values, axis=-1, keepdims=True) + NORM_EPS)
    unit_rows = values * inv_rms
    return unit_rows, inv_rms, (unit_rows * gain).astype(BF)


def rms_backward(grad_normed, unit_rows, inv_rms, gain):
    scaled = grad_normed * gain
    return inv_rms * (scaled - unit_rows * jnp.mean(scaled * unit_rows, axis=-1, keepdims=True))


def mm(a, b):
    return jnp.dot(a, b, preferred_element_type=F32)


def mm_nt(a, b):
    return lax.dot_general(a, b, (((1,), (1,)), ((), ())), preferred_element_type=F32)


def mm_tn(a, b):
    return lax.dot_general(a, b, (((0,), (0,)), ((), ())), preferred_element_type=F32)


def head_sums(products):
    width = products.shape[-1]
    head = jnp.arange(width) // HD
    ones = (head[:, None] == head[None, :]).astype(BF)
    high = products.astype(BF)
    low = (products - high.astype(F32)).astype(BF)
    return mm(high, ones) + mm(low, ones)


def attend(query, key, value):
    depth = query.shape[0]
    q32, k32, v32 = (v.astype(F32) for v in (query, key, value))
    pairs = [(p, q) for p in range(depth) for q in range(p + 1)]
    rows = query.shape[1]
    products = jnp.concatenate([q32[p] * k32[q] for p, q in pairs], 0)
    sums = head_sums(products) * HD ** (-0.5)
    scores = {pq: sums[i * rows : (i + 1) * rows] for i, pq in enumerate(pairs)}
    probs = {}
    context = []
    for p in range(depth):
        top = scores[p, 0]
        for q in range(1, p + 1):
            top = jnp.maximum(top, scores[p, q])
        terms = [jnp.exp(scores[p, q] - top) for q in range(p + 1)]
        total = sum(terms[1:], terms[0])
        acc = 0.0
        for q in range(p + 1):
            probs[p, q] = terms[q] / total
            acc = acc + probs[p, q].astype(BF).astype(F32) * v32[q]
        context.append(acc.astype(BF))
    return jnp.stack(context), probs


def attend_back(query, key, value, probs, grad_context):
    depth = query.shape[0]
    q32, k32, v32, g32 = (v.astype(F32) for v in (query, key, value, grad_context))
    pairs = [(p, q) for p in range(depth) for q in range(p + 1)]
    rows = query.shape[1]
    products = jnp.concatenate([g32[p] * v32[q] for p, q in pairs], 0)
    sums = head_sums(products)
    grad_probs = {pq: sums[i * rows : (i + 1) * rows] for i, pq in enumerate(pairs)}
    grad_scores = {}
    for p in range(depth):
        inner = probs[p, 0] * grad_probs[p, 0]
        for q in range(1, p + 1):
            inner = inner + probs[p, q] * grad_probs[p, q]
        for q in range(p + 1):
            grad_scores[p, q] = (
                (probs[p, q] * (grad_probs[p, q] - inner)).astype(BF).astype(F32)
            )
    scale = HD ** (-0.5)
    grad_query = []
    grad_key = []
    grad_value = []
    for p in range(depth):
        grad_query.append(
            (scale * sum(grad_scores[p, q] * k32[q] for q in range(p + 1))).astype(BF)
        )
        grad_key.append(
            (scale * sum(grad_scores[o, p] * q32[o] for o in range(p, depth))).astype(BF)
        )
        grad_value.append(
            sum(probs[o, p].astype(BF).astype(F32) * g32[o] for o in range(p, depth)).astype(BF)
        )
    return jnp.concatenate(
        [jnp.stack(grad_query), jnp.stack(grad_key), jnp.stack(grad_value)], -1
    )


def adamw_update(weights, first, second, grads, clip_factor, decay_rate, step_rate):
    clipped = clip_factor * grads
    first_new = BETA_ONE * first + (1.0 - BETA_ONE) * clipped
    second_new = BETA_TWO * second + (1.0 - BETA_TWO) * clipped * clipped
    first_hat = first_new / (1.0 - BETA_ONE**STEP)
    second_hat = second_new / (1.0 - BETA_TWO**STEP)
    new_weights = weights - step_rate * (
        first_hat / (jnp.sqrt(second_hat) + ADAM_EPS) + decay_rate * weights
    )
    return (new_weights, first_new, second_new)


OWNERS = ("pz", "rs")


def weights_to_planes(weights):
    rows, kinds, depth, cols = weights.shape
    parts = lax.axis_size("rs")
    low = weights.astype(BF).reshape(rows, kinds, depth, parts, cols // parts)
    low = low.transpose(2, 3, 0, 1, 4).reshape(depth * parts, rows, kinds * cols // parts)
    full = all_to_all(low, OWNERS)
    if lax.axis_size("rf") > 1:
        full = full.reshape((depth, parts) + full.shape[1:])
        full = lax.all_gather(full, "rf", axis=1)
    return full.reshape(-1, full.shape[-1])


def grads_to_owners(grads):
    depth = lax.axis_size("pz")
    parts = lax.axis_size("rs")
    width = grads.shape[-1]
    if lax.axis_size("rf") > 1:
        grads = grads.reshape(depth, lax.axis_size("rf"), -1, width)
        grads = lax.psum_scatter(grads, "rf", scatter_dimension=1)
    squares = jnp.sum(grads * grads)
    low = grads.astype(BF).reshape(depth * parts, -1, width)
    return all_to_all(low, OWNERS), squares


def owners_view(chunks, kinds):
    depth = lax.axis_size("pz")
    parts = lax.axis_size("rs")
    rows = chunks.shape[1]
    view = chunks.reshape(depth, parts, rows, kinds, -1).transpose(2, 3, 0, 1, 4)
    return view.reshape(rows, kinds, depth, -1).astype(F32)


def body(
    inputs,
    depth_counts,
    out_grad,
    attn_weight,
    attn_first,
    attn_second,
    ffn_weight,
    ffn_first,
    ffn_second,
    norm_gains,
    gain_first,
    gain_second,
):
    depth, frames, model = inputs.shape
    mp_axes = ("mx", "mc")
    share = frames // axis_total(mp_axes)
    gain_attn = norm_gains[0]
    gain_ffn = norm_gains[1]

    mine = linear_index(mp_axes) * share
    counts = lax.dynamic_slice_in_dim(depth_counts, mine, share, 0)
    live = (jnp.arange(depth)[:, None] < counts[None, :]).astype(BF)
    sent = jnp.stack(
        [
            lax.dynamic_slice_in_dim(inputs, mine, share, 1),
            lax.dynamic_slice_in_dim(out_grad, mine, share, 1),
        ],
        1,
    )
    live = jnp.broadcast_to(live[:, None, :, None], (depth, 2, share, 128))
    got = all_to_all(jnp.concatenate([sent, live], -1), ("pz",))
    rows_in = got[:, 0, :, :model].reshape(-1, model).astype(F32)
    rows_grad = got[:, 1, :, :model].reshape(-1, model).astype(F32)
    mask = got[:, 0, :, model : model + 1].reshape(-1, 1).astype(F32)

    attn_w = weights_to_planes(attn_weight)
    gate_up_w = weights_to_planes(ffn_weight[:, 0:2])
    down_w = weights_to_planes(ffn_weight[:, 2:3])
    width = attn_w.shape[1] // 4
    hidden = down_w.shape[1]

    unit1, inv1, normed1_rows = rms_forward(rows_in, gain_attn)
    normed1 = plane_gather(normed1_rows)
    grad_ffn = plane_gather((mask * rows_grad).astype(BF))

    qkv = mm(normed1, attn_w[:, : 3 * width]).astype(BF)
    tokens = qkv.shape[0]
    qkv = all_to_all(qkv.reshape(depth, tokens // depth, 3 * width), ("pz",))
    query, key, value = (qkv[..., j * width : (j + 1) * width] for j in range(3))
    context, probs = attend(query, key, value)
    context = all_to_all(context, ("pz",)).reshape(tokens, width)
    out_w = attn_w[:, 3 * width :]
    attn_out = plane_scatter(mm_nt(context, out_w))
    hidden_in = rows_in + mask * attn_out
    unit2, inv2, normed2_rows = rms_forward(hidden_in, gain_ffn)
    normed2 = plane_gather(normed2_rows)

    gate_up = mm(normed2, gate_up_w)
    gate_pre = gate_up[:, :hidden]
    up_proj = gate_up[:, hidden:]
    sig = jax.nn.sigmoid(gate_pre)
    acts = (gate_pre * sig * up_proj).astype(BF)
    down_chunks, squares_down = grads_to_owners(mm_tn(grad_ffn, acts))
    grad_act = mm(grad_ffn, down_w)
    grad_gate = (grad_act * up_proj * sig * (1.0 + gate_pre * (1.0 - sig))).astype(BF)
    grad_up = (grad_act * gate_pre * sig).astype(BF)
    grad_gate_up = jnp.concatenate([grad_gate, grad_up], 1)
    grad_normed2 = plane_scatter(mm_nt(grad_gate_up, gate_up_w))
    gate_up_chunks, squares_gate_up = grads_to_owners(mm_tn(normed2, grad_gate_up))
    ffn_out = plane_scatter(mm_nt(acts, down_w))
    out_rows = (hidden_in + mask * ffn_out).astype(BF)

    grad_hidden = rows_grad + rms_backward(grad_normed2, unit2, inv2, gain_ffn)
    grad_attn = plane_gather((mask * grad_hidden).astype(BF))
    grad_context = mm(grad_attn, out_w).astype(BF)
    grad_context = all_to_all(grad_context.reshape(depth, tokens // depth, width), ("pz",))
    grad_qkv = attend_back(query, key, value, probs, grad_context)
    grad_qkv = all_to_all(grad_qkv, ("pz",)).reshape(tokens, 3 * width)
    grad_normed1 = plane_scatter(mm_nt(grad_qkv, attn_w[:, : 3 * width]))
    attn_chunks, squares_attn = grads_to_owners(
        jnp.concatenate([mm_tn(normed1, grad_qkv), mm_tn(grad_attn, context)], 1)
    )
    grad_rows = (grad_hidden + rms_backward(grad_normed1, unit1, inv1, gain_attn)).astype(BF)

    def to_frames(rows):
        back = all_to_all(rows.reshape(depth, share, model), ("pz",))
        wide = all_gather(all_gather(back, ("mx",)), ("mc",))
        return wide.transpose(2, 1, 0, 3, 4).reshape(depth, frames, model)

    output = to_frames(out_rows)
    input_grad = to_frames(grad_rows)

    gain_part = jnp.stack(
        [jnp.sum(grad_normed1 * unit1, axis=0), jnp.sum(grad_normed2 * unit2, axis=0)]
    )
    squares = squares_down + squares_gate_up + squares_attn
    row = jnp.zeros((1, model), F32).at[0, 0].set(squares)
    total = jnp.concatenate([gain_part, row], 0)
    if lax.axis_size("rf") > 1:
        total = lax.psum(total, "rf")
    total = all_sum(all_sum(total, CHIPS + CORES), ("pz",))
    gain_grad = total[:2]
    grad_norm = jnp.sqrt(total[2, 0] + jnp.sum(gain_grad * gain_grad))
    clip_factor = CLIP_NORM / jnp.maximum(grad_norm, CLIP_NORM)

    ffn_grad = jnp.concatenate([owners_view(gate_up_chunks, 2), owners_view(down_chunks, 1)], 1)
    ffn_new = adamw_update(
        ffn_weight, ffn_first, ffn_second, ffn_grad, clip_factor, WEIGHT_DECAY, LEARN_RATE
    )
    attn_grad = owners_view(attn_chunks, 4)
    attn_new = adamw_update(
        attn_weight, attn_first, attn_second, attn_grad, clip_factor, WEIGHT_DECAY, LEARN_RATE
    )
    gain_new = adamw_update(
        norm_gains, gain_first, gain_second, gain_grad, clip_factor, 0.0, GAIN_RATE
    )
    return (output, input_grad, grad_norm) + attn_new + ffn_new + gain_new


def solution(mesh):
    dp = mesh.shape["dp"]
    mp = mesh.shape["mp"]

    def run(*args):
        depth, _, model = args[0].shape
        heads = args[3].shape[3] // mp // HD
        parts = math.gcd(dp // depth, heads)
        fine = Mesh(
            mesh.devices.reshape(depth, dp // depth // parts, parts, mp // 2, 2),
            ("pz", "rf", "rs", "mx", "mc"),
        )
        rows = ("pz", "rf", "rs")
        cols = ("mx", "mc")
        acts = P(None, rows, None)
        weight = P(rows, None, None, cols)
        return jax.shard_map(
            body,
            mesh=fine,
            in_specs=(acts, P(rows), acts) + (weight,) * 6 + (P(),) * 3,
            out_specs=(acts, acts, P()) + (weight,) * 6 + (P(),) * 3,
            check_vma=False,
        )(*args)

    return run
```

```python
import functools
import math

import jax
import jax.numpy as jnp
from jax import lax
from jax.experimental import pallas as pl
from jax.experimental.pallas import tpu as pltpu
from jax.sharding import Mesh, PartitionSpec as P

HD = 64
STEP = 5
NORM_EPS = 1e-05
BETA_ONE = 0.5
BETA_TWO = 0.5
LEARN_RATE = 0.02
GAIN_RATE = 0.4
WEIGHT_DECAY = 0.1
ADAM_EPS = 1e-08
CLIP_NORM = 1.0

VMEM_LIMIT = 16 << 20

BF = jnp.bfloat16
F32 = jnp.float32


def axis_total(axes):
    return math.prod(lax.axis_size(a) for a in axes)


def linear_index(axes):
    index = 0
    for a in axes:
        index = index * lax.axis_size(a) + lax.axis_index(a)
    return index


def hop(value, axes, step):
    n = axis_total(axes)
    return lax.ppermute(value, axes, [(i, i ^ step) for i in range(n)])


def take(stack, index):
    return lax.dynamic_index_in_dim(stack, index, 0, keepdims=False)


def put(stack, value, index):
    return lax.dynamic_update_index_in_dim(stack, value, index, 0)


def gather_parts(parts, me):
    full = jnp.zeros((len(parts),) + parts[0].shape, parts[0].dtype)
    for s, part in enumerate(parts):
        full = put(full, part, me ^ s)
    return full


def all_to_all(stack, axes):
    n = axis_total(axes)
    me = linear_index(axes)
    parts = [take(stack, me)]
    for s in range(1, n):
        parts.append(hop(take(stack, me ^ s), axes, s))
    return gather_parts(parts, me)


def all_gather(value, axes):
    n = axis_total(axes)
    me = linear_index(axes)
    return gather_parts([value] + [hop(value, axes, s) for s in range(1, n)], me)


def tree_sum(parts):
    while len(parts) > 1:
        parts = [a + b for a, b in zip(parts[::2], parts[1::2])]
    return parts[0]


def all_sum(value, axes):
    n = axis_total(axes)
    return tree_sum([value] + [hop(value, axes, s) for s in range(1, n)])


CHIPS = ("rs", "mx")
CORES = ("mc",)


def rms_forward(values, gain):
    inv_rms = lax.rsqrt(jnp.mean(values * values, axis=-1, keepdims=True) + NORM_EPS)
    unit_rows = values * inv_rms
    return unit_rows, inv_rms, (unit_rows * gain).astype(BF)


def rms_backward(grad_normed, unit_rows, inv_rms, gain):
    scaled = grad_normed * gain
    return inv_rms * (scaled - unit_rows * jnp.mean(scaled * unit_rows, axis=-1, keepdims=True))


def mm(a, b):
    return jnp.dot(a, b, preferred_element_type=F32)


def mm_nt(a, b):
    return lax.dot_general(a, b, (((1,), (1,)), ((), ())), preferred_element_type=F32)


def mm_tn(a, b):
    return lax.dot_general(a, b, (((0,), (0,)), ((), ())), preferred_element_type=F32)


def head_sums(products):
    width = products.shape[-1]
    head_in = lax.broadcasted_iota(jnp.int32, (width, width), 0) // HD
    head_out = lax.broadcasted_iota(jnp.int32, (width, width), 1) // HD
    ones = jnp.where(head_in == head_out, 1.0, 0.0).astype(BF)
    high = products.astype(BF)
    low = (products - high.astype(F32)).astype(BF)
    return mm(high, ones) + mm(low, ones)


def attend(query, key, value):
    depth = len(query)
    q32, k32, v32 = ([v.astype(F32) for v in rows] for rows in (query, key, value))
    pairs = [(p, q) for p in range(depth) for q in range(p + 1)]
    rows = query[0].shape[0]
    sums = head_sums(jnp.concatenate([q32[p] * k32[q] for p, q in pairs], 0)) * HD ** (-0.5)
    scores = {pq: sums[i * rows : (i + 1) * rows] for i, pq in enumerate(pairs)}
    probs = {}
    context = []
    for p in range(depth):
        top = scores[p, 0]
        for q in range(1, p + 1):
            top = jnp.maximum(top, scores[p, q])
        terms = [jnp.exp(scores[p, q] - top) for q in range(p + 1)]
        scale = 1.0 / sum(terms[1:], terms[0])
        acc = 0.0
        for q in range(p + 1):
            probs[p, q] = terms[q] * scale
            acc = acc + probs[p, q].astype(BF).astype(F32) * v32[q]
        context.append(acc.astype(BF))
    return context, probs


def attend_back(query, key, value, probs, grad_context):
    depth = len(query)
    q32, k32, v32, g32 = ([v.astype(F32) for v in r] for r in (query, key, value, grad_context))
    pairs = [(p, q) for p in range(depth) for q in range(p + 1)]
    rows = query[0].shape[0]
    sums = head_sums(jnp.concatenate([g32[p] * v32[q] for p, q in pairs], 0))
    grad_probs = {pq: sums[i * rows : (i + 1) * rows] for i, pq in enumerate(pairs)}
    grad_scores = {}
    for p in range(depth):
        inner = sum(probs[p, q] * grad_probs[p, q] for q in range(p + 1))
        for q in range(p + 1):
            low = (probs[p, q] * (grad_probs[p, q] - inner)).astype(BF)
            grad_scores[p, q] = low.astype(F32)
    scale = HD ** (-0.5)
    grad_query, grad_key, grad_value = [], [], []
    for p in range(depth):
        later = range(p, depth)
        grad_query.append(
            (scale * sum(grad_scores[p, q] * k32[q] for q in range(p + 1))).astype(BF)
        )
        grad_key.append((scale * sum(grad_scores[o, p] * q32[o] for o in later)).astype(BF))
        grad_value.append(
            sum(probs[o, p].astype(BF).astype(F32) * g32[o] for o in later).astype(BF)
        )
    return grad_query, grad_key, grad_value


def vmem_call(kernel, outs, *args, index=None, scratch=(), flops=0, wait_for=()):
    size = sum(v.size * v.dtype.itemsize for v in args)
    size += sum(math.prod(v.shape) * v.dtype.itemsize for v in outs)
    first = () if index is None else (jnp.reshape(index, (-1,)).astype(jnp.int32),)
    specs = [pl.BlockSpec(memory_space=pltpu.SMEM)] * len(first)
    specs += [pl.BlockSpec(memory_space=pltpu.VMEM)] * len(args)
    specs += [pl.BlockSpec(memory_space=pl.ANY)] * len(wait_for)
    read = len(first) + len(args)

    def run(*refs):
        kernel(*refs[:read], *refs[read + len(wait_for) :])

    return pl.pallas_call(
        run,
        out_shape=list(outs),
        in_specs=specs,
        out_specs=[pl.BlockSpec(memory_space=pltpu.VMEM)] * len(outs),
        scratch_shapes=list(scratch),
        compiler_params=pltpu.CompilerParams(vmem_limit_bytes=VMEM_LIMIT),
        cost_estimate=pl.CostEstimate(flops=flops, bytes_accessed=size, transcendentals=0),
        name=getattr(kernel, "func", kernel).__name__,
    )(*first, *args, *wait_for)


def sds(shape, dtype):
    return jax.ShapeDtypeStruct(shape, dtype)


def pass_kernel(*refs):
    pass


def after(value, *others):
    anywhere = pl.BlockSpec(memory_space=pl.ANY)
    return pl.pallas_call(
        pass_kernel,
        out_shape=sds(value.shape, value.dtype),
        in_specs=[anywhere] * (1 + len(others)),
        out_specs=anywhere,
        input_output_aliases={0: 0},
        name="after",
    )(value, *others)


def swap_parts(parts, axes):
    return [parts[0]] + [hop(part, axes, t) for t, part in enumerate(parts) if t]


def stack_kernel(*refs):
    at = 0
    for ref in refs[:-1]:
        rows = ref.shape[0]
        refs[-1][at : at + rows, :] = ref[...]
        at += rows


def stack_rows(parts):
    shape = (sum(p.shape[0] for p in parts), parts[0].shape[1])
    return vmem_call(stack_kernel, [sds(shape, parts[0].dtype)], *parts)[0]


def gather_pieces(rows):
    near = [rows] + [hop(rows, CHIPS, t) for t in range(1, axis_total(CHIPS))]
    return near + [hop(stack_rows(near), CORES, 1)]


def pair_kernel(near_ref, far_ref, *out_refs):
    rows = out_refs[0].shape[0]
    for t, ref in enumerate(out_refs):
        at = slice(t * rows, (t + 1) * rows)
        ref[...] = (near_ref[at, :].astype(F32) + far_ref[at, :].astype(F32)).astype(BF)


def scatter_pieces(near, far):
    chips = axis_total(CHIPS)
    got = hop(far, CORES, 1)
    rows = near.shape[0] // chips
    pair = vmem_call(pair_kernel, [sds((rows, near.shape[1]), BF)] * chips, near, got)
    return swap_parts(pair, CHIPS)


def sum_refs(refs):
    return tree_sum([ref[...].astype(F32) for ref in refs])


def pack_rows(inputs, out_grad, depth_counts, me, mine, share):
    depth = inputs.shape[0]
    counts = lax.dynamic_slice_in_dim(depth_counts, mine * share, share, 0)
    live = (jnp.arange(depth)[:, None] < counts[None, :]).astype(BF)
    live = jnp.broadcast_to(live[:, None, :, None], (depth, 2, share, 128))
    rows = [lax.dynamic_slice_in_dim(v, mine * share, share, 1) for v in (inputs, out_grad)]
    sent = jnp.concatenate([jnp.stack(rows, 1), live], -1)
    return [take(sent, me ^ t) for t in range(depth)]


def unpack_kernel(depth, me_ref, *refs):
    got = refs[:depth]
    gain_ref, rows_ref, grad_ref, mask_ref, normed_ref, masked_ref = refs[depth:]
    share, wide = got[0].shape[1:]
    model = rows_ref.shape[1]
    for t in range(depth):
        at = pl.ds(pl.multiple_of((me_ref[0] ^ t) * share, share), share)
        rows_ref[at, :] = got[t][0, :, :model].astype(F32)
        grad_ref[at, :] = got[t][1, :, :model].astype(F32)
        mask_ref[at, :] = got[t][0, :, model:].astype(F32)
    normed_ref[...] = rms_forward(rows_ref[...], gain_ref[...])[2]
    masked_ref[...] = (mask_ref[:, :1] * grad_ref[...]).astype(BF)


def unpack_rows(got, gain, me):
    depth = len(got)
    share, wide = got[0].shape[1:]
    shape = (depth * share, wide - 128)
    return vmem_call(
        functools.partial(unpack_kernel, depth),
        [sds(shape, F32), sds(shape, F32), sds((shape[0], 128), F32), sds(shape, BF), sds(shape, BF)],
        *got,
        gain[None],
        index=me,
    )


def project_kernel(width, parts, *refs):
    me_ref = refs[0]
    pieces = refs[1 : 1 + parts]
    w_ref = refs[1 + parts]
    normed_ref = refs[2 + parts]
    out_refs = refs[3 + parts : -1]
    all_ref = refs[-1]
    stack_kernel(*pieces, normed_ref)
    depth, rows, _ = all_ref.shape
    weights = w_ref[:, : 3 * width]
    for c in range(depth):
        all_ref[c] = mm(normed_ref[c * rows : (c + 1) * rows, :], weights).astype(BF)
    for t, ref in enumerate(out_refs):
        ref[...] = all_ref[me_ref[0] ^ t]


def project(pieces, attn_w, width, me, depth):
    tokens = sum(p.shape[0] for p in pieces)
    rows = tokens // depth
    out = vmem_call(
        functools.partial(project_kernel, width, len(pieces)),
        [sds((tokens, attn_w.shape[0]), BF)] + [sds((rows, 3 * width), BF)] * depth,
        *pieces,
        attn_w,
        index=me,
        scratch=[pltpu.VMEM((depth, rows, 3 * width), BF)],
        flops=6 * tokens * width * attn_w.shape[0],
    )
    return out[0], out[1:]


def attend_kernel(depth, me_ref, *refs):
    got = refs[:depth]
    outs = refs[depth : 2 * depth]
    qkv, ctx = refs[2 * depth :]
    width = ctx.shape[-1]
    for t in range(depth):
        qkv[me_ref[0] ^ t] = got[t][...]
    q, k, v = ([qkv[p, :, j * width : (j + 1) * width] for p in range(depth)] for j in range(3))
    context, _ = attend(q, k, v)
    for p in range(depth):
        ctx[p] = context[p]
    for t in range(depth):
        outs[t][...] = ctx[me_ref[0] ^ t]


def attend_pieces(got, me):
    depth = len(got)
    rows, wide = got[0].shape
    return vmem_call(
        functools.partial(attend_kernel, depth),
        [sds((rows, wide // 3), BF)] * depth,
        *got,
        index=me,
        scratch=[pltpu.VMEM((depth, rows, wide), BF), pltpu.VMEM((depth, rows, wide // 3), BF)],
        flops=depth * rows * wide * 60,
    )


def attend_back_kernel(depth, me_ref, *refs):
    got = refs[:depth]
    got_context = refs[depth : 2 * depth]
    outs = refs[2 * depth : 3 * depth]
    qkv, ctx = refs[3 * depth :]
    width = ctx.shape[-1]
    for t in range(depth):
        qkv[me_ref[0] ^ t] = got[t][...]
        ctx[me_ref[0] ^ t] = got_context[t][...]
    q, k, v = ([qkv[p, :, j * width : (j + 1) * width] for p in range(depth)] for j in range(3))
    _, probs = attend(q, k, v)
    grads = attend_back(q, k, v, probs, [ctx[p] for p in range(depth)])
    for p in range(depth):
        for j in range(3):
            qkv[p, :, j * width : (j + 1) * width] = grads[j][p]
    for t in range(depth):
        outs[t][...] = qkv[me_ref[0] ^ t]


def attend_back_pieces(got, got_context, me):
    depth = len(got)
    rows, wide = got[0].shape
    return vmem_call(
        functools.partial(attend_back_kernel, depth),
        [sds((rows, wide), BF)] * depth,
        *got,
        *got_context,
        index=me,
        scratch=[pltpu.VMEM((depth, rows, wide), BF), pltpu.VMEM((depth, rows, wide // 3), BF)],
        flops=depth * rows * wide * 100,
    )


def attn_out_kernel(depth, width, me_ref, *refs):
    got = refs[:depth]
    w_ref = refs[depth]
    ctx_ref, near_ref, far_ref = refs[depth + 1 : depth + 4]
    by_chunk = refs[depth + 4]
    for t in range(depth):
        by_chunk[me_ref[0] ^ t] = got[t][...]
    rows = by_chunk.shape[1]
    half = depth // 2
    for c in range(depth):
        ctx_ref[c * rows : (c + 1) * rows, :] = by_chunk[c]
        out = near_ref if c < half else far_ref
        at = (c % half) * rows
        out[at : at + rows, :] = mm_nt(by_chunk[c], w_ref[:, 3 * width :]).astype(BF)


def attn_out_terms(got, attn_w, me):
    depth = len(got)
    rows, width = got[0].shape
    model = attn_w.shape[0]
    tokens = depth * rows
    return vmem_call(
        functools.partial(attn_out_kernel, depth, width),
        [sds((tokens, width), BF)] + [sds((tokens // 2, model), BF)] * 2,
        *got,
        attn_w,
        index=me,
        scratch=[pltpu.VMEM((depth, rows, width), BF)],
        flops=2 * tokens * width * model,
    )


def join_kernel(chips, *refs):
    terms = refs[:chips]
    rows_ref, mask_ref, gain_ref = refs[chips : chips + 3]
    hidden_ref, normed_ref = refs[chips + 3 :]
    hidden = rows_ref[...] + mask_ref[:, :1] * sum_refs(terms)
    hidden_ref[...] = hidden
    normed_ref[...] = rms_forward(hidden, gain_ref[...])[2]


def join_rows(terms, rows_in, mask, gain):
    shape = rows_in.shape
    return vmem_call(
        functools.partial(join_kernel, len(terms)),
        [sds(shape, F32), sds(shape, BF)],
        *terms,
        rows_in,
        mask,
        gain[None],
    )


def norm_back_kernel(chips, _, *refs):
    terms = refs[:chips]
    rows_ref, grad_ref, mask_ref, gain_ref = refs[chips : chips + 4]
    out_ref, masked_ref, gain_out_ref = refs[chips + 4 :]
    grad_normed = sum_refs(terms)
    unit_rows, inv_rms, _ = rms_forward(rows_ref[...], gain_ref[...])
    grad = grad_ref[...] + rms_backward(grad_normed, unit_rows, inv_rms, gain_ref[...])
    out_ref[...] = grad
    masked_ref[...] = (mask_ref[:, :1] * grad).astype(BF)
    gain_out_ref[...] = jnp.sum(grad_normed * unit_rows, axis=0, keepdims=True)


def norm_back(terms, rows, grad_rows, mask, gain, index):
    shape = rows.shape
    return vmem_call(
        functools.partial(norm_back_kernel, len(terms)),
        [sds(shape, F32), sds(shape, BF), sds((1, shape[1]), F32)],
        *terms,
        rows,
        grad_rows,
        mask,
        gain[None],
        index=index,
    )


def finish_kernel(depth, chips, me_ref, *refs):
    terms, ffn_terms = refs[:chips], refs[chips : 2 * chips]
    rows_ref, grad_ref, hidden_ref, mask_ref, gain_ref = refs[2 * chips : 2 * chips + 5]
    outs = refs[2 * chips + 5 : -2]
    output, input_grad = refs[-2:]
    unit_rows, inv_rms, _ = rms_forward(rows_ref[...], gain_ref[...])
    grad = rms_backward(sum_refs(terms), unit_rows, inv_rms, gain_ref[...])
    output[...] = (hidden_ref[...] + mask_ref[:, :1] * sum_refs(ffn_terms)).astype(BF)
    input_grad[...] = (grad_ref[...] + grad).astype(BF)
    share = outs[0].shape[1]
    for t, ref in enumerate(outs):
        at = pl.ds(pl.multiple_of((me_ref[0] ^ t) * share, share), share)
        ref[0] = output[at, :]
        ref[1] = input_grad[at, :]


def finish_rows(terms, ffn_terms, rows, grad_rows, hidden, mask, gain, me, depth):
    tokens, model = rows.shape
    return vmem_call(
        functools.partial(finish_kernel, depth, len(terms)),
        [sds((2, tokens // depth, model), BF)] * depth,
        *terms,
        *ffn_terms,
        rows,
        grad_rows,
        hidden,
        mask,
        gain[None],
        index=me,
        scratch=[pltpu.VMEM((tokens, model), BF)] * 2,
    )


def by_position_kernel(depth, me_ref, *refs):
    for t in range(depth):
        refs[depth][me_ref[0] ^ t] = refs[t][...]


def by_position(got, me):
    return vmem_call(
        functools.partial(by_position_kernel, len(got)),
        [sds((len(got),) + got[0].shape, got[0].dtype)],
        *got,
        index=me,
    )[0]


def whole_frames_kernel(parts, me_ref, *refs):
    share = refs[0].shape[2]
    for t in range(parts):
        at = pl.ds(pl.multiple_of((me_ref[0] ^ t) * share, share), share)
        for p in range(refs[0].shape[0]):
            for j in range(2):
                refs[parts + j][p, at, :] = refs[t][p, j]


def whole_frames(got, me):
    depth, _, share, model = got[0].shape
    return vmem_call(
        functools.partial(whole_frames_kernel, len(got)),
        [sds((depth, len(got) * share, model), BF)] * 2,
        *got,
        index=me,
    )


def ffn_tile(x, g, w_ref, hidden):
    gate_up = mm(x, w_ref[:, : 2 * hidden])
    gate_pre = gate_up[:, :hidden]
    up_proj = gate_up[:, hidden:]
    sig = jax.nn.sigmoid(gate_pre)
    acts = (gate_pre * sig * up_proj).astype(BF)
    grad_act = mm(g, w_ref[:, 2 * hidden :])
    grad_gate = (grad_act * up_proj * sig * (1.0 + gate_pre * (1.0 - sig))).astype(BF)
    grad_up = (grad_act * gate_pre * sig).astype(BF)
    return acts, grad_gate, grad_up


def ffn_kernel(x_ref, g_ref, w_ref, acts_ref, grads_ref, near_ref, far_ref):
    hidden = w_ref.shape[1] // 3
    half = near_ref.shape[0]
    for j, out_ref in enumerate((near_ref, far_ref)):
        at = slice(j * half, (j + 1) * half)
        acts, grad_gate, grad_up = ffn_tile(x_ref[at, :], g_ref[at, :], w_ref, hidden)
        acts_ref[at, :] = acts
        grads_ref[at, :hidden] = grad_gate
        grads_ref[at, hidden:] = grad_up
        out_ref[...] = mm_nt(grads_ref[at, :], w_ref[:, : 2 * hidden]).astype(BF)


def ffn_block(normed, grad_ffn, ffn_w):
    tokens, model = normed.shape
    hidden = ffn_w.shape[1] // 3
    return vmem_call(
        ffn_kernel,
        [sds((tokens, hidden), BF), sds((tokens, 2 * hidden), BF)]
        + [sds((tokens // 2, model), BF)] * 2,
        normed,
        grad_ffn,
        ffn_w,
        flops=10 * tokens * hidden * model,
    )


def weight_grad_kernel(count, *refs):
    out_ref, square_ref = refs[2 * count :]
    total = jnp.zeros((1, 128), F32)
    lane = 0
    for i in range(count):
        left, right = refs[2 * i], refs[2 * i + 1]
        width = right.shape[1]
        grads = mm_tn(left[...], right[...])
        out_ref[:, lane : lane + width] = grads.astype(BF)
        squares = jnp.sum(grads * grads, axis=0, keepdims=True)
        for j in range(0, width, 128):
            total = total + squares[:, j : j + 128]
        lane += width

    @pl.when(pl.program_id(0) == 0)
    def _():
        square_ref[...] = total

    @pl.when(pl.program_id(0) > 0)
    def _():
        square_ref[...] += total


def weight_grads(*pairs):
    owners = axis_total(OWNERS)
    tokens, model = pairs[0][0].shape
    widths = [last - first for _, _, first, last in pairs]
    width = sum(widths)
    if lax.axis_size("rf") > 1 or any(w % 128 for w in widths):
        grads = [mm_tn(left, right[:, first:last]) for left, right, first, last in pairs]
        grads = jnp.concatenate(grads, 1)
        if lax.axis_size("rf") > 1:
            grads = grads.reshape(lax.axis_size("pz"), lax.axis_size("rf"), -1, width)
            grads = lax.psum_scatter(grads, "rf", scatter_dimension=1)
        squares = jnp.sum((grads * grads).reshape(-1, 128), axis=0, keepdims=True)
        return grads.astype(BF).reshape(owners, -1, width), squares
    step = 512
    in_specs = []
    for (_, _, first, _), w in zip(pairs, widths):
        in_specs.append(pl.BlockSpec((tokens, step), lambda i: (0, i)))
        in_specs.append(pl.BlockSpec((tokens, w), lambda i, at=first // w: (0, at)))
    out, squares = pl.pallas_call(
        functools.partial(weight_grad_kernel, len(pairs)),
        out_shape=[sds((model, width), BF), sds((1, 128), F32)],
        grid=(model // step,),
        in_specs=in_specs,
        out_specs=[
            pl.BlockSpec((step, width), lambda i: (i, 0)),
            pl.BlockSpec((1, 128), lambda i: (0, 0)),
        ],
        compiler_params=pltpu.CompilerParams(vmem_limit_bytes=VMEM_LIMIT),
        cost_estimate=pl.CostEstimate(
            flops=2 * tokens * model * width,
            bytes_accessed=2 * (tokens * (2 * model + width) + model * width),
            transcendentals=0,
        ),
        name="weight_grads",
    )(*[v for left, right, _, _ in pairs for v in (left, right)])
    return out.reshape(owners, -1, width), squares


def context_kernel(depth, width, *refs):
    me_ref = refs[0]
    parts = len(refs) - 4 - depth
    pieces = refs[1 : 1 + parts]
    w_ref = refs[1 + parts]
    rows_ref = refs[2 + parts]
    outs = refs[3 + parts : 3 + parts + depth]
    by_chunk = refs[-1]
    stack_kernel(*pieces, rows_ref)
    rows = by_chunk.shape[1]
    for c in range(depth):
        by_chunk[c] = mm(rows_ref[c * rows : (c + 1) * rows, :], w_ref[:, 3 * width :]).astype(BF)
    for t in range(depth):
        outs[t][...] = by_chunk[me_ref[0] ^ t]


def context_grads(pieces, attn_w, width, me, depth):
    tokens = sum(p.shape[0] for p in pieces)
    rows = tokens // depth
    out = vmem_call(
        functools.partial(context_kernel, depth, width),
        [sds((tokens, attn_w.shape[0]), BF)] + [sds((rows, width), BF)] * depth,
        *pieces,
        attn_w,
        index=me,
        scratch=[pltpu.VMEM((depth, rows, width), BF)],
        flops=2 * tokens * width * attn_w.shape[0],
    )
    return out[0], out[1:]


def qkv_back_kernel(depth, width, me_ref, *refs):
    got = refs[:depth]
    w_ref, normed_ref, gain_ref, rows_ref, near_ref, far_ref, gain_out_ref, by_chunk = refs[depth:]
    for t in range(depth):
        by_chunk[me_ref[0] ^ t] = got[t][...]
    rows = by_chunk.shape[1]
    half = depth // 2
    total = jnp.zeros(gain_out_ref.shape, F32)
    for c in range(depth):
        here = slice(c * rows, (c + 1) * rows)
        rows_ref[here, :] = by_chunk[c]
        out = near_ref if c < half else far_ref
        at = (c % half) * rows
        terms = mm_nt(by_chunk[c], w_ref[:, : 3 * width])
        out[at : at + rows, :] = terms.astype(BF)
        total = total + jnp.sum(terms * normed_ref[here, :].astype(F32), axis=0, keepdims=True)
    gain_out_ref[...] = total / gain_ref[...]


def qkv_back(got, attn_w, normed, gain, width, me):
    depth = len(got)
    rows = got[0].shape[0]
    tokens = depth * rows
    model = attn_w.shape[0]
    return vmem_call(
        functools.partial(qkv_back_kernel, depth, width),
        [sds((tokens, 3 * width), BF)]
        + [sds((tokens // 2, model), BF)] * 2
        + [sds((1, model), F32)],
        *got,
        attn_w,
        normed,
        gain[None],
        index=me,
        scratch=[pltpu.VMEM((depth, rows, 3 * width), BF)],
        flops=6 * tokens * width * model,
    )


OWNERS = ("pz", "rs")


def lanes_view(array):
    rows, kinds, depth, cols = array.shape
    split = array.reshape(rows, kinds, depth, cols // 128, 128)
    return split.transpose(0, 1, 3, 2, 4).reshape(-1, 128)


def lanes_back(view, shape):
    rows, kinds, depth, cols = shape
    split = view.reshape(rows, kinds, cols // 128, depth, 128)
    return split.transpose(0, 1, 3, 2, 4).reshape(shape)


def tiles_of(dims, pieces):
    kinds, tiles, depth, parts = dims
    per = tiles // parts
    for number, piece in enumerate(pieces):
        lane = 0
        for k, first, count in piece:
            for t in range(first, first + count):
                for part in range(parts):
                    for p in range(depth):
                        at = (k * tiles + part * per + t) * depth + p
                        yield at, p * parts + part, number, lane
                lane += 128


def widths_of(pieces):
    return [128 * sum(count for _, _, count in piece) for piece in pieces]


def whole_message(kinds, cols):
    return [[(k, 0, cols // 128) for k in range(kinds)]]


def split_kernel(dims, pieces, w_ref, *out_refs):
    kinds, tiles, depth, _ = dims
    rows = out_refs[0].shape[1]
    for at, chunk, number, lane in tiles_of(dims, pieces):
        values = w_ref[pl.ds(at, rows, stride=kinds * tiles * depth), :]
        out_refs[number][chunk, :, lane : lane + 128] = values.astype(BF)


def in_blocks(kernel, grid, in_specs, out_shape, out_specs, args, vmem, scalars=(), scratch=(), **more):
    n_in, n_out, n_scalar = len(in_specs), len(out_specs), len(scalars)

    def run(*refs):
        fixed = refs[:n_scalar]
        arrays = refs[n_scalar : n_scalar + n_in + n_out]
        held = refs[n_scalar + n_in + n_out :]
        pltpu.emit_pipeline(
            lambda *blocks: kernel(*fixed, *blocks, *held),
            grid=grid,
            in_specs=in_specs,
            out_specs=out_specs,
        )(*arrays)

    return pl.pallas_call(
        run,
        out_shape=out_shape,
        in_specs=[pl.BlockSpec(memory_space=pltpu.SMEM)] * n_scalar
        + [pl.BlockSpec(memory_space=pltpu.HBM)] * n_in,
        out_specs=[pl.BlockSpec(memory_space=pltpu.HBM)] * n_out,
        scratch_shapes=list(scratch),
        compiler_params=pltpu.CompilerParams(vmem_limit_bytes=vmem << 20),
        **more,
    )(*scalars, *args)


def split_weights(weights, vmem, pieces=None):
    rows, kinds, depth, cols = weights.shape
    parts = lax.axis_size("rs")
    if (cols // parts) % 128 or rows % 16:
        low = weights.astype(BF).reshape(rows, kinds, depth, parts, cols // parts)
        return [low.transpose(2, 3, 0, 1, 4).reshape(depth * parts, rows, -1)]
    pieces = pieces or whole_message(kinds, cols // parts)
    tiles = cols // 128
    step = math.gcd(rows, 32)
    chunks = depth * parts
    return in_blocks(
        functools.partial(split_kernel, (kinds, tiles, depth, parts), pieces),
        (rows // step,),
        [pl.BlockSpec((step * kinds * tiles * depth, 128), lambda i: (i, 0))],
        [sds((chunks, rows, w), BF) for w in widths_of(pieces)],
        [pl.BlockSpec((chunks, step, w), lambda i: (0, i, 0)) for w in widths_of(pieces)],
        [lanes_view(weights)],
        vmem=vmem,
        cost_estimate=pl.CostEstimate(
            flops=weights.size, bytes_accessed=6 * weights.size, transcendentals=0
        ),
        name="split_weights",
    )


def to_planes(low):
    full = lax.all_to_all(low, OWNERS, 0, 0, tiled=True)
    if lax.axis_size("rf") > 1:
        full = full.reshape((lax.axis_size("pz"), lax.axis_size("rs")) + full.shape[1:])
        full = lax.all_gather(full, "rf", axis=1)
    return full.reshape(-1, full.shape[-1])


def to_owners(chunks):
    return lax.all_to_all(chunks, OWNERS, 0, 0, tiled=True)


def adamw_update(weights, first, second, grads, clip_factor, decay_rate, step_rate):
    clipped = clip_factor * grads
    first_new = BETA_ONE * first + (1.0 - BETA_ONE) * clipped
    second_new = BETA_TWO * second + (1.0 - BETA_TWO) * clipped * clipped
    first_hat = first_new * (1.0 / (1.0 - BETA_ONE**STEP))
    second_hat = second_new * (1.0 / (1.0 - BETA_TWO**STEP))
    new_weights = weights - step_rate * (
        first_hat / (jnp.sqrt(second_hat) + ADAM_EPS) + decay_rate * weights
    )
    return (new_weights, first_new, second_new)


def adamw_kernel(dims, pieces, clip_ref, *refs):
    kinds, tiles, depth, _ = dims
    g_refs = refs[: len(pieces)]
    w_ref, m_ref, v_ref, wn_ref, mn_ref, vn_ref, grads = refs[len(pieces) :]
    rows, units, _ = grads.shape
    places = {at: (number, chunk, lane) for at, chunk, number, lane in tiles_of(dims, pieces)}
    for first in range(0, units, 8):
        tile = [
            g_refs[number][chunk, :, lane : lane + 128].astype(F32)
            for number, chunk, lane in (places[at] for at in range(first, first + 8))
        ]
        grads[:, first : first + 8, :] = jnp.swapaxes(jnp.stack(tile), 0, 1)
    clip = clip_ref[0, 0]

    @pl.loop(0, rows)
    def _(row):
        at = pl.ds(pl.multiple_of(row * units, units), units)
        wn_ref[at, :], mn_ref[at, :], vn_ref[at, :] = adamw_update(
            w_ref[at, :], m_ref[at, :], v_ref[at, :], grads[row], clip, WEIGHT_DECAY, LEARN_RATE
        )


def adamw_owned(weights, first, second, chunks, clip_factor, step, vmem, pieces=None):
    rows, kinds, depth, cols = weights.shape
    parts = lax.axis_size("rs")
    units = kinds * cols // 128 * depth
    if (cols // parts) % 128 or rows % 16 or units % 8:
        grads = chunks[0].reshape(depth, parts, rows, kinds, -1).transpose(2, 3, 0, 1, 4)
        grads = grads.reshape(weights.shape).astype(F32)
        new = adamw_update(weights, first, second, grads, clip_factor, WEIGHT_DECAY, LEARN_RATE)
        return new, new[0]
    pieces = pieces or whole_message(kinds, cols // parts)
    step = math.gcd(rows, step)
    block = pl.BlockSpec((step * units, 128), lambda i: (i, 0))
    new = in_blocks(
        functools.partial(adamw_kernel, (kinds, cols // 128, depth, parts), pieces),
        (rows // step,),
        [pl.BlockSpec((depth * parts, step, w), lambda i: (0, i, 0)) for w in widths_of(pieces)]
        + [block] * 3,
        [sds((weights.size // 128, 128), F32)] * 3,
        [block] * 3,
        [*chunks, lanes_view(weights), lanes_view(first), lanes_view(second)],
        scalars=[clip_factor.reshape(1, 1)],
        vmem=vmem,
        scratch=[pltpu.VMEM((step, units, 128), F32)],
        cost_estimate=pl.CostEstimate(
            flops=20 * weights.size, bytes_accessed=26 * weights.size, transcendentals=0
        ),
        name="adamw",
    )
    return tuple(lanes_back(v, weights.shape) for v in new), new[0]


def body(
    inputs,
    depth_counts,
    out_grad,
    attn_weight,
    attn_first,
    attn_second,
    ffn_weight,
    ffn_first,
    ffn_second,
    norm_gains,
    gain_first,
    gain_second,
):
    depth, frames, model = inputs.shape
    mp_axes = ("mx", "mc")
    share = frames // axis_total(mp_axes)
    gain_attn = norm_gains[0]
    gain_ffn = norm_gains[1]

    me = lax.axis_index("pz")
    positions = ("pz",)
    per = ffn_weight.shape[3] // lax.axis_size("rs") // 128
    packed = pack_rows(inputs, out_grad, depth_counts, me, linear_index(mp_axes), share)
    packed = swap_parts(packed, positions)
    attn_low = split_weights(attn_weight, 48)[0]
    rows_in, rows_grad, mask, normed1_rows, masked = unpack_rows(packed, gain_attn, me)
    attn_w = to_planes(after(attn_low, normed1_rows))
    ffn_low = split_weights(ffn_weight, 48)[0]
    width = attn_w.shape[1] // 4
    normed1_pieces = gather_pieces(normed1_rows)
    grad_ffn = stack_rows(gather_pieces(masked))

    normed1, qkv = project(normed1_pieces, attn_w, width, after(me.reshape(1), ffn_low), depth)
    qkv = swap_parts(qkv, positions)
    context = swap_parts(attend_pieces(qkv, me), positions)
    ffn_w = to_planes(after(ffn_low, *context))
    context, near, far = attn_out_terms(context, attn_w, me)
    hidden_in, normed2_rows = join_rows(scatter_pieces(near, far), rows_in, mask, gain_ffn)
    normed2 = stack_rows(gather_pieces(normed2_rows))

    acts, gate_up_grads, near, far = ffn_block(normed2, grad_ffn, ffn_w)
    terms = scatter_pieces(near, far)
    hidden = acts.shape[1]
    pieces = [[(0, 0, per), (1, 0, per)], [(2, 0, per)]]
    chunks_a, squares_a = weight_grads((normed2, gate_up_grads, 0, 2 * hidden))
    owned_a = to_owners(chunks_a)
    chunks_b, squares_b = weight_grads((grad_ffn, acts, 0, hidden))

    ffn_terms = mm_nt(acts, ffn_w[:, 2 * hidden :]).astype(BF)

    grad_hidden, masked, gain_part2 = norm_back(
        terms, hidden_in, rows_grad, mask, gain_ffn, after(me.reshape(1), chunks_b, ffn_terms)
    )
    grad_attn, grad_context = context_grads(gather_pieces(masked), attn_w, width, me, depth)
    grad_context = swap_parts(grad_context, positions)
    grad_qkv = swap_parts(attend_back_pieces(qkv, grad_context, me), positions)
    half = ffn_terms.shape[0] // 2
    ffn_terms = scatter_pieces(ffn_terms[:half], ffn_terms[half:])
    owned_b = to_owners(after(chunks_b, *grad_qkv, *ffn_terms))
    grad_qkv, near, far, gain_part1 = qkv_back(
        grad_qkv, attn_w, normed1, gain_attn, width, after(me.reshape(1), owned_a)
    )
    attn_chunks, squares_attn = weight_grads(
        (normed1, grad_qkv, 0, 3 * width), (grad_attn, context, 0, width)
    )

    squares = squares_a + squares_b + squares_attn
    squares = jnp.pad(squares, ((0, 0), (0, model - 128)))
    total = jnp.concatenate([gain_part1, gain_part2, squares], 0)
    if lax.axis_size("rf") > 1:
        total = lax.psum(total, "rf")
    for axis in ("mc", "mx", "rs"):
        total = all_sum(total, (axis,))
    back = finish_rows(
        scatter_pieces(near, far),
        ffn_terms,
        rows_in,
        grad_hidden,
        hidden_in,
        mask,
        gain_attn,
        me,
        depth,
    )
    total = all_sum(after(total, back[0]), positions)
    attn_owned = to_owners(after(attn_chunks, total, owned_b))
    back = by_position(swap_parts(back, positions), me)

    gain_grad = total[:2]
    grad_norm = jnp.sqrt(jnp.sum(total[2]) + jnp.sum(gain_grad * gain_grad))
    clip_factor = CLIP_NORM / jnp.maximum(grad_norm, CLIP_NORM)

    ffn_new, ffn_done = adamw_owned(
        ffn_weight, ffn_first, ffn_second, [owned_a, owned_b], clip_factor, 16, 48, pieces
    )
    attn_new, _ = adamw_owned(attn_weight, attn_first, attn_second, [attn_owned], clip_factor, 64, 48)

    back = after(back, attn_owned, ffn_done)
    back = swap_parts([back] * axis_total(mp_axes), mp_axes)
    output, input_grad = whole_frames(back, linear_index(mp_axes))
    gain_new = adamw_update(
        norm_gains, gain_first, gain_second, gain_grad, clip_factor, 0.0, GAIN_RATE
    )
    return (output, input_grad, grad_norm) + attn_new + ffn_new + gain_new


def solution(mesh):
    dp = mesh.shape["dp"]
    mp = mesh.shape["mp"]

    def run(*args):
        depth, _, model = args[0].shape
        heads = args[3].shape[3] // mp // HD
        parts = math.gcd(dp // depth, heads)
        fine = Mesh(
            mesh.devices.reshape(depth, dp // depth // parts, parts, mp // 2, 2),
            ("pz", "rf", "rs", "mx", "mc"),
        )
        rows = ("pz", "rf", "rs")
        cols = ("mx", "mc")
        acts = P(None, rows, None)
        weight = P(rows, None, None, cols)
        return jax.shard_map(
            body,
            mesh=fine,
            in_specs=(acts, P(rows), acts) + (weight,) * 6 + (P(),) * 3,
            out_specs=(acts, acts, P()) + (weight,) * 6 + (P(),) * 3,
            check_vma=False,
        )(*args)

    return run
```

```python
import functools
import math

import jax
import jax.numpy as jnp
from jax import lax
from jax.experimental import pallas as pl
from jax.experimental.pallas import tpu as pltpu
from jax.sharding import Mesh, PartitionSpec as P

HD = 64
STEP = 5
NORM_EPS = 1e-05
BETA_ONE = 0.5
BETA_TWO = 0.5
LEARN_RATE = 0.02
GAIN_RATE = 0.4
WEIGHT_DECAY = 0.1
ADAM_EPS = 1e-08
CLIP_NORM = 1.0

VMEM_LIMIT = 16 << 20

BF = jnp.bfloat16
F32 = jnp.float32


def axis_total(axes):
    return math.prod(lax.axis_size(a) for a in axes)


def linear_index(axes):
    index = 0
    for a in axes:
        index = index * lax.axis_size(a) + lax.axis_index(a)
    return index


def hop(value, axes, step):
    n = axis_total(axes)
    return lax.ppermute(value, axes, [(i, i ^ step) for i in range(n)])


def take(stack, index):
    return lax.dynamic_index_in_dim(stack, index, 0, keepdims=False)


def put(stack, value, index):
    return lax.dynamic_update_index_in_dim(stack, value, index, 0)


def gather_parts(parts, me):
    full = jnp.zeros((len(parts),) + parts[0].shape, parts[0].dtype)
    for s, part in enumerate(parts):
        full = put(full, part, me ^ s)
    return full


def all_to_all(stack, axes):
    n = axis_total(axes)
    me = linear_index(axes)
    parts = [take(stack, me)]
    for s in range(1, n):
        parts.append(hop(take(stack, me ^ s), axes, s))
    return gather_parts(parts, me)


def all_gather(value, axes):
    n = axis_total(axes)
    me = linear_index(axes)
    return gather_parts([value] + [hop(value, axes, s) for s in range(1, n)], me)


def tree_sum(parts):
    while len(parts) > 1:
        parts = [a + b for a, b in zip(parts[::2], parts[1::2])]
    return parts[0]


def all_sum(value, axes):
    n = axis_total(axes)
    return tree_sum([value] + [hop(value, axes, s) for s in range(1, n)])


CHIPS = ("rs", "mx")
CORES = ("mc",)


def rms_forward(values, gain):
    inv_rms = lax.rsqrt(jnp.mean(values * values, axis=-1, keepdims=True) + NORM_EPS)
    unit_rows = values * inv_rms
    return unit_rows, inv_rms, (unit_rows * gain).astype(BF)


def rms_backward(grad_normed, unit_rows, inv_rms, gain):
    scaled = grad_normed * gain
    return inv_rms * (scaled - unit_rows * jnp.mean(scaled * unit_rows, axis=-1, keepdims=True))


def mm(a, b):
    return jnp.dot(a, b, preferred_element_type=F32)


def mm_nt(a, b):
    return lax.dot_general(a, b, (((1,), (1,)), ((), ())), preferred_element_type=F32)


def mm_tn(a, b):
    return lax.dot_general(a, b, (((0,), (0,)), ((), ())), preferred_element_type=F32)


def head_sums(products):
    width = products.shape[-1]
    head_in = lax.broadcasted_iota(jnp.int32, (width, width), 0) // HD
    head_out = lax.broadcasted_iota(jnp.int32, (width, width), 1) // HD
    ones = jnp.where(head_in == head_out, 1.0, 0.0).astype(BF)
    high = products.astype(BF)
    low = (products - high.astype(F32)).astype(BF)
    return mm(high, ones) + mm(low, ones)


def attend(query, key, value):
    depth = len(query)
    q32, k32, v32 = ([v.astype(F32) for v in rows] for rows in (query, key, value))
    pairs = [(p, q) for p in range(depth) for q in range(p + 1)]
    rows = query[0].shape[0]
    sums = head_sums(jnp.concatenate([q32[p] * k32[q] for p, q in pairs], 0)) * HD ** (-0.5)
    scores = {pq: sums[i * rows : (i + 1) * rows] for i, pq in enumerate(pairs)}
    probs = {}
    context = []
    for p in range(depth):
        top = scores[p, 0]
        for q in range(1, p + 1):
            top = jnp.maximum(top, scores[p, q])
        terms = [jnp.exp(scores[p, q] - top) for q in range(p + 1)]
        scale = 1.0 / sum(terms[1:], terms[0])
        acc = 0.0
        for q in range(p + 1):
            probs[p, q] = terms[q] * scale
            acc = acc + probs[p, q].astype(BF).astype(F32) * v32[q]
        context.append(acc.astype(BF))
    return context, probs


def attend_back(query, key, value, probs, grad_context):
    depth = len(query)
    q32, k32, v32, g32 = ([v.astype(F32) for v in r] for r in (query, key, value, grad_context))
    pairs = [(p, q) for p in range(depth) for q in range(p + 1)]
    rows = query[0].shape[0]
    sums = head_sums(jnp.concatenate([g32[p] * v32[q] for p, q in pairs], 0))
    grad_probs = {pq: sums[i * rows : (i + 1) * rows] for i, pq in enumerate(pairs)}
    grad_scores = {}
    for p in range(depth):
        inner = sum(probs[p, q] * grad_probs[p, q] for q in range(p + 1))
        for q in range(p + 1):
            low = (probs[p, q] * (grad_probs[p, q] - inner)).astype(BF)
            grad_scores[p, q] = low.astype(F32)
    scale = HD ** (-0.5)
    grad_query, grad_key, grad_value = [], [], []
    for p in range(depth):
        later = range(p, depth)
        grad_query.append(
            (scale * sum(grad_scores[p, q] * k32[q] for q in range(p + 1))).astype(BF)
        )
        grad_key.append((scale * sum(grad_scores[o, p] * q32[o] for o in later)).astype(BF))
        grad_value.append(
            sum(probs[o, p].astype(BF).astype(F32) * g32[o] for o in later).astype(BF)
        )
    return grad_query, grad_key, grad_value


def vmem_call(kernel, outs, *args, index=None, scratch=(), flops=0, vmem=None):
    size = sum(v.size * v.dtype.itemsize for v in args)
    size += sum(math.prod(v.shape) * v.dtype.itemsize for v in outs)
    first = () if index is None else (jnp.reshape(index, (-1,)).astype(jnp.int32),)
    array = pl.BlockSpec() if vmem else pl.BlockSpec(memory_space=pltpu.VMEM)
    return pl.pallas_call(
        kernel,
        out_shape=list(outs),
        in_specs=[pl.BlockSpec(memory_space=pltpu.SMEM)] * len(first) + [array] * len(args),
        out_specs=[array] * len(outs),
        scratch_shapes=list(scratch),
        compiler_params=pltpu.CompilerParams(
            vmem_limit_bytes=vmem << 20 if vmem else VMEM_LIMIT
        ),
        cost_estimate=pl.CostEstimate(flops=flops, bytes_accessed=size, transcendentals=0),
        name=getattr(kernel, "func", kernel).__name__,
    )(*first, *args)


def sds(shape, dtype):
    return jax.ShapeDtypeStruct(shape, dtype)


def pass_kernel(*refs):
    pass


def after(value, *others):
    anywhere = pl.BlockSpec(memory_space=pl.ANY)
    return pl.pallas_call(
        pass_kernel,
        out_shape=sds(value.shape, value.dtype),
        in_specs=[anywhere] * (1 + len(others)),
        out_specs=anywhere,
        input_output_aliases={0: 0},
        name="after",
    )(value, *others)


def swap_parts(parts, axes):
    return [parts[0]] + [hop(part, axes, t) for t, part in enumerate(parts) if t]


def stack_kernel(*refs):
    at = 0
    for ref in refs[:-1]:
        rows = ref.shape[0]
        refs[-1][at : at + rows, :] = ref[...]
        at += rows


def stack_rows(parts):
    shape = (sum(p.shape[0] for p in parts), parts[0].shape[1])
    return vmem_call(stack_kernel, [sds(shape, parts[0].dtype)], *parts)[0]


def gather_pieces(rows):
    near = [rows] + [hop(rows, CHIPS, t) for t in range(1, axis_total(CHIPS))]
    return near + [hop(stack_rows(near), CORES, 1)]


def pair_kernel(near_ref, far_ref, *out_refs):
    rows = out_refs[0].shape[0]
    for t, ref in enumerate(out_refs):
        at = slice(t * rows, (t + 1) * rows)
        ref[...] = (near_ref[at, :].astype(F32) + far_ref[at, :].astype(F32)).astype(BF)


def scatter_pieces(near, far):
    chips = axis_total(CHIPS)
    got = hop(far, CORES, 1)
    rows = near.shape[0] // chips
    pair = vmem_call(pair_kernel, [sds((rows, near.shape[1]), BF)] * chips, near, got)
    return swap_parts(pair, CHIPS)


def sum_refs(refs):
    return tree_sum([ref[...].astype(F32) for ref in refs])


def pack_rows(inputs, out_grad, depth_counts, me, mine, share):
    depth = inputs.shape[0]
    counts = lax.dynamic_slice_in_dim(depth_counts, mine * share, share, 0)
    live = (jnp.arange(depth)[:, None] < counts[None, :]).astype(BF)
    live = jnp.broadcast_to(live[:, None, :, None], (depth, 2, share, 128))
    rows = [lax.dynamic_slice_in_dim(v, mine * share, share, 1) for v in (inputs, out_grad)]
    sent = jnp.concatenate([jnp.stack(rows, 1), live], -1)
    return [take(sent, me ^ t) for t in range(depth)]


def unpack_kernel(depth, me_ref, *refs):
    got = refs[:depth]
    gain_ref, rows_ref, grad_ref, mask_ref, normed_ref, masked_ref = refs[depth:]
    share, wide = got[0].shape[1:]
    model = rows_ref.shape[1]
    for t in range(depth):
        at = pl.ds(pl.multiple_of((me_ref[0] ^ t) * share, share), share)
        rows_ref[at, :] = got[t][0, :, :model].astype(F32)
        grad_ref[at, :] = got[t][1, :, :model].astype(F32)
        mask_ref[at, :] = got[t][0, :, model:].astype(F32)
    normed_ref[...] = rms_forward(rows_ref[...], gain_ref[...])[2]
    masked_ref[...] = (mask_ref[:, :1] * grad_ref[...]).astype(BF)


def unpack_rows(got, gain, me):
    depth = len(got)
    share, wide = got[0].shape[1:]
    shape = (depth * share, wide - 128)
    return vmem_call(
        functools.partial(unpack_kernel, depth),
        [sds(shape, F32), sds(shape, F32), sds((shape[0], 128), F32), sds(shape, BF), sds(shape, BF)],
        *got,
        gain[None],
        index=me,
    )


def project_kernel(width, parts, *refs):
    me_ref = refs[0]
    pieces = refs[1 : 1 + parts]
    w_ref = refs[1 + parts]
    normed_ref = refs[2 + parts]
    out_refs = refs[3 + parts : -1]
    all_ref = refs[-1]
    stack_kernel(*pieces, normed_ref)
    depth, rows, _ = all_ref.shape
    weights = w_ref[:, : 3 * width]
    for c in range(depth):
        all_ref[c] = mm(normed_ref[c * rows : (c + 1) * rows, :], weights).astype(BF)
    for t, ref in enumerate(out_refs):
        ref[...] = all_ref[me_ref[0] ^ t]


def project(pieces, attn_w, width, me, depth):
    tokens = sum(p.shape[0] for p in pieces)
    rows = tokens // depth
    out = vmem_call(
        functools.partial(project_kernel, width, len(pieces)),
        [sds((tokens, attn_w.shape[0]), BF)] + [sds((rows, 3 * width), BF)] * depth,
        *pieces,
        attn_w,
        index=me,
        scratch=[pltpu.VMEM((depth, rows, 3 * width), BF)],
        flops=6 * tokens * width * attn_w.shape[0],
    )
    return out[0], out[1:]


def attend_kernel(depth, me_ref, *refs):
    got = refs[:depth]
    outs = refs[depth : 2 * depth]
    qkv, ctx = refs[2 * depth :]
    width = ctx.shape[-1]
    for t in range(depth):
        qkv[me_ref[0] ^ t] = got[t][...]
    q, k, v = ([qkv[p, :, j * width : (j + 1) * width] for p in range(depth)] for j in range(3))
    context, _ = attend(q, k, v)
    for p in range(depth):
        ctx[p] = context[p]
    for t in range(depth):
        outs[t][...] = ctx[me_ref[0] ^ t]


def attend_pieces(got, me):
    depth = len(got)
    rows, wide = got[0].shape
    return vmem_call(
        functools.partial(attend_kernel, depth),
        [sds((rows, wide // 3), BF)] * depth,
        *got,
        index=me,
        scratch=[pltpu.VMEM((depth, rows, wide), BF), pltpu.VMEM((depth, rows, wide // 3), BF)],
        flops=depth * rows * wide * 60,
    )


def attend_back_kernel(depth, me_ref, *refs):
    got = refs[:depth]
    got_context = refs[depth : 2 * depth]
    outs = refs[2 * depth : 3 * depth]
    qkv, ctx = refs[3 * depth :]
    width = ctx.shape[-1]
    for t in range(depth):
        qkv[me_ref[0] ^ t] = got[t][...]
        ctx[me_ref[0] ^ t] = got_context[t][...]
    q, k, v = ([qkv[p, :, j * width : (j + 1) * width] for p in range(depth)] for j in range(3))
    _, probs = attend(q, k, v)
    grads = attend_back(q, k, v, probs, [ctx[p] for p in range(depth)])
    for p in range(depth):
        for j in range(3):
            qkv[p, :, j * width : (j + 1) * width] = grads[j][p]
    for t in range(depth):
        outs[t][...] = qkv[me_ref[0] ^ t]


def attend_back_pieces(got, got_context, me):
    depth = len(got)
    rows, wide = got[0].shape
    return vmem_call(
        functools.partial(attend_back_kernel, depth),
        [sds((rows, wide), BF)] * depth,
        *got,
        *got_context,
        index=me,
        scratch=[pltpu.VMEM((depth, rows, wide), BF), pltpu.VMEM((depth, rows, wide // 3), BF)],
        flops=depth * rows * wide * 100,
    )


def attn_out_kernel(depth, width, me_ref, *refs):
    got = refs[:depth]
    w_ref = refs[depth]
    ctx_ref, near_ref, far_ref = refs[depth + 1 : depth + 4]
    by_chunk = refs[depth + 4]
    for t in range(depth):
        by_chunk[me_ref[0] ^ t] = got[t][...]
    rows = by_chunk.shape[1]
    half = depth // 2
    for c in range(depth):
        ctx_ref[c * rows : (c + 1) * rows, :] = by_chunk[c]
        out = near_ref if c < half else far_ref
        at = (c % half) * rows
        out[at : at + rows, :] = mm_nt(by_chunk[c], w_ref[:, 3 * width :]).astype(BF)


def attn_out_terms(got, attn_w, me):
    depth = len(got)
    rows, width = got[0].shape
    model = attn_w.shape[0]
    tokens = depth * rows
    return vmem_call(
        functools.partial(attn_out_kernel, depth, width),
        [sds((tokens, width), BF)] + [sds((tokens // 2, model), BF)] * 2,
        *got,
        attn_w,
        index=me,
        scratch=[pltpu.VMEM((depth, rows, width), BF)],
        flops=2 * tokens * width * model,
    )


def join_kernel(chips, *refs):
    terms = refs[:chips]
    rows_ref, mask_ref, gain_ref = refs[chips : chips + 3]
    hidden_ref, normed_ref = refs[chips + 3 :]
    hidden = rows_ref[...] + mask_ref[:, :1] * sum_refs(terms)
    hidden_ref[...] = hidden
    normed_ref[...] = rms_forward(hidden, gain_ref[...])[2]


def join_rows(terms, rows_in, mask, gain):
    shape = rows_in.shape
    return vmem_call(
        functools.partial(join_kernel, len(terms)),
        [sds(shape, F32), sds(shape, BF)],
        *terms,
        rows_in,
        mask,
        gain[None],
    )


def norm_back_kernel(chips, _, *refs):
    terms = refs[:chips]
    rows_ref, grad_ref, mask_ref, gain_ref = refs[chips : chips + 4]
    out_ref, masked_ref, gain_out_ref = refs[chips + 4 :]
    grad_normed = sum_refs(terms)
    unit_rows, inv_rms, _ = rms_forward(rows_ref[...], gain_ref[...])
    grad = grad_ref[...] + rms_backward(grad_normed, unit_rows, inv_rms, gain_ref[...])
    out_ref[...] = grad
    masked_ref[...] = (mask_ref[:, :1] * grad).astype(BF)
    gain_out_ref[...] = jnp.sum(grad_normed * unit_rows, axis=0, keepdims=True)


def norm_back(terms, rows, grad_rows, mask, gain, index):
    shape = rows.shape
    return vmem_call(
        functools.partial(norm_back_kernel, len(terms)),
        [sds(shape, F32), sds(shape, BF), sds((1, shape[1]), F32)],
        *terms,
        rows,
        grad_rows,
        mask,
        gain[None],
        index=index,
    )


def finish_kernel(depth, chips, me_ref, *refs):
    terms, ffn_terms = refs[:chips], refs[chips : 2 * chips]
    rows_ref, grad_ref, hidden_ref, mask_ref, gain_ref = refs[2 * chips : 2 * chips + 5]
    outs = refs[2 * chips + 5 : -2]
    output, input_grad = refs[-2:]
    unit_rows, inv_rms, _ = rms_forward(rows_ref[...], gain_ref[...])
    grad = rms_backward(sum_refs(terms), unit_rows, inv_rms, gain_ref[...])
    output[...] = (hidden_ref[...] + mask_ref[:, :1] * sum_refs(ffn_terms)).astype(BF)
    input_grad[...] = (grad_ref[...] + grad).astype(BF)
    share = outs[0].shape[1]
    for t, ref in enumerate(outs):
        at = pl.ds(pl.multiple_of((me_ref[0] ^ t) * share, share), share)
        ref[0] = output[at, :]
        ref[1] = input_grad[at, :]


def finish_rows(terms, ffn_terms, rows, grad_rows, hidden, mask, gain, me, depth):
    tokens, model = rows.shape
    return vmem_call(
        functools.partial(finish_kernel, depth, len(terms)),
        [sds((2, tokens // depth, model), BF)] * depth,
        *terms,
        *ffn_terms,
        rows,
        grad_rows,
        hidden,
        mask,
        gain[None],
        index=me,
        vmem=56,
        scratch=[pltpu.VMEM((tokens, model), BF)] * 2,
    )


def by_position_kernel(depth, me_ref, *refs):
    for t in range(depth):
        refs[depth][me_ref[0] ^ t] = refs[t][...]


def by_position(got, me):
    return vmem_call(
        functools.partial(by_position_kernel, len(got)),
        [sds((len(got),) + got[0].shape, got[0].dtype)],
        *got,
        index=me,
    )[0]


def whole_frames_kernel(parts, me_ref, *refs):
    share = refs[0].shape[2]
    for t in range(parts):
        at = pl.ds(pl.multiple_of((me_ref[0] ^ t) * share, share), share)
        for p in range(refs[0].shape[0]):
            for j in range(2):
                refs[parts + j][p, at, :] = refs[t][p, j]


def whole_frames(got, me):
    depth, _, share, model = got[0].shape
    return vmem_call(
        functools.partial(whole_frames_kernel, len(got)),
        [sds((depth, len(got) * share, model), BF)] * 2,
        *got,
        index=me,
    )


def ffn_tile(x, g, w_ref, hidden):
    gate_up = mm(x, w_ref[:, : 2 * hidden])
    gate_pre = gate_up[:, :hidden]
    up_proj = gate_up[:, hidden:]
    sig = jax.nn.sigmoid(gate_pre)
    acts = (gate_pre * sig * up_proj).astype(BF)
    grad_act = mm(g, w_ref[:, 2 * hidden :])
    grad_gate = (grad_act * up_proj * sig * (1.0 + gate_pre * (1.0 - sig))).astype(BF)
    grad_up = (grad_act * gate_pre * sig).astype(BF)
    return acts, grad_gate, grad_up


def ffn_kernel(x_ref, g_ref, w_ref, acts_ref, grads_ref, near_ref, far_ref):
    hidden = w_ref.shape[1] // 3
    half = near_ref.shape[0]
    for j, out_ref in enumerate((near_ref, far_ref)):
        at = slice(j * half, (j + 1) * half)
        acts, grad_gate, grad_up = ffn_tile(x_ref[at, :], g_ref[at, :], w_ref, hidden)
        acts_ref[at, :] = acts
        grads_ref[at, :hidden] = grad_gate
        grads_ref[at, hidden:] = grad_up
        out_ref[...] = mm_nt(grads_ref[at, :], w_ref[:, : 2 * hidden]).astype(BF)


def ffn_block(normed, grad_ffn, ffn_w):
    tokens, model = normed.shape
    hidden = ffn_w.shape[1] // 3
    return vmem_call(
        ffn_kernel,
        [sds((tokens, hidden), BF), sds((tokens, 2 * hidden), BF)]
        + [sds((tokens // 2, model), BF)] * 2,
        normed,
        grad_ffn,
        ffn_w,
        flops=10 * tokens * hidden * model,
    )


def weight_grad_kernel(count, *refs):
    out_ref, square_ref = refs[2 * count :]
    total = jnp.zeros((1, 128), F32)
    lane = 0
    for i in range(count):
        left, right = refs[2 * i], refs[2 * i + 1]
        width = right.shape[1]
        grads = mm_tn(left[...], right[...])
        out_ref[:, lane : lane + width] = grads.astype(BF)
        squares = jnp.sum(grads * grads, axis=0, keepdims=True)
        for j in range(0, width, 128):
            total = total + squares[:, j : j + 128]
        lane += width

    @pl.when(pl.program_id(0) == 0)
    def _():
        square_ref[...] = total

    @pl.when(pl.program_id(0) > 0)
    def _():
        square_ref[...] += total


def weight_grads(*pairs):
    owners = axis_total(OWNERS)
    tokens, model = pairs[0][0].shape
    widths = [last - first for _, _, first, last in pairs]
    width = sum(widths)
    if lax.axis_size("rf") > 1 or any(w % 128 for w in widths):
        grads = [mm_tn(left, right[:, first:last]) for left, right, first, last in pairs]
        grads = jnp.concatenate(grads, 1)
        if lax.axis_size("rf") > 1:
            grads = grads.reshape(lax.axis_size("pz"), lax.axis_size("rf"), -1, width)
            grads = lax.psum_scatter(grads, "rf", scatter_dimension=1)
        squares = jnp.sum((grads * grads).reshape(-1, 128), axis=0, keepdims=True)
        return grads.astype(BF).reshape(owners, -1, width), squares
    step = 512
    in_specs = []
    for (_, _, first, _), w in zip(pairs, widths):
        in_specs.append(pl.BlockSpec((tokens, step), lambda i: (0, i)))
        in_specs.append(pl.BlockSpec((tokens, w), lambda i, at=first // w: (0, at)))
    out, squares = pl.pallas_call(
        functools.partial(weight_grad_kernel, len(pairs)),
        out_shape=[sds((model, width), BF), sds((1, 128), F32)],
        grid=(model // step,),
        in_specs=in_specs,
        out_specs=[
            pl.BlockSpec((step, width), lambda i: (i, 0)),
            pl.BlockSpec((1, 128), lambda i: (0, 0)),
        ],
        compiler_params=pltpu.CompilerParams(vmem_limit_bytes=VMEM_LIMIT),
        cost_estimate=pl.CostEstimate(
            flops=2 * tokens * model * width,
            bytes_accessed=2 * (tokens * (2 * model + width) + model * width),
            transcendentals=0,
        ),
        name="weight_grads",
    )(*[v for left, right, _, _ in pairs for v in (left, right)])
    return out.reshape(owners, -1, width), squares


def context_kernel(depth, width, *refs):
    me_ref = refs[0]
    parts = len(refs) - 4 - depth
    pieces = refs[1 : 1 + parts]
    w_ref = refs[1 + parts]
    rows_ref = refs[2 + parts]
    outs = refs[3 + parts : 3 + parts + depth]
    by_chunk = refs[-1]
    stack_kernel(*pieces, rows_ref)
    rows = by_chunk.shape[1]
    for c in range(depth):
        by_chunk[c] = mm(rows_ref[c * rows : (c + 1) * rows, :], w_ref[:, 3 * width :]).astype(BF)
    for t in range(depth):
        outs[t][...] = by_chunk[me_ref[0] ^ t]


def context_grads(pieces, attn_w, width, me, depth):
    tokens = sum(p.shape[0] for p in pieces)
    rows = tokens // depth
    out = vmem_call(
        functools.partial(context_kernel, depth, width),
        [sds((tokens, attn_w.shape[0]), BF)] + [sds((rows, width), BF)] * depth,
        *pieces,
        attn_w,
        index=me,
        scratch=[pltpu.VMEM((depth, rows, width), BF)],
        flops=2 * tokens * width * attn_w.shape[0],
    )
    return out[0], out[1:]


def qkv_back_kernel(depth, width, me_ref, *refs):
    got = refs[:depth]
    w_ref, normed_ref, gain_ref, rows_ref, near_ref, far_ref, gain_out_ref, by_chunk = refs[depth:]
    for t in range(depth):
        by_chunk[me_ref[0] ^ t] = got[t][...]
    rows = by_chunk.shape[1]
    half = depth // 2
    total = jnp.zeros(gain_out_ref.shape, F32)
    for c in range(depth):
        here = slice(c * rows, (c + 1) * rows)
        rows_ref[here, :] = by_chunk[c]
        out = near_ref if c < half else far_ref
        at = (c % half) * rows
        terms = mm_nt(by_chunk[c], w_ref[:, : 3 * width])
        out[at : at + rows, :] = terms.astype(BF)
        total = total + jnp.sum(terms * normed_ref[here, :].astype(F32), axis=0, keepdims=True)
    gain_out_ref[...] = total / gain_ref[...]


def qkv_back(got, attn_w, normed, gain, width, me):
    depth = len(got)
    rows = got[0].shape[0]
    tokens = depth * rows
    model = attn_w.shape[0]
    return vmem_call(
        functools.partial(qkv_back_kernel, depth, width),
        [sds((tokens, 3 * width), BF)]
        + [sds((tokens // 2, model), BF)] * 2
        + [sds((1, model), F32)],
        *got,
        attn_w,
        normed,
        gain[None],
        index=me,
        scratch=[pltpu.VMEM((depth, rows, 3 * width), BF)],
        flops=6 * tokens * width * model,
    )


def attn_grads_kernel(depth, width, me_ref, *refs):
    got = refs[:depth]
    w_ref, normed_ref, grad_ref, context_ref, gain_ref, gain2_ref, square_ref = refs[depth : depth + 7]
    near_ref, far_ref, chunk_ref, total_ref, by_chunk, grads = refs[depth + 7 :]
    for t in range(depth):
        by_chunk[me_ref[0] ^ t] = got[t][...]
    rows = by_chunk.shape[1]
    half = depth // 2
    total = jnp.zeros(gain_ref.shape, F32)
    for c in range(depth):
        here = slice(c * rows, (c + 1) * rows)
        grads[here, :] = by_chunk[c]
        out = near_ref if c < half else far_ref
        at = (c % half) * rows
        terms = mm_nt(by_chunk[c], w_ref[:, : 3 * width])
        out[at : at + rows, :] = terms.astype(BF)
        total = total + jnp.sum(terms * normed_ref[here, :].astype(F32), axis=0, keepdims=True)
    total_ref[0:1, :] = total / gain_ref[...]
    total_ref[1:2, :] = gain2_ref[...]
    squares = square_ref[...]
    for first, left, right in ((0, normed_ref, grads), (3 * width, grad_ref, context_ref)):
        chunk = mm_tn(left[...], right[...])
        last = first + chunk.shape[1]
        chunk_ref[:, first:last] = chunk.astype(BF)
        column = jnp.sum(chunk * chunk, axis=0, keepdims=True)
        for j in range(0, last - first, 128):
            squares = squares + column[:, j : j + 128]
    total_ref[2:3, :] = jnp.zeros(gain_ref.shape, F32)
    total_ref[2:3, :128] = squares


def attn_grads(got, attn_w, normed, grad_attn, context, gain, gain_part2, squares, me):
    depth = len(got)
    rows, wide = got[0].shape
    width = wide // 3
    tokens = depth * rows
    model = attn_w.shape[0]
    if lax.axis_size("rf") > 1 or width % 128:
        grads, near, far, gain_part1 = qkv_back(got, attn_w, normed, gain, width, me)
        chunks, more = weight_grads((normed, grads, 0, wide), (grad_attn, context, 0, width))
        squares = jnp.pad(squares + more, ((0, 0), (0, model - 128)))
        return near, far, chunks, jnp.concatenate([gain_part1, gain_part2, squares], 0)
    near, far, chunks, total = vmem_call(
        functools.partial(attn_grads_kernel, depth, width),
        [sds((tokens // 2, model), BF)] * 2 + [sds((model, 4 * width), BF), sds((3, model), F32)],
        *got,
        attn_w,
        normed,
        grad_attn,
        context,
        gain[None],
        gain_part2,
        squares,
        index=me,
        scratch=[pltpu.VMEM((depth, rows, wide), BF), pltpu.VMEM((tokens, wide), BF)],
        flops=14 * tokens * width * model,
        vmem=56,
    )
    return near, far, chunks.reshape(axis_total(OWNERS), -1, 4 * width), total


OWNERS = ("pz", "rs")


def lanes_view(array):
    rows, kinds, depth, cols = array.shape
    split = array.reshape(rows, kinds, depth, cols // 128, 128)
    return split.transpose(0, 1, 3, 2, 4).reshape(-1, 128)


def lanes_back(view, shape):
    rows, kinds, depth, cols = shape
    split = view.reshape(rows, kinds, cols // 128, depth, 128)
    return split.transpose(0, 1, 3, 2, 4).reshape(shape)


def tiles_of(dims, pieces):
    kinds, tiles, depth, parts = dims
    per = tiles // parts
    for number, piece in enumerate(pieces):
        lane = 0
        for k, first, count in piece:
            for t in range(first, first + count):
                for part in range(parts):
                    for p in range(depth):
                        at = (k * tiles + part * per + t) * depth + p
                        yield at, p * parts + part, number, lane
                lane += 128


def widths_of(pieces):
    return [128 * sum(count for _, _, count in piece) for piece in pieces]


def whole_message(kinds, cols):
    return [[(k, 0, cols // 128) for k in range(kinds)]]


def split_kernel(dims, pieces, w_ref, *out_refs):
    kinds, tiles, depth, _ = dims
    rows = out_refs[0].shape[1]
    for at, chunk, number, lane in tiles_of(dims, pieces):
        values = w_ref[pl.ds(at, rows, stride=kinds * tiles * depth), :]
        out_refs[number][chunk, :, lane : lane + 128] = values.astype(BF)


def in_blocks(kernel, grid, in_specs, out_shape, out_specs, args, vmem, scalars=(), scratch=(), **more):
    n_in, n_out, n_scalar = len(in_specs), len(out_specs), len(scalars)

    def run(*refs):
        fixed = refs[:n_scalar]
        arrays = refs[n_scalar : n_scalar + n_in + n_out]
        held = refs[n_scalar + n_in + n_out :]
        pltpu.emit_pipeline(
            lambda *blocks: kernel(*fixed, *blocks, *held),
            grid=grid,
            in_specs=in_specs,
            out_specs=out_specs,
        )(*arrays)

    return pl.pallas_call(
        run,
        out_shape=out_shape,
        in_specs=[pl.BlockSpec(memory_space=pltpu.SMEM)] * n_scalar
        + [pl.BlockSpec(memory_space=pltpu.HBM)] * n_in,
        out_specs=[pl.BlockSpec(memory_space=pltpu.HBM)] * n_out,
        scratch_shapes=list(scratch),
        compiler_params=pltpu.CompilerParams(vmem_limit_bytes=vmem << 20),
        **more,
    )(*scalars, *args)


def split_weights(weights, vmem, pieces=None):
    rows, kinds, depth, cols = weights.shape
    parts = lax.axis_size("rs")
    if (cols // parts) % 128 or rows % 16:
        low = weights.astype(BF).reshape(rows, kinds, depth, parts, cols // parts)
        return [low.transpose(2, 3, 0, 1, 4).reshape(depth * parts, rows, -1)]
    pieces = pieces or whole_message(kinds, cols // parts)
    tiles = cols // 128
    step = math.gcd(rows, 32)
    chunks = depth * parts
    return in_blocks(
        functools.partial(split_kernel, (kinds, tiles, depth, parts), pieces),
        (rows // step,),
        [pl.BlockSpec((step * kinds * tiles * depth, 128), lambda i: (i, 0))],
        [sds((chunks, rows, w), BF) for w in widths_of(pieces)],
        [pl.BlockSpec((chunks, step, w), lambda i: (0, i, 0)) for w in widths_of(pieces)],
        [lanes_view(weights)],
        vmem=vmem,
        cost_estimate=pl.CostEstimate(
            flops=weights.size, bytes_accessed=6 * weights.size, transcendentals=0
        ),
        name="split_weights",
    )


def to_planes(low):
    full = lax.all_to_all(low, OWNERS, 0, 0, tiled=True)
    if lax.axis_size("rf") > 1:
        full = full.reshape((lax.axis_size("pz"), lax.axis_size("rs")) + full.shape[1:])
        full = lax.all_gather(full, "rf", axis=1)
    return full.reshape(-1, full.shape[-1])


def to_owners(chunks):
    return lax.all_to_all(chunks, OWNERS, 0, 0, tiled=True)


def adamw_update(weights, first, second, grads, clip_factor, decay_rate, step_rate):
    clipped = clip_factor * grads
    first_new = BETA_ONE * first + (1.0 - BETA_ONE) * clipped
    second_new = BETA_TWO * second + (1.0 - BETA_TWO) * clipped * clipped
    first_hat = first_new * (1.0 / (1.0 - BETA_ONE**STEP))
    second_hat = second_new * (1.0 / (1.0 - BETA_TWO**STEP))
    new_weights = weights - step_rate * (
        first_hat / (jnp.sqrt(second_hat) + ADAM_EPS) + decay_rate * weights
    )
    return (new_weights, first_new, second_new)


def norm_of(total):
    sums = jnp.sum(total[:2] * total[:2], axis=0, keepdims=True) + total[2:3]
    return jnp.sqrt(jnp.sum(sums, axis=1, keepdims=True))


def adamw_kernel(dims, pieces, steps, stages, total_ref, *refs):
    kinds, tiles, depth, _ = dims
    n = len(pieces)
    g_refs, state, refs = refs[:n], refs[n : n + 3], refs[n + 3 :]
    stage_refs, new_refs, staged_refs = refs[:stages], refs[stages : stages + 3], refs[stages + 3 :]
    staged_refs, refs = staged_refs[:stages], staged_refs[stages:]
    g_held, refs = refs[:n], refs[n:]
    here = len(refs) == 6
    state_held, refs = (state, refs) if here else (refs[:3], refs[3:])
    new_held, grads, in_sems, out_sems = refs[:3], refs[3], refs[4], refs[5]
    rows, units, _ = grads.shape
    count = rows * units
    places = {at: (number, chunk, lane) for at, chunk, number, lane in tiles_of(dims, pieces)}

    def fetches(i):
        some = pl.ds(pl.multiple_of(i * rows, rows), rows)
        pairs = [(g.at[:, some, :], held.at[:, some, :]) for g, held in zip(g_refs, g_held)]
        if not here:
            some = pl.ds(pl.multiple_of(i * count, count), count)
            pairs += [(v.at[some, :], held.at[some, :]) for v, held in zip(state, state_held)]
        return [pltpu.make_async_copy(*pair, in_sems.at[i, j]) for j, pair in enumerate(pairs)]

    def stores(i):
        some = pl.ds(pl.multiple_of(i * count, count), count)
        pairs = [(held.at[some, :], new.at[some, :]) for held, new in zip(new_held, new_refs)]
        return [pltpu.make_async_copy(*pair, out_sems.at[i, j]) for j, pair in enumerate(pairs)]

    staging = [
        pltpu.make_async_copy(source, to, out_sems.at[steps, j])
        for j, (source, to) in enumerate(zip(stage_refs, staged_refs))
    ]

    @pl.loop(0, steps)
    def _(i):
        for copy in fetches(i):
            copy.start()

    for copy in staging:
        copy.start()
    clip = CLIP_NORM / jnp.maximum(norm_of(total_ref[...]), CLIP_NORM)

    @pl.loop(0, steps)
    def _(i):
        for copy in fetches(i):
            copy.wait()
        some = pl.ds(pl.multiple_of(i * rows, rows), rows)
        for first in range(0, units, 8):
            tile = [
                g_held[number][chunk, some, lane : lane + 128].astype(F32)
                for number, chunk, lane in (places[at] for at in range(first, first + 8))
            ]
            grads[:, first : first + 8, :] = jnp.swapaxes(jnp.stack(tile), 0, 1)

        @pl.loop(0, rows)
        def _(row):
            at = pl.ds(pl.multiple_of(i * count + row * units, units), units)
            new = adamw_update(
                *(held[at, :] for held in state_held), grads[row], clip, WEIGHT_DECAY, LEARN_RATE
            )
            for held, values in zip(new_held, new):
                held[at, :] = values

        for copy in stores(i):
            copy.start()

    @pl.loop(0, steps)
    def _(i):
        for copy in stores(i):
            copy.wait()

    for copy in staging:
        copy.wait()


def adamw_owned(state, chunks, total, shape, pieces=None, stage=(), here=False):
    rows, kinds, depth, cols = shape
    parts = lax.axis_size("rs")
    pieces = pieces or whole_message(kinds, cols // parts)
    units = kinds * cols // 128 * depth
    step = math.gcd(rows, 16)
    steps = rows // step
    anywhere = pl.BlockSpec(memory_space=pl.ANY)
    inside = pl.BlockSpec(memory_space=pltpu.VMEM)
    view = state[0].shape
    out = pl.pallas_call(
        functools.partial(
            adamw_kernel, (kinds, cols // 128, depth, parts), pieces, steps, len(stage)
        ),
        out_shape=[sds(view, F32)] * 3 + [sds(v.shape, F32) for v in stage],
        in_specs=[inside]
        + [anywhere] * len(chunks)
        + [inside if here else anywhere] * 3
        + [anywhere] * len(stage),
        out_specs=[anywhere] * 3 + [inside] * len(stage),
        scratch_shapes=[pltpu.VMEM(v.shape, BF) for v in chunks]
        + [pltpu.VMEM(view, F32)] * (3 if here else 6)
        + [pltpu.VMEM((step, units, 128), F32)]
        + [pltpu.SemaphoreType.DMA((steps, len(chunks) + 3))]
        + [pltpu.SemaphoreType.DMA((steps + 1, 3))],
        compiler_params=pltpu.CompilerParams(vmem_limit_bytes=(20 if here else 52) << 20),
        cost_estimate=pl.CostEstimate(
            flops=20 * math.prod(shape), bytes_accessed=26 * math.prod(shape), transcendentals=0
        ),
        name="adamw",
    )(total, *chunks, *state, *stage)
    return out[:3], out[3:]


def body(
    inputs,
    depth_counts,
    out_grad,
    attn_weight,
    attn_first,
    attn_second,
    ffn_weight,
    ffn_first,
    ffn_second,
    norm_gains,
    gain_first,
    gain_second,
):
    depth, frames, model = inputs.shape
    mp_axes = ("mx", "mc")
    share = frames // axis_total(mp_axes)
    gain_attn = norm_gains[0]
    gain_ffn = norm_gains[1]

    me = lax.axis_index("pz")
    positions = ("pz",)
    per = ffn_weight.shape[3] // lax.axis_size("rs") // 128
    packed = pack_rows(inputs, out_grad, depth_counts, me, linear_index(mp_axes), share)
    packed = swap_parts(packed, positions)
    attn_low = split_weights(attn_weight, 48)[0]
    rows_in, rows_grad, mask, normed1_rows, masked = unpack_rows(packed, gain_attn, me)
    attn_w = to_planes(after(attn_low, normed1_rows))
    ffn_low = split_weights(ffn_weight, 48)[0]
    width = attn_w.shape[1] // 4
    normed1_pieces = gather_pieces(normed1_rows)
    grad_ffn = stack_rows(gather_pieces(masked))

    normed1, qkv = project(normed1_pieces, attn_w, width, after(me.reshape(1), ffn_low), depth)
    qkv = swap_parts(qkv, positions)
    context = swap_parts(attend_pieces(qkv, me), positions)
    ffn_w = to_planes(after(ffn_low, *context))
    context, near, far = attn_out_terms(context, attn_w, me)
    hidden_in, normed2_rows = join_rows(scatter_pieces(near, far), rows_in, mask, gain_ffn)
    normed2 = stack_rows(gather_pieces(normed2_rows))

    acts, gate_up_grads, near, far = ffn_block(normed2, grad_ffn, ffn_w)
    terms = scatter_pieces(near, far)
    hidden = acts.shape[1]
    pieces = [[(0, 0, per), (1, 0, per)], [(2, 0, per)]]
    chunks_a, squares_a = weight_grads((normed2, gate_up_grads, 0, 2 * hidden))
    owned_a = to_owners(chunks_a)
    chunks_b, squares_b = weight_grads((grad_ffn, acts, 0, hidden))

    ffn_terms = mm_nt(acts, ffn_w[:, 2 * hidden :]).astype(BF)

    grad_hidden, masked, gain_part2 = norm_back(
        terms, hidden_in, rows_grad, mask, gain_ffn, after(me.reshape(1), chunks_b, ffn_terms)
    )
    grad_attn, grad_context = context_grads(gather_pieces(masked), attn_w, width, me, depth)
    grad_context = swap_parts(grad_context, positions)
    grad_qkv = swap_parts(attend_back_pieces(qkv, grad_context, me), positions)
    half = ffn_terms.shape[0] // 2
    ffn_terms = scatter_pieces(ffn_terms[:half], ffn_terms[half:])
    owned_b = to_owners(after(chunks_b, *grad_qkv, *ffn_terms[1:]))
    near, far, attn_chunks, total = attn_grads(
        grad_qkv,
        attn_w,
        normed1,
        grad_attn,
        context,
        gain_attn,
        gain_part2,
        squares_a + squares_b,
        after(me.reshape(1), owned_a),
    )
    terms = scatter_pieces(near, far)

    if lax.axis_size("rf") > 1:
        total = lax.psum(total, "rf")
    total = all_sum(all_sum(total, mp_axes), ("rs",))
    total = all_sum(after(total, *terms[1:]), positions)
    back = finish_rows(
        terms, ffn_terms, rows_in, grad_hidden, hidden_in, mask, gain_attn, me, depth
    )
    back = swap_parts(back, positions)
    attn_owned = to_owners(after(attn_chunks, total, owned_b, *back[1:]))

    back = by_position(back, me)
    back = swap_parts([back] * axis_total(mp_axes), mp_axes)
    output, input_grad = whole_frames(back, linear_index(mp_axes))

    gain_grad = total[:2]
    grad_norm = norm_of(total)[0, 0]
    clip_factor = CLIP_NORM / jnp.maximum(grad_norm, CLIP_NORM)

    ffn_state = [lanes_view(v) for v in (ffn_weight, ffn_first, ffn_second)]
    attn_state = [lanes_view(v) for v in (attn_weight, attn_first, attn_second)]
    ffn_new, _ = adamw_owned(ffn_state, [owned_a, owned_b], total, ffn_weight.shape, pieces)
    if width % 128:
        grads = attn_owned.reshape(depth, lax.axis_size("rs"), -1, 4, width)
        grads = grads.transpose(2, 3, 0, 1, 4).reshape(attn_weight.shape).astype(F32)
        attn_new = adamw_update(
            attn_weight, attn_first, attn_second, grads, clip_factor, WEIGHT_DECAY, LEARN_RATE
        )
    else:
        attn_new, _ = adamw_owned(
            attn_state, [attn_owned], after(total, ffn_new[0], output), attn_weight.shape
        )
        attn_new = tuple(lanes_back(v, attn_weight.shape) for v in attn_new)
    ffn_new = tuple(lanes_back(v, ffn_weight.shape) for v in ffn_new)

    gain_new = adamw_update(
        norm_gains, gain_first, gain_second, gain_grad, clip_factor, 0.0, GAIN_RATE
    )
    return (output, input_grad, grad_norm) + attn_new + ffn_new + gain_new


def solution(mesh):
    dp = mesh.shape["dp"]
    mp = mesh.shape["mp"]

    def run(*args):
        depth, _, model = args[0].shape
        heads = args[3].shape[3] // mp // HD
        parts = math.gcd(dp // depth, heads)
        fine = Mesh(
            mesh.devices.reshape(depth, dp // depth // parts, parts, mp // 2, 2),
            ("pz", "rf", "rs", "mx", "mc"),
        )
        rows = ("pz", "rf", "rs")
        cols = ("mx", "mc")
        acts = P(None, rows, None)
        weight = P(rows, None, None, cols)
        return jax.shard_map(
            body,
            mesh=fine,
            in_specs=(acts, P(rows), acts) + (weight,) * 6 + (P(),) * 3,
            out_specs=(acts, acts, P()) + (weight,) * 6 + (P(),) * 3,
            check_vma=False,
        )(*args)

    return run
```

```python
import functools
import math

import jax
import jax.numpy as jnp
from jax import lax
from jax.experimental import pallas as pl
from jax.experimental.pallas import tpu as pltpu
from jax.sharding import Mesh, PartitionSpec as P

HD = 64
STEP = 5
NORM_EPS = 1e-05
BETA_ONE = 0.5
BETA_TWO = 0.5
LEARN_RATE = 0.02
GAIN_RATE = 0.4
WEIGHT_DECAY = 0.1
ADAM_EPS = 1e-08
CLIP_NORM = 1.0

VMEM_LIMIT = 16 << 20

BF = jnp.bfloat16
F32 = jnp.float32


def axis_total(axes):
    return math.prod(lax.axis_size(a) for a in axes)


def linear_index(axes):
    index = 0
    for a in axes:
        index = index * lax.axis_size(a) + lax.axis_index(a)
    return index


def hop(value, axes, step):
    n = axis_total(axes)
    return lax.ppermute(value, axes, [(i, i ^ step) for i in range(n)])


def take(stack, index):
    return lax.dynamic_index_in_dim(stack, index, 0, keepdims=False)


def put(stack, value, index):
    return lax.dynamic_update_index_in_dim(stack, value, index, 0)


def gather_parts(parts, me):
    full = jnp.zeros((len(parts),) + parts[0].shape, parts[0].dtype)
    for s, part in enumerate(parts):
        full = put(full, part, me ^ s)
    return full


def all_to_all(stack, axes):
    n = axis_total(axes)
    me = linear_index(axes)
    parts = [take(stack, me)]
    for s in range(1, n):
        parts.append(hop(take(stack, me ^ s), axes, s))
    return gather_parts(parts, me)


def all_gather(value, axes):
    n = axis_total(axes)
    me = linear_index(axes)
    return gather_parts([value] + [hop(value, axes, s) for s in range(1, n)], me)


def tree_sum(parts):
    while len(parts) > 1:
        parts = [a + b for a, b in zip(parts[::2], parts[1::2])]
    return parts[0]


def all_sum(value, axes):
    n = axis_total(axes)
    return tree_sum([value] + [hop(value, axes, s) for s in range(1, n)])


CHIPS = ("rs", "mx")
CORES = ("mc",)


def rms_forward(values, gain):
    inv_rms = lax.rsqrt(jnp.mean(values * values, axis=-1, keepdims=True) + NORM_EPS)
    unit_rows = values * inv_rms
    return unit_rows, inv_rms, (unit_rows * gain).astype(BF)


def rms_backward(grad_normed, unit_rows, inv_rms, gain):
    scaled = grad_normed * gain
    return inv_rms * (scaled - unit_rows * jnp.mean(scaled * unit_rows, axis=-1, keepdims=True))


def mm(a, b):
    return jnp.dot(a, b, preferred_element_type=F32)


def mm_nt(a, b):
    return lax.dot_general(a, b, (((1,), (1,)), ((), ())), preferred_element_type=F32)


def mm_tn(a, b):
    return lax.dot_general(a, b, (((0,), (0,)), ((), ())), preferred_element_type=F32)


def head_sums(products):
    width = products.shape[-1]
    head_in = lax.broadcasted_iota(jnp.int32, (width, width), 0) // HD
    head_out = lax.broadcasted_iota(jnp.int32, (width, width), 1) // HD
    ones = jnp.where(head_in == head_out, 1.0, 0.0).astype(BF)
    high = products.astype(BF)
    low = (products - high.astype(F32)).astype(BF)
    return mm(high, ones) + mm(low, ones)


def attend(query, key, value):
    depth = len(query)
    q32, k32, v32 = ([v.astype(F32) for v in rows] for rows in (query, key, value))
    pairs = [(p, q) for p in range(depth) for q in range(p + 1)]
    rows = query[0].shape[0]
    sums = head_sums(jnp.concatenate([q32[p] * k32[q] for p, q in pairs], 0)) * HD ** (-0.5)
    scores = {pq: sums[i * rows : (i + 1) * rows] for i, pq in enumerate(pairs)}
    probs = {}
    context = []
    for p in range(depth):
        top = scores[p, 0]
        for q in range(1, p + 1):
            top = jnp.maximum(top, scores[p, q])
        terms = [jnp.exp(scores[p, q] - top) for q in range(p + 1)]
        scale = 1.0 / sum(terms[1:], terms[0])
        acc = 0.0
        for q in range(p + 1):
            probs[p, q] = terms[q] * scale
            acc = acc + probs[p, q].astype(BF).astype(F32) * v32[q]
        context.append(acc.astype(BF))
    return context, probs


def attend_back(query, key, value, probs, grad_context):
    depth = len(query)
    q32, k32, v32, g32 = ([v.astype(F32) for v in r] for r in (query, key, value, grad_context))
    pairs = [(p, q) for p in range(depth) for q in range(p + 1)]
    rows = query[0].shape[0]
    sums = head_sums(jnp.concatenate([g32[p] * v32[q] for p, q in pairs], 0))
    grad_probs = {pq: sums[i * rows : (i + 1) * rows] for i, pq in enumerate(pairs)}
    grad_scores = {}
    for p in range(depth):
        inner = sum(probs[p, q] * grad_probs[p, q] for q in range(p + 1))
        for q in range(p + 1):
            low = (probs[p, q] * (grad_probs[p, q] - inner)).astype(BF)
            grad_scores[p, q] = low.astype(F32)
    scale = HD ** (-0.5)
    grad_query, grad_key, grad_value = [], [], []
    for p in range(depth):
        later = range(p, depth)
        grad_query.append(
            (scale * sum(grad_scores[p, q] * k32[q] for q in range(p + 1))).astype(BF)
        )
        grad_key.append((scale * sum(grad_scores[o, p] * q32[o] for o in later)).astype(BF))
        grad_value.append(
            sum(probs[o, p].astype(BF).astype(F32) * g32[o] for o in later).astype(BF)
        )
    return grad_query, grad_key, grad_value


def vmem_call(kernel, outs, *args, index=None, scratch=(), flops=0, vmem=None):
    size = sum(v.size * v.dtype.itemsize for v in args)
    size += sum(math.prod(v.shape) * v.dtype.itemsize for v in outs)
    first = () if index is None else (jnp.reshape(index, (-1,)).astype(jnp.int32),)
    array = pl.BlockSpec() if vmem else pl.BlockSpec(memory_space=pltpu.VMEM)
    return pl.pallas_call(
        kernel,
        out_shape=list(outs),
        in_specs=[pl.BlockSpec(memory_space=pltpu.SMEM)] * len(first) + [array] * len(args),
        out_specs=[array] * len(outs),
        scratch_shapes=list(scratch),
        compiler_params=pltpu.CompilerParams(
            vmem_limit_bytes=vmem << 20 if vmem else VMEM_LIMIT
        ),
        cost_estimate=pl.CostEstimate(flops=flops, bytes_accessed=size, transcendentals=0),
        name=getattr(kernel, "func", kernel).__name__,
    )(*first, *args)


def sds(shape, dtype):
    return jax.ShapeDtypeStruct(shape, dtype)


def pass_kernel(*refs):
    pass


def after(value, *others):
    anywhere = pl.BlockSpec(memory_space=pl.ANY)
    return pl.pallas_call(
        pass_kernel,
        out_shape=sds(value.shape, value.dtype),
        in_specs=[anywhere] * (1 + len(others)),
        out_specs=anywhere,
        input_output_aliases={0: 0},
        name="after",
    )(value, *others)


def swap_parts(parts, axes):
    return [parts[0]] + [hop(part, axes, t) for t, part in enumerate(parts) if t]


def stack_kernel(*refs):
    at = 0
    for ref in refs[:-1]:
        rows = ref.shape[0]
        refs[-1][at : at + rows, :] = ref[...]
        at += rows


def stack_rows(parts):
    shape = (sum(p.shape[0] for p in parts), parts[0].shape[1])
    return vmem_call(stack_kernel, [sds(shape, parts[0].dtype)], *parts)[0]


def gather_pieces(rows):
    near = [rows] + [hop(rows, CHIPS, t) for t in range(1, axis_total(CHIPS))]
    return near + [hop(stack_rows(near), CORES, 1)]


def pair_kernel(near_ref, far_ref, *out_refs):
    rows = out_refs[0].shape[0]
    for t, ref in enumerate(out_refs):
        at = slice(t * rows, (t + 1) * rows)
        ref[...] = (near_ref[at, :].astype(F32) + far_ref[at, :].astype(F32)).astype(BF)


def scatter_pieces(near, far):
    chips = axis_total(CHIPS)
    got = hop(far, CORES, 1)
    rows = near.shape[0] // chips
    pair = vmem_call(pair_kernel, [sds((rows, near.shape[1]), BF)] * chips, near, got)
    return swap_parts(pair, CHIPS)


def sum_refs(refs):
    return tree_sum([ref[...].astype(F32) for ref in refs])


def pack_rows(inputs, out_grad, depth_counts, me, mine, share):
    depth = inputs.shape[0]
    counts = lax.dynamic_slice_in_dim(depth_counts, mine * share, share, 0)
    live = (jnp.arange(depth)[:, None] < counts[None, :]).astype(BF)
    live = jnp.broadcast_to(live[:, None, :, None], (depth, 2, share, 128))
    rows = [lax.dynamic_slice_in_dim(v, mine * share, share, 1) for v in (inputs, out_grad)]
    sent = jnp.concatenate([jnp.stack(rows, 1), live], -1)
    return [take(sent, me ^ t) for t in range(depth)]


def unpack_kernel(depth, me_ref, *refs):
    got = refs[:depth]
    gain_ref, rows_ref, grad_ref, mask_ref, normed_ref, masked_ref = refs[depth:]
    share, wide = got[0].shape[1:]
    model = rows_ref.shape[1]
    for t in range(depth):
        at = pl.ds(pl.multiple_of((me_ref[0] ^ t) * share, share), share)
        rows_ref[at, :] = got[t][0, :, :model].astype(F32)
        grad_ref[at, :] = got[t][1, :, :model].astype(F32)
        mask_ref[at, :] = got[t][0, :, model:].astype(F32)
    normed_ref[...] = rms_forward(rows_ref[...], gain_ref[...])[2]
    masked_ref[...] = (mask_ref[:, :1] * grad_ref[...]).astype(BF)


def unpack_rows(got, gain, me):
    depth = len(got)
    share, wide = got[0].shape[1:]
    shape = (depth * share, wide - 128)
    return vmem_call(
        functools.partial(unpack_kernel, depth),
        [sds(shape, F32), sds(shape, F32), sds((shape[0], 128), F32), sds(shape, BF), sds(shape, BF)],
        *got,
        gain[None],
        index=me,
    )


def project_kernel(width, parts, *refs):
    me_ref = refs[0]
    pieces = refs[1 : 1 + parts]
    w_ref = refs[1 + parts]
    normed_ref = refs[2 + parts]
    out_refs = refs[3 + parts : -1]
    all_ref = refs[-1]
    stack_kernel(*pieces, normed_ref)
    depth, rows, _ = all_ref.shape
    weights = w_ref[:, : 3 * width]
    for c in range(depth):
        all_ref[c] = mm(normed_ref[c * rows : (c + 1) * rows, :], weights).astype(BF)
    for t, ref in enumerate(out_refs):
        ref[...] = all_ref[me_ref[0] ^ t]


def project(pieces, attn_w, width, me, depth):
    tokens = sum(p.shape[0] for p in pieces)
    rows = tokens // depth
    out = vmem_call(
        functools.partial(project_kernel, width, len(pieces)),
        [sds((tokens, attn_w.shape[0]), BF)] + [sds((rows, 3 * width), BF)] * depth,
        *pieces,
        attn_w,
        index=me,
        scratch=[pltpu.VMEM((depth, rows, 3 * width), BF)],
        flops=6 * tokens * width * attn_w.shape[0],
    )
    return out[0], out[1:]


def attend_kernel(depth, me_ref, *refs):
    got = refs[:depth]
    outs = refs[depth : 2 * depth]
    qkv, ctx = refs[2 * depth :]
    width = ctx.shape[-1]
    for t in range(depth):
        qkv[me_ref[0] ^ t] = got[t][...]
    q, k, v = ([qkv[p, :, j * width : (j + 1) * width] for p in range(depth)] for j in range(3))
    context, _ = attend(q, k, v)
    for p in range(depth):
        ctx[p] = context[p]
    for t in range(depth):
        outs[t][...] = ctx[me_ref[0] ^ t]


def attend_pieces(got, me):
    depth = len(got)
    rows, wide = got[0].shape
    return vmem_call(
        functools.partial(attend_kernel, depth),
        [sds((rows, wide // 3), BF)] * depth,
        *got,
        index=me,
        scratch=[pltpu.VMEM((depth, rows, wide), BF), pltpu.VMEM((depth, rows, wide // 3), BF)],
        flops=depth * rows * wide * 60,
    )


def attend_back_kernel(depth, me_ref, *refs):
    got = refs[:depth]
    got_context = refs[depth : 2 * depth]
    outs = refs[2 * depth : 3 * depth]
    qkv, ctx = refs[3 * depth :]
    width = ctx.shape[-1]
    for t in range(depth):
        qkv[me_ref[0] ^ t] = got[t][...]
        ctx[me_ref[0] ^ t] = got_context[t][...]
    q, k, v = ([qkv[p, :, j * width : (j + 1) * width] for p in range(depth)] for j in range(3))
    _, probs = attend(q, k, v)
    grads = attend_back(q, k, v, probs, [ctx[p] for p in range(depth)])
    for p in range(depth):
        for j in range(3):
            qkv[p, :, j * width : (j + 1) * width] = grads[j][p]
    for t in range(depth):
        outs[t][...] = qkv[me_ref[0] ^ t]


def attend_back_pieces(got, got_context, me):
    depth = len(got)
    rows, wide = got[0].shape
    return vmem_call(
        functools.partial(attend_back_kernel, depth),
        [sds((rows, wide), BF)] * depth,
        *got,
        *got_context,
        index=me,
        scratch=[pltpu.VMEM((depth, rows, wide), BF), pltpu.VMEM((depth, rows, wide // 3), BF)],
        flops=depth * rows * wide * 100,
    )


def attn_out_kernel(depth, width, me_ref, *refs):
    got = refs[:depth]
    w_ref = refs[depth]
    ctx_ref, near_ref, far_ref = refs[depth + 1 : depth + 4]
    by_chunk = refs[depth + 4]
    for t in range(depth):
        by_chunk[me_ref[0] ^ t] = got[t][...]
    rows = by_chunk.shape[1]
    half = depth // 2
    for c in range(depth):
        ctx_ref[c * rows : (c + 1) * rows, :] = by_chunk[c]
        out = near_ref if c < half else far_ref
        at = (c % half) * rows
        out[at : at + rows, :] = mm_nt(by_chunk[c], w_ref[:, 3 * width :]).astype(BF)


def attn_out_terms(got, attn_w, me):
    depth = len(got)
    rows, width = got[0].shape
    model = attn_w.shape[0]
    tokens = depth * rows
    return vmem_call(
        functools.partial(attn_out_kernel, depth, width),
        [sds((tokens, width), BF)] + [sds((tokens // 2, model), BF)] * 2,
        *got,
        attn_w,
        index=me,
        scratch=[pltpu.VMEM((depth, rows, width), BF)],
        flops=2 * tokens * width * model,
    )


def join_kernel(chips, *refs):
    terms = refs[:chips]
    rows_ref, mask_ref, gain_ref = refs[chips : chips + 3]
    hidden_ref, normed_ref = refs[chips + 3 :]
    hidden = rows_ref[...] + mask_ref[:, :1] * sum_refs(terms)
    hidden_ref[...] = hidden
    normed_ref[...] = rms_forward(hidden, gain_ref[...])[2]


def join_rows(terms, rows_in, mask, gain):
    shape = rows_in.shape
    return vmem_call(
        functools.partial(join_kernel, len(terms)),
        [sds(shape, F32), sds(shape, BF)],
        *terms,
        rows_in,
        mask,
        gain[None],
    )


def norm_back_kernel(chips, _, *refs):
    terms = refs[:chips]
    rows_ref, grad_ref, mask_ref, gain_ref = refs[chips : chips + 4]
    out_ref, masked_ref, gain_out_ref = refs[chips + 4 :]
    grad_normed = sum_refs(terms)
    unit_rows, inv_rms, _ = rms_forward(rows_ref[...], gain_ref[...])
    grad = grad_ref[...] + rms_backward(grad_normed, unit_rows, inv_rms, gain_ref[...])
    out_ref[...] = grad
    masked_ref[...] = (mask_ref[:, :1] * grad).astype(BF)
    gain_out_ref[...] = jnp.sum(grad_normed * unit_rows, axis=0, keepdims=True)


def norm_back(terms, rows, grad_rows, mask, gain, index):
    shape = rows.shape
    return vmem_call(
        functools.partial(norm_back_kernel, len(terms)),
        [sds(shape, F32), sds(shape, BF), sds((1, shape[1]), F32)],
        *terms,
        rows,
        grad_rows,
        mask,
        gain[None],
        index=index,
    )


def finish_kernel(depth, chips, me_ref, *refs):
    terms, ffn_terms = refs[:chips], refs[chips : 2 * chips]
    totals, refs = refs[2 * chips : 2 * chips + 2], refs[2 * chips + 2 :]
    rows_ref, grad_ref, hidden_ref, mask_ref, gain_ref = refs[:5]
    outs, (output, input_grad) = refs[5:-2], refs[-2:]
    unit_rows, inv_rms, _ = rms_forward(rows_ref[...], gain_ref[...])
    grad = rms_backward(sum_refs(terms), unit_rows, inv_rms, gain_ref[...])
    output[...] = (hidden_ref[...] + mask_ref[:, :1] * sum_refs(ffn_terms)).astype(BF)
    input_grad[...] = (grad_ref[...] + grad).astype(BF)
    total = totals[0][...] + totals[1][...]
    high = total.astype(BF)
    low = (total - high.astype(F32)).astype(BF)
    share, model = outs[0].shape[1:]
    count = total.shape[0]
    for t, ref in enumerate(outs):
        at = pl.ds(pl.multiple_of((me_ref[0] ^ t) * share, share), share)
        ref[0] = output[at, :]
        ref[1] = input_grad[at, :]
        ref[2] = jnp.zeros((share, model), BF)
        ref[2, :count, :] = high
        ref[2, 8 : 8 + count, :] = low


def finish_rows(terms, ffn_terms, totals, rows, grad_rows, hidden, mask, gain, me, depth):
    tokens, model = rows.shape
    return vmem_call(
        functools.partial(finish_kernel, depth, len(terms)),
        [sds((3, tokens // depth, model), BF)] * depth,
        *terms,
        *ffn_terms,
        *totals,
        rows,
        grad_rows,
        hidden,
        mask,
        gain[None],
        index=me,
        scratch=[pltpu.VMEM((tokens, model), BF)] * 2,
        vmem=56,
    )


def by_position_kernel(depth, me_ref, *refs):
    rows_ref, total_ref = refs[depth:]
    count = total_ref.shape[0]
    parts = []
    for t in range(depth):
        rows_ref[me_ref[0] ^ t] = refs[t][:2]
        high, low = refs[t][2, :count, :], refs[t][2, 8 : 8 + count, :]
        parts.append(high.astype(F32) + low.astype(F32))
    total_ref[...] = tree_sum(parts)


def by_position(got, me, count):
    depth = len(got)
    _, share, model = got[0].shape
    return vmem_call(
        functools.partial(by_position_kernel, depth),
        [sds((depth, 2, share, model), BF), sds((count, model), F32)],
        *got,
        index=me,
    )


def whole_frames_kernel(parts, me_ref, *refs):
    share = refs[0].shape[2]
    for t in range(parts):
        at = pl.ds(pl.multiple_of((me_ref[0] ^ t) * share, share), share)
        for p in range(refs[0].shape[0]):
            for j in range(2):
                refs[parts + j][p, at, :] = refs[t][p, j]


def whole_frames(got, me):
    depth, _, share, model = got[0].shape
    return vmem_call(
        functools.partial(whole_frames_kernel, len(got)),
        [sds((depth, len(got) * share, model), BF)] * 2,
        *got,
        index=me,
    )


def ffn_tile(x, g, w_ref, hidden):
    gate_up = mm(x, w_ref[:, : 2 * hidden])
    gate_pre = gate_up[:, :hidden]
    up_proj = gate_up[:, hidden:]
    sig = jax.nn.sigmoid(gate_pre)
    acts = (gate_pre * sig * up_proj).astype(BF)
    grad_act = mm(g, w_ref[:, 2 * hidden :])
    grad_gate = (grad_act * up_proj * sig * (1.0 + gate_pre * (1.0 - sig))).astype(BF)
    grad_up = (grad_act * gate_pre * sig).astype(BF)
    return acts, grad_gate, grad_up


def ffn_kernel(x_ref, g_ref, w_ref, acts_ref, grads_ref, near_ref, far_ref):
    hidden = w_ref.shape[1] // 3
    half = near_ref.shape[0]
    for j, out_ref in enumerate((near_ref, far_ref)):
        at = slice(j * half, (j + 1) * half)
        acts, grad_gate, grad_up = ffn_tile(x_ref[at, :], g_ref[at, :], w_ref, hidden)
        acts_ref[at, :] = acts
        grads_ref[at, :hidden] = grad_gate
        grads_ref[at, hidden:] = grad_up
        out_ref[...] = mm_nt(grads_ref[at, :], w_ref[:, : 2 * hidden]).astype(BF)


def ffn_block(normed, grad_ffn, ffn_w):
    tokens, model = normed.shape
    hidden = ffn_w.shape[1] // 3
    return vmem_call(
        ffn_kernel,
        [sds((tokens, hidden), BF), sds((tokens, 2 * hidden), BF)]
        + [sds((tokens // 2, model), BF)] * 2,
        normed,
        grad_ffn,
        ffn_w,
        flops=10 * tokens * hidden * model,
    )


def weight_grad_kernel(count, *refs):
    out_ref, square_ref = refs[2 * count :]
    total = jnp.zeros((1, 128), F32)
    lane = 0
    for i in range(count):
        left, right = refs[2 * i], refs[2 * i + 1]
        width = right.shape[1]
        grads = mm_tn(left[...], right[...])
        out_ref[:, lane : lane + width] = grads.astype(BF)
        squares = jnp.sum(grads * grads, axis=0, keepdims=True)
        for j in range(0, width, 128):
            total = total + squares[:, j : j + 128]
        lane += width

    @pl.when(pl.program_id(0) == 0)
    def _():
        square_ref[...] = total

    @pl.when(pl.program_id(0) > 0)
    def _():
        square_ref[...] += total


def weight_grads(*pairs):
    owners = axis_total(OWNERS)
    tokens, model = pairs[0][0].shape
    widths = [last - first for _, _, first, last in pairs]
    width = sum(widths)
    if lax.axis_size("rf") > 1 or any(w % 128 for w in widths):
        grads = [mm_tn(left, right[:, first:last]) for left, right, first, last in pairs]
        grads = jnp.concatenate(grads, 1)
        if lax.axis_size("rf") > 1:
            grads = grads.reshape(lax.axis_size("pz"), lax.axis_size("rf"), -1, width)
            grads = lax.psum_scatter(grads, "rf", scatter_dimension=1)
        squares = jnp.sum((grads * grads).reshape(-1, 128), axis=0, keepdims=True)
        return grads.astype(BF).reshape(owners, -1, width), squares
    step = 512
    in_specs = []
    for (_, _, first, _), w in zip(pairs, widths):
        in_specs.append(pl.BlockSpec((tokens, step), lambda i: (0, i)))
        in_specs.append(pl.BlockSpec((tokens, w), lambda i, at=first // w: (0, at)))
    out, squares = pl.pallas_call(
        functools.partial(weight_grad_kernel, len(pairs)),
        out_shape=[sds((model, width), BF), sds((1, 128), F32)],
        grid=(model // step,),
        in_specs=in_specs,
        out_specs=[
            pl.BlockSpec((step, width), lambda i: (i, 0)),
            pl.BlockSpec((1, 128), lambda i: (0, 0)),
        ],
        compiler_params=pltpu.CompilerParams(vmem_limit_bytes=VMEM_LIMIT),
        cost_estimate=pl.CostEstimate(
            flops=2 * tokens * model * width,
            bytes_accessed=2 * (tokens * (2 * model + width) + model * width),
            transcendentals=0,
        ),
        name="weight_grads",
    )(*[v for left, right, _, _ in pairs for v in (left, right)])
    return out.reshape(owners, -1, width), squares


def context_kernel(depth, width, *refs):
    me_ref = refs[0]
    parts = len(refs) - 4 - depth
    pieces = refs[1 : 1 + parts]
    w_ref = refs[1 + parts]
    rows_ref = refs[2 + parts]
    outs = refs[3 + parts : 3 + parts + depth]
    by_chunk = refs[-1]
    stack_kernel(*pieces, rows_ref)
    rows = by_chunk.shape[1]
    for c in range(depth):
        by_chunk[c] = mm(rows_ref[c * rows : (c + 1) * rows, :], w_ref[:, 3 * width :]).astype(BF)
    for t in range(depth):
        outs[t][...] = by_chunk[me_ref[0] ^ t]


def context_grads(pieces, attn_w, width, me, depth):
    tokens = sum(p.shape[0] for p in pieces)
    rows = tokens // depth
    out = vmem_call(
        functools.partial(context_kernel, depth, width),
        [sds((tokens, attn_w.shape[0]), BF)] + [sds((rows, width), BF)] * depth,
        *pieces,
        attn_w,
        index=me,
        scratch=[pltpu.VMEM((depth, rows, width), BF)],
        flops=2 * tokens * width * attn_w.shape[0],
    )
    return out[0], out[1:]


def qkv_back_kernel(depth, width, me_ref, *refs):
    got = refs[:depth]
    w_ref, normed_ref, gain_ref, rows_ref, near_ref, far_ref, gain_out_ref, by_chunk = refs[depth:]
    for t in range(depth):
        by_chunk[me_ref[0] ^ t] = got[t][...]
    rows = by_chunk.shape[1]
    half = depth // 2
    total = jnp.zeros(gain_out_ref.shape, F32)
    for c in range(depth):
        here = slice(c * rows, (c + 1) * rows)
        rows_ref[here, :] = by_chunk[c]
        out = near_ref if c < half else far_ref
        at = (c % half) * rows
        terms = mm_nt(by_chunk[c], w_ref[:, : 3 * width])
        out[at : at + rows, :] = terms.astype(BF)
        total = total + jnp.sum(terms * normed_ref[here, :].astype(F32), axis=0, keepdims=True)
    gain_out_ref[...] = total / gain_ref[...]


def qkv_back(got, attn_w, normed, gain, width, me):
    depth = len(got)
    rows = got[0].shape[0]
    tokens = depth * rows
    model = attn_w.shape[0]
    return vmem_call(
        functools.partial(qkv_back_kernel, depth, width),
        [sds((tokens, 3 * width), BF)]
        + [sds((tokens // 2, model), BF)] * 2
        + [sds((1, model), F32)],
        *got,
        attn_w,
        normed,
        gain[None],
        index=me,
        scratch=[pltpu.VMEM((depth, rows, 3 * width), BF)],
        flops=6 * tokens * width * model,
    )


def attn_grads_kernel(depth, width, me_ref, *refs):
    got = refs[:depth]
    w_ref, normed_ref, gain_ref, gain2_ref, square_ref = refs[depth : depth + 5]
    near_ref, far_ref, chunk_ref, total_ref, by_chunk, grads = refs[depth + 5 :]
    for t in range(depth):
        by_chunk[me_ref[0] ^ t] = got[t][...]
    rows = by_chunk.shape[1]
    half = depth // 2
    total = jnp.zeros(gain_ref.shape, F32)
    for c in range(depth):
        here = slice(c * rows, (c + 1) * rows)
        grads[here, :] = by_chunk[c]
        out = near_ref if c < half else far_ref
        at = (c % half) * rows
        terms = mm_nt(by_chunk[c], w_ref[:, : 3 * width])
        out[at : at + rows, :] = terms.astype(BF)
        total = total + jnp.sum(terms * normed_ref[here, :].astype(F32), axis=0, keepdims=True)
    total_ref[0:1, :] = total / gain_ref[...]
    total_ref[1:2, :] = gain2_ref[...]
    chunk = mm_tn(normed_ref[...], grads[...])
    chunk_ref[...] = chunk.astype(BF)
    column = jnp.sum(chunk * chunk, axis=0, keepdims=True)
    squares = square_ref[...]
    for j in range(0, 3 * width, 128):
        squares = squares + column[:, j : j + 128]
    total_ref[2:3, :] = jnp.zeros(gain_ref.shape, F32)
    total_ref[2:3, :128] = squares


def attn_grads(got, attn_w, normed, gain, gain_part2, squares, me):
    depth = len(got)
    rows, wide = got[0].shape
    width = wide // 3
    tokens = depth * rows
    model = attn_w.shape[0]
    if lax.axis_size("rf") > 1 or width % 128:
        grads, near, far, gain_part1 = qkv_back(got, attn_w, normed, gain, width, me)
        chunks, more = weight_grads((normed, grads, 0, wide))
        squares = jnp.pad(squares + more, ((0, 0), (0, model - 128)))
        return near, far, chunks, jnp.concatenate([gain_part1, gain_part2, squares], 0)
    near, far, chunks, total = vmem_call(
        functools.partial(attn_grads_kernel, depth, width),
        [sds((tokens // 2, model), BF)] * 2 + [sds((model, wide), BF), sds((3, model), F32)],
        *got,
        attn_w,
        normed,
        gain[None],
        gain_part2,
        squares,
        index=me,
        scratch=[pltpu.VMEM((depth, rows, wide), BF), pltpu.VMEM((tokens, wide), BF)],
        flops=12 * tokens * width * model,
        vmem=56,
    )
    return near, far, chunks.reshape(axis_total(OWNERS), -1, wide), total


OWNERS = ("pz", "rs")


def lanes_view(array):
    rows, kinds, depth, cols = array.shape
    split = array.reshape(rows, kinds, depth, cols // 128, 128)
    return split.transpose(0, 1, 3, 2, 4).reshape(-1, 128)


def lanes_back(view, shape):
    rows, kinds, depth, cols = shape
    split = view.reshape(rows, kinds, cols // 128, depth, 128)
    return split.transpose(0, 1, 3, 2, 4).reshape(shape)


def tiles_of(dims, pieces):
    kinds, tiles, depth, parts = dims
    per = tiles // parts
    for number, piece in enumerate(pieces):
        lane = 0
        for k, first, count in piece:
            if k is None:
                lane += 128 * count
                continue
            for t in range(first, first + count):
                for part in range(parts):
                    for p in range(depth):
                        at = (k * tiles + part * per + t) * depth + p
                        yield at, p * parts + part, number, lane
                lane += 128


def widths_of(pieces):
    return [128 * sum(count for _, _, count in piece) for piece in pieces]


def whole_message(kinds, cols):
    return [[(k, 0, cols // 128) for k in range(kinds)]]


def split_kernel(dims, pieces, w_ref, *out_refs):
    kinds, tiles, depth, _ = dims
    rows = out_refs[0].shape[1]
    for at, chunk, number, lane in tiles_of(dims, pieces):
        values = w_ref[pl.ds(at, rows, stride=kinds * tiles * depth), :]
        out_refs[number][chunk, :, lane : lane + 128] = values.astype(BF)


def in_blocks(kernel, grid, in_specs, out_shape, out_specs, args, vmem, scalars=(), scratch=(), **more):
    n_in, n_out, n_scalar = len(in_specs), len(out_specs), len(scalars)

    def run(*refs):
        fixed = refs[:n_scalar]
        arrays = refs[n_scalar : n_scalar + n_in + n_out]
        held = refs[n_scalar + n_in + n_out :]
        pltpu.emit_pipeline(
            lambda *blocks: kernel(*fixed, *blocks, *held),
            grid=grid,
            in_specs=in_specs,
            out_specs=out_specs,
        )(*arrays)

    return pl.pallas_call(
        run,
        out_shape=out_shape,
        in_specs=[pl.BlockSpec(memory_space=pltpu.SMEM)] * n_scalar
        + [pl.BlockSpec(memory_space=pltpu.HBM)] * n_in,
        out_specs=[pl.BlockSpec(memory_space=pltpu.HBM)] * n_out,
        scratch_shapes=list(scratch),
        compiler_params=pltpu.CompilerParams(vmem_limit_bytes=vmem << 20),
        **more,
    )(*scalars, *args)


def split_weights(weights, vmem, pieces=None):
    rows, kinds, depth, cols = weights.shape
    parts = lax.axis_size("rs")
    if (cols // parts) % 128 or rows % 16:
        low = weights.astype(BF).reshape(rows, kinds, depth, parts, cols // parts)
        return [low.transpose(2, 3, 0, 1, 4).reshape(depth * parts, rows, -1)]
    pieces = pieces or whole_message(kinds, cols // parts)
    tiles = cols // 128
    step = math.gcd(rows, 32)
    chunks = depth * parts
    return in_blocks(
        functools.partial(split_kernel, (kinds, tiles, depth, parts), pieces),
        (rows // step,),
        [pl.BlockSpec((step * kinds * tiles * depth, 128), lambda i: (i, 0))],
        [sds((chunks, rows, w), BF) for w in widths_of(pieces)],
        [pl.BlockSpec((chunks, step, w), lambda i: (0, i, 0)) for w in widths_of(pieces)],
        [lanes_view(weights)],
        vmem=vmem,
        cost_estimate=pl.CostEstimate(
            flops=weights.size, bytes_accessed=6 * weights.size, transcendentals=0
        ),
        name="split_weights",
    )


def to_planes(low):
    full = lax.all_to_all(low, OWNERS, 0, 0, tiled=True)
    if lax.axis_size("rf") > 1:
        full = full.reshape((lax.axis_size("pz"), lax.axis_size("rs")) + full.shape[1:])
        full = lax.all_gather(full, "rf", axis=1)
    return full.reshape(-1, full.shape[-1])


def to_owners(chunks):
    return lax.all_to_all(chunks, OWNERS, 0, 0, tiled=True)


def adamw_update(weights, first, second, grads, clip_factor, decay_rate, step_rate):
    clipped = clip_factor * grads
    first_new = BETA_ONE * first + (1.0 - BETA_ONE) * clipped
    second_new = BETA_TWO * second + (1.0 - BETA_TWO) * clipped * clipped
    first_hat = first_new * (1.0 / (1.0 - BETA_ONE**STEP))
    second_hat = second_new * (1.0 / (1.0 - BETA_TWO**STEP))
    new_weights = weights - step_rate * (
        first_hat / (jnp.sqrt(second_hat) + ADAM_EPS) + decay_rate * weights
    )
    return (new_weights, first_new, second_new)


def norm_of(total):
    sums = jnp.sum(total[:2] * total[:2], axis=0, keepdims=True) + total[2:3]
    return jnp.sqrt(jnp.sum(sums, axis=1, keepdims=True))


def adamw_kernel(dims, pieces, steps, stages, total_ref, *refs):
    kinds, tiles, depth, _ = dims
    n = len(pieces)
    g_refs, state, refs = refs[:n], refs[n : n + 3], refs[n + 3 :]
    stage_refs, new_refs, staged_refs = refs[:stages], refs[stages : stages + 3], refs[stages + 3 :]
    staged_refs, refs = staged_refs[:stages], staged_refs[stages:]
    g_held, refs = refs[:n], refs[n:]
    here = len(refs) == 6
    state_held, refs = (state, refs) if here else (refs[:3], refs[3:])
    new_held, grads, in_sems, out_sems = refs[:3], refs[3], refs[4], refs[5]
    rows, units, _ = grads.shape
    count = rows * units
    places = {at: (number, chunk, lane) for at, chunk, number, lane in tiles_of(dims, pieces)}

    def fetches(i):
        some = pl.ds(pl.multiple_of(i * rows, rows), rows)
        pairs = [(g.at[:, some, :], held.at[:, some, :]) for g, held in zip(g_refs, g_held)]
        if not here:
            some = pl.ds(pl.multiple_of(i * count, count), count)
            pairs += [(v.at[some, :], held.at[some, :]) for v, held in zip(state, state_held)]
        return [pltpu.make_async_copy(*pair, in_sems.at[i, j]) for j, pair in enumerate(pairs)]

    def stores(i):
        some = pl.ds(pl.multiple_of(i * count, count), count)
        pairs = [(held.at[some, :], new.at[some, :]) for held, new in zip(new_held, new_refs)]
        return [pltpu.make_async_copy(*pair, out_sems.at[i, j]) for j, pair in enumerate(pairs)]

    staging = [
        pltpu.make_async_copy(source, to, out_sems.at[steps, j])
        for j, (source, to) in enumerate(zip(stage_refs, staged_refs))
    ]

    @pl.loop(0, steps)
    def _(i):
        for copy in fetches(i):
            copy.start()

    for copy in staging:
        copy.start()
    clip = CLIP_NORM / jnp.maximum(norm_of(total_ref[...]), CLIP_NORM)

    @pl.loop(0, steps)
    def _(i):
        for copy in fetches(i):
            copy.wait()
        some = pl.ds(pl.multiple_of(i * rows, rows), rows)
        for first in range(0, units, 8):
            tile = [
                g_held[number][chunk, some, lane : lane + 128].astype(F32)
                for number, chunk, lane in (places[at] for at in range(first, first + 8))
            ]
            grads[:, first : first + 8, :] = jnp.swapaxes(jnp.stack(tile), 0, 1)

        @pl.loop(0, rows)
        def _(row):
            at = pl.ds(pl.multiple_of(i * count + row * units, units), units)
            new = adamw_update(
                *(held[at, :] for held in state_held), grads[row], clip, WEIGHT_DECAY, LEARN_RATE
            )
            for held, values in zip(new_held, new):
                held[at, :] = values

        for copy in stores(i):
            copy.start()

    @pl.loop(0, steps)
    def _(i):
        for copy in stores(i):
            copy.wait()

    for copy in staging:
        copy.wait()


def adamw_owned(state, chunks, total, shape, pieces=None, stage=(), here=False):
    rows, kinds, depth, cols = shape
    parts = lax.axis_size("rs")
    pieces = pieces or whole_message(kinds, cols // parts)
    units = kinds * cols // 128 * depth
    step = math.gcd(rows, 16)
    steps = rows // step
    anywhere = pl.BlockSpec(memory_space=pl.ANY)
    inside = pl.BlockSpec(memory_space=pltpu.VMEM)
    view = state[0].shape
    out = pl.pallas_call(
        functools.partial(
            adamw_kernel, (kinds, cols // 128, depth, parts), pieces, steps, len(stage)
        ),
        out_shape=[sds(view, F32)] * 3 + [sds(v.shape, F32) for v in stage],
        in_specs=[inside]
        + [anywhere] * len(chunks)
        + [inside if here else anywhere] * 3
        + [anywhere] * len(stage),
        out_specs=[anywhere] * 3 + [inside] * len(stage),
        scratch_shapes=[pltpu.VMEM(v.shape, BF) for v in chunks]
        + [pltpu.VMEM(view, F32)] * (3 if here else 6)
        + [pltpu.VMEM((step, units, 128), F32)]
        + [pltpu.SemaphoreType.DMA((steps, len(chunks) + 3))]
        + [pltpu.SemaphoreType.DMA((steps + 1, 3))],
        compiler_params=pltpu.CompilerParams(vmem_limit_bytes=(20 if here else 52) << 20),
        cost_estimate=pl.CostEstimate(
            flops=20 * math.prod(shape), bytes_accessed=26 * math.prod(shape), transcendentals=0
        ),
        name="adamw",
    )(total, *chunks, *state, *stage)
    return out[:3], out[3:]


def body(
    inputs,
    depth_counts,
    out_grad,
    attn_weight,
    attn_first,
    attn_second,
    ffn_weight,
    ffn_first,
    ffn_second,
    norm_gains,
    gain_first,
    gain_second,
):
    depth, frames, model = inputs.shape
    mp_axes = ("mx", "mc")
    share = frames // axis_total(mp_axes)
    gain_attn = norm_gains[0]
    gain_ffn = norm_gains[1]

    me = lax.axis_index("pz")
    positions = ("pz",)
    per = ffn_weight.shape[3] // lax.axis_size("rs") // 128
    packed = pack_rows(inputs, out_grad, depth_counts, me, linear_index(mp_axes), share)
    packed = swap_parts(packed, positions)
    attn_low = split_weights(attn_weight, 48)[0]
    rows_in, rows_grad, mask, normed1_rows, masked = unpack_rows(packed, gain_attn, me)
    attn_w = to_planes(after(attn_low, normed1_rows))
    ffn_low = split_weights(ffn_weight, 48)[0]
    width = attn_w.shape[1] // 4
    normed1_pieces = gather_pieces(normed1_rows)
    grad_ffn = stack_rows(gather_pieces(masked))

    normed1, qkv = project(normed1_pieces, attn_w, width, me, depth)
    qkv = swap_parts(qkv, positions)
    context = swap_parts(attend_pieces(qkv, after(me.reshape(1), ffn_low)), positions)
    ffn_w = to_planes(after(ffn_low, *context))
    context, near, far = attn_out_terms(context, attn_w, me)
    hidden_in, normed2_rows = join_rows(scatter_pieces(near, far), rows_in, mask, gain_ffn)
    normed2 = stack_rows(gather_pieces(normed2_rows))

    acts, gate_up_grads, near, far = ffn_block(normed2, grad_ffn, ffn_w)
    terms = scatter_pieces(near, far)
    hidden = acts.shape[1]
    pieces = [[(0, 0, per), (1, 0, per)], [(2, 0, per), (None, 0, width // 128)]]
    chunks_a, squares_a = weight_grads((normed2, gate_up_grads, 0, 2 * hidden))
    owned_a = to_owners(chunks_a)
    ffn_terms = mm_nt(acts, ffn_w[:, 2 * hidden :]).astype(BF)

    grad_hidden, masked, gain_part2 = norm_back(
        terms, hidden_in, rows_grad, mask, gain_ffn, after(me.reshape(1), ffn_terms)
    )
    grad_attn, grad_context = context_grads(gather_pieces(masked), attn_w, width, me, depth)
    grad_context = swap_parts(grad_context, positions)
    grad_qkv = swap_parts(attend_back_pieces(qkv, grad_context, me), positions)
    half = ffn_terms.shape[0] // 2
    ffn_terms = scatter_pieces(ffn_terms[:half], ffn_terms[half:])
    chunks_b, squares_b = weight_grads((grad_ffn, acts, 0, hidden), (grad_attn, context, 0, width))
    owned_b = to_owners(after(chunks_b, *grad_qkv, *ffn_terms[1:]))
    near, far, attn_chunks, total = attn_grads(
        grad_qkv,
        attn_w,
        normed1,
        gain_attn,
        gain_part2,
        squares_a + squares_b,
        after(me.reshape(1), owned_a),
    )
    terms = scatter_pieces(near, far)

    if lax.axis_size("rf") > 1:
        total = lax.psum(total, "rf")
    total = all_sum(total, mp_axes)
    totals = [total] + [hop(total, ("rs",), t) for t in range(1, lax.axis_size("rs"))]
    if len(totals) != 2:
        totals = [tree_sum(totals), jnp.zeros_like(total)]
    back = finish_rows(
        terms, ffn_terms, totals, rows_in, grad_hidden, hidden_in, mask, gain_attn, me, depth
    )

    back, total = by_position(swap_parts(back, positions), me, total.shape[0])
    attn_owned = to_owners(after(attn_chunks, total, owned_b))
    back = swap_parts([back] * axis_total(mp_axes), mp_axes)
    output, input_grad = whole_frames(back, linear_index(mp_axes))

    gain_grad = total[:2]
    grad_norm = norm_of(total)[0, 0]
    clip_factor = CLIP_NORM / jnp.maximum(grad_norm, CLIP_NORM)

    ffn_state = [lanes_view(v) for v in (ffn_weight, ffn_first, ffn_second)]
    attn_state = [lanes_view(v) for v in (attn_weight, attn_first, attn_second)]
    ffn_new, _ = adamw_owned(ffn_state, [owned_a, owned_b], total, ffn_weight.shape, pieces)
    if width % 128:
        grads = jnp.concatenate([attn_owned, owned_b[:, :, hidden:]], -1)
        grads = grads.reshape(depth, lax.axis_size("rs"), -1, 4, width)
        grads = grads.transpose(2, 3, 0, 1, 4).reshape(attn_weight.shape).astype(F32)
        attn_new = adamw_update(
            attn_weight, attn_first, attn_second, grads, clip_factor, WEIGHT_DECAY, LEARN_RATE
        )
    else:
        tiles = width // 128
        attn_pieces = [[(k, 0, tiles) for k in range(3)], [(None, 0, per), (3, 0, tiles)]]
        attn_new, _ = adamw_owned(
            attn_state,
            [attn_owned, owned_b],
            after(total, ffn_new[0], output),
            attn_weight.shape,
            attn_pieces,
        )
        attn_new = tuple(lanes_back(v, attn_weight.shape) for v in attn_new)
    ffn_new = tuple(lanes_back(v, ffn_weight.shape) for v in ffn_new)

    gain_new = adamw_update(
        norm_gains, gain_first, gain_second, gain_grad, clip_factor, 0.0, GAIN_RATE
    )
    return (output, input_grad, grad_norm) + attn_new + ffn_new + gain_new


def solution(mesh):
    dp = mesh.shape["dp"]
    mp = mesh.shape["mp"]

    def run(*args):
        depth, _, model = args[0].shape
        heads = args[3].shape[3] // mp // HD
        parts = math.gcd(dp // depth, heads)
        fine = Mesh(
            mesh.devices.reshape(depth, dp // depth // parts, parts, mp // 2, 2),
            ("pz", "rf", "rs", "mx", "mc"),
        )
        rows = ("pz", "rf", "rs")
        cols = ("mx", "mc")
        acts = P(None, rows, None)
        weight = P(rows, None, None, cols)
        return jax.shard_map(
            body,
            mesh=fine,
            in_specs=(acts, P(rows), acts) + (weight,) * 6 + (P(),) * 3,
            out_specs=(acts, acts, P()) + (weight,) * 6 + (P(),) * 3,
            check_vma=False,
        )(*args)

    return run
```

```python
import functools
import math

import jax
import jax.numpy as jnp
from jax import lax
from jax.experimental import pallas as pl
from jax.experimental.pallas import tpu as pltpu
from jax.sharding import Mesh, PartitionSpec as P

HD = 64
STEP = 5
NORM_EPS = 1e-05
BETA_ONE = 0.5
BETA_TWO = 0.5
LEARN_RATE = 0.02
GAIN_RATE = 0.4
WEIGHT_DECAY = 0.1
ADAM_EPS = 1e-08
CLIP_NORM = 1.0

VMEM_LIMIT = 16 << 20

BF = jnp.bfloat16
F32 = jnp.float32


def axis_total(axes):
    return math.prod(lax.axis_size(a) for a in axes)


def linear_index(axes):
    index = 0
    for a in axes:
        index = index * lax.axis_size(a) + lax.axis_index(a)
    return index


def hop(value, axes, step):
    n = axis_total(axes)
    return lax.ppermute(value, axes, [(i, i ^ step) for i in range(n)])


def take(stack, index):
    return lax.dynamic_index_in_dim(stack, index, 0, keepdims=False)


def put(stack, value, index):
    return lax.dynamic_update_index_in_dim(stack, value, index, 0)


def gather_parts(parts, me):
    full = jnp.zeros((len(parts),) + parts[0].shape, parts[0].dtype)
    for s, part in enumerate(parts):
        full = put(full, part, me ^ s)
    return full


def all_to_all(stack, axes):
    n = axis_total(axes)
    me = linear_index(axes)
    parts = [take(stack, me)]
    for s in range(1, n):
        parts.append(hop(take(stack, me ^ s), axes, s))
    return gather_parts(parts, me)


def all_gather(value, axes):
    n = axis_total(axes)
    me = linear_index(axes)
    return gather_parts([value] + [hop(value, axes, s) for s in range(1, n)], me)


def tree_sum(parts):
    while len(parts) > 1:
        parts = [a + b for a, b in zip(parts[::2], parts[1::2])]
    return parts[0]


def all_sum(value, axes):
    n = axis_total(axes)
    return tree_sum([value] + [hop(value, axes, s) for s in range(1, n)])


CHIPS = ("rs", "mx")
CORES = ("mc",)


def rms_forward(values, gain):
    inv_rms = lax.rsqrt(jnp.mean(values * values, axis=-1, keepdims=True) + NORM_EPS)
    unit_rows = values * inv_rms
    return unit_rows, inv_rms, (unit_rows * gain).astype(BF)


def rms_backward(grad_normed, unit_rows, inv_rms, gain):
    scaled = grad_normed * gain
    return inv_rms * (scaled - unit_rows * jnp.mean(scaled * unit_rows, axis=-1, keepdims=True))


def mm(a, b):
    return jnp.dot(a, b, preferred_element_type=F32)


def mm_nt(a, b):
    return lax.dot_general(a, b, (((1,), (1,)), ((), ())), preferred_element_type=F32)


def mm_tn(a, b):
    return lax.dot_general(a, b, (((0,), (0,)), ((), ())), preferred_element_type=F32)


def head_sums(products):
    width = products.shape[-1]
    head_in = lax.broadcasted_iota(jnp.int32, (width, width), 0) // HD
    head_out = lax.broadcasted_iota(jnp.int32, (width, width), 1) // HD
    ones = jnp.where(head_in == head_out, 1.0, 0.0).astype(BF)
    high = products.astype(BF)
    low = (products - high.astype(F32)).astype(BF)
    return mm(high, ones) + mm(low, ones)


def attend(query, key, value):
    depth = len(query)
    q32, k32, v32 = ([v.astype(F32) for v in rows] for rows in (query, key, value))
    pairs = [(p, q) for p in range(depth) for q in range(p + 1)]
    rows = query[0].shape[0]
    sums = head_sums(jnp.concatenate([q32[p] * k32[q] for p, q in pairs], 0)) * HD ** (-0.5)
    scores = {pq: sums[i * rows : (i + 1) * rows] for i, pq in enumerate(pairs)}
    probs = {}
    context = []
    for p in range(depth):
        top = scores[p, 0]
        for q in range(1, p + 1):
            top = jnp.maximum(top, scores[p, q])
        terms = [jnp.exp(scores[p, q] - top) for q in range(p + 1)]
        scale = 1.0 / sum(terms[1:], terms[0])
        acc = 0.0
        for q in range(p + 1):
            probs[p, q] = terms[q] * scale
            acc = acc + probs[p, q].astype(BF).astype(F32) * v32[q]
        context.append(acc.astype(BF))
    return context, probs


def attend_back(query, key, value, probs, grad_context):
    depth = len(query)
    q32, k32, v32, g32 = ([v.astype(F32) for v in r] for r in (query, key, value, grad_context))
    pairs = [(p, q) for p in range(depth) for q in range(p + 1)]
    rows = query[0].shape[0]
    sums = head_sums(jnp.concatenate([g32[p] * v32[q] for p, q in pairs], 0))
    grad_probs = {pq: sums[i * rows : (i + 1) * rows] for i, pq in enumerate(pairs)}
    grad_scores = {}
    for p in range(depth):
        inner = sum(probs[p, q] * grad_probs[p, q] for q in range(p + 1))
        for q in range(p + 1):
            low = (probs[p, q] * (grad_probs[p, q] - inner)).astype(BF)
            grad_scores[p, q] = low.astype(F32)
    scale = HD ** (-0.5)
    grad_query, grad_key, grad_value = [], [], []
    for p in range(depth):
        later = range(p, depth)
        grad_query.append(
            (scale * sum(grad_scores[p, q] * k32[q] for q in range(p + 1))).astype(BF)
        )
        grad_key.append((scale * sum(grad_scores[o, p] * q32[o] for o in later)).astype(BF))
        grad_value.append(
            sum(probs[o, p].astype(BF).astype(F32) * g32[o] for o in later).astype(BF)
        )
    return grad_query, grad_key, grad_value


def vmem_call(kernel, outs, *args, index=None, scratch=(), flops=0, vmem=None):
    size = sum(v.size * v.dtype.itemsize for v in args)
    size += sum(math.prod(v.shape) * v.dtype.itemsize for v in outs)
    first = () if index is None else (jnp.reshape(index, (-1,)).astype(jnp.int32),)
    array = pl.BlockSpec() if vmem else pl.BlockSpec(memory_space=pltpu.VMEM)
    return pl.pallas_call(
        kernel,
        out_shape=list(outs),
        in_specs=[pl.BlockSpec(memory_space=pltpu.SMEM)] * len(first) + [array] * len(args),
        out_specs=[array] * len(outs),
        scratch_shapes=list(scratch),
        compiler_params=pltpu.CompilerParams(
            vmem_limit_bytes=vmem << 20 if vmem else VMEM_LIMIT
        ),
        cost_estimate=pl.CostEstimate(flops=flops, bytes_accessed=size, transcendentals=0),
        name=getattr(kernel, "func", kernel).__name__,
    )(*first, *args)


def sds(shape, dtype):
    return jax.ShapeDtypeStruct(shape, dtype)


def pass_kernel(*refs):
    pass


def after(value, *others):
    anywhere = pl.BlockSpec(memory_space=pl.ANY)
    return pl.pallas_call(
        pass_kernel,
        out_shape=sds(value.shape, value.dtype),
        in_specs=[anywhere] * (1 + len(others)),
        out_specs=anywhere,
        input_output_aliases={0: 0},
        name="after",
    )(value, *others)


def swap_parts(parts, axes):
    return [parts[0]] + [hop(part, axes, t) for t, part in enumerate(parts) if t]


def stack_kernel(*refs):
    at = 0
    for ref in refs[:-1]:
        rows = ref.shape[0]
        refs[-1][at : at + rows, :] = ref[...]
        at += rows


def stack_rows(parts):
    shape = (sum(p.shape[0] for p in parts), parts[0].shape[1])
    return vmem_call(stack_kernel, [sds(shape, parts[0].dtype)], *parts)[0]


def gather_pieces(rows):
    near = [rows] + [hop(rows, CHIPS, t) for t in range(1, axis_total(CHIPS))]
    return near + [hop(stack_rows(near), CORES, 1)]


def pair_kernel(near_ref, far_ref, *out_refs):
    rows = out_refs[0].shape[0]
    for t, ref in enumerate(out_refs):
        at = slice(t * rows, (t + 1) * rows)
        ref[...] = (near_ref[at, :].astype(F32) + far_ref[at, :].astype(F32)).astype(BF)


def scatter_pieces(near, far):
    chips = axis_total(CHIPS)
    got = hop(far, CORES, 1)
    rows = near.shape[0] // chips
    pair = vmem_call(pair_kernel, [sds((rows, near.shape[1]), BF)] * chips, near, got)
    return swap_parts(pair, CHIPS)


def sum_refs(refs):
    return tree_sum([ref[...].astype(F32) for ref in refs])


def pack_rows(inputs, out_grad, depth_counts, me, mine, share):
    depth = inputs.shape[0]
    counts = lax.dynamic_slice_in_dim(depth_counts, mine * share, share, 0)
    live = (jnp.arange(depth)[:, None] < counts[None, :]).astype(BF)
    live = jnp.broadcast_to(live[:, None, :, None], (depth, 2, share, 128))
    rows = [lax.dynamic_slice_in_dim(v, mine * share, share, 1) for v in (inputs, out_grad)]
    sent = jnp.concatenate([jnp.stack(rows, 1), live], -1)
    return [take(sent, me ^ t) for t in range(depth)]


def unpack_kernel(depth, me_ref, *refs):
    got = refs[:depth]
    gain_ref, rows_ref, grad_ref, mask_ref, normed_ref, masked_ref = refs[depth:]
    share, wide = got[0].shape[1:]
    model = rows_ref.shape[1]
    for t in range(depth):
        at = pl.ds(pl.multiple_of((me_ref[0] ^ t) * share, share), share)
        rows_ref[at, :] = got[t][0, :, :model].astype(F32)
        grad_ref[at, :] = got[t][1, :, :model].astype(F32)
        mask_ref[at, :] = got[t][0, :, model:].astype(F32)
    normed_ref[...] = rms_forward(rows_ref[...], gain_ref[0:1, :])[2]
    masked_ref[...] = (mask_ref[:, :1] * grad_ref[...]).astype(BF)


def unpack_rows(got, gains, me):
    depth = len(got)
    share, wide = got[0].shape[1:]
    shape = (depth * share, wide - 128)
    return vmem_call(
        functools.partial(unpack_kernel, depth),
        [sds(shape, F32), sds(shape, F32), sds((shape[0], 128), F32), sds(shape, BF), sds(shape, BF)],
        *got,
        gains,
        index=me,
    )


def project_kernel(width, parts, *refs):
    me_ref = refs[0]
    pieces = refs[1 : 1 + parts]
    w_ref = refs[1 + parts]
    normed_ref = refs[2 + parts]
    out_refs = refs[3 + parts : -1]
    all_ref = refs[-1]
    stack_kernel(*pieces, normed_ref)
    depth, rows, _ = all_ref.shape
    weights = w_ref[:, : 3 * width]
    for c in range(depth):
        all_ref[c] = mm(normed_ref[c * rows : (c + 1) * rows, :], weights).astype(BF)
    for t, ref in enumerate(out_refs):
        ref[...] = all_ref[me_ref[0] ^ t]


def project(pieces, attn_w, width, me, depth):
    tokens = sum(p.shape[0] for p in pieces)
    rows = tokens // depth
    out = vmem_call(
        functools.partial(project_kernel, width, len(pieces)),
        [sds((tokens, attn_w.shape[0]), BF)] + [sds((rows, 3 * width), BF)] * depth,
        *pieces,
        attn_w,
        index=me,
        scratch=[pltpu.VMEM((depth, rows, 3 * width), BF)],
        flops=6 * tokens * width * attn_w.shape[0],
    )
    return out[0], out[1:]


def attend_kernel(depth, me_ref, *refs):
    got = refs[:depth]
    outs = refs[depth : 2 * depth]
    qkv, ctx = refs[2 * depth :]
    width = ctx.shape[-1]
    for t in range(depth):
        qkv[me_ref[0] ^ t] = got[t][...]
    q, k, v = ([qkv[p, :, j * width : (j + 1) * width] for p in range(depth)] for j in range(3))
    context, _ = attend(q, k, v)
    for p in range(depth):
        ctx[p] = context[p]
    for t in range(depth):
        outs[t][...] = ctx[me_ref[0] ^ t]


def attend_pieces(got, me):
    depth = len(got)
    rows, wide = got[0].shape
    return vmem_call(
        functools.partial(attend_kernel, depth),
        [sds((rows, wide // 3), BF)] * depth,
        *got,
        index=me,
        scratch=[pltpu.VMEM((depth, rows, wide), BF), pltpu.VMEM((depth, rows, wide // 3), BF)],
        flops=depth * rows * wide * 60,
    )


def attend_back_kernel(depth, me_ref, *refs):
    got = refs[:depth]
    got_context = refs[depth : 2 * depth]
    outs = refs[2 * depth : 3 * depth]
    qkv, ctx = refs[3 * depth :]
    width = ctx.shape[-1]
    for t in range(depth):
        qkv[me_ref[0] ^ t] = got[t][...]
        ctx[me_ref[0] ^ t] = got_context[t][...]
    q, k, v = ([qkv[p, :, j * width : (j + 1) * width] for p in range(depth)] for j in range(3))
    _, probs = attend(q, k, v)
    grads = attend_back(q, k, v, probs, [ctx[p] for p in range(depth)])
    for p in range(depth):
        for j in range(3):
            qkv[p, :, j * width : (j + 1) * width] = grads[j][p]
    for t in range(depth):
        outs[t][...] = qkv[me_ref[0] ^ t]


def attend_back_pieces(got, got_context, me):
    depth = len(got)
    rows, wide = got[0].shape
    return vmem_call(
        functools.partial(attend_back_kernel, depth),
        [sds((rows, wide), BF)] * depth,
        *got,
        *got_context,
        index=me,
        scratch=[pltpu.VMEM((depth, rows, wide), BF), pltpu.VMEM((depth, rows, wide // 3), BF)],
        flops=depth * rows * wide * 100,
    )


def attn_out_kernel(depth, width, me_ref, *refs):
    got = refs[:depth]
    w_ref = refs[depth]
    ctx_ref, near_ref, far_ref = refs[depth + 1 : depth + 4]
    by_chunk = refs[depth + 4]
    for t in range(depth):
        by_chunk[me_ref[0] ^ t] = got[t][...]
    rows = by_chunk.shape[1]
    half = depth // 2
    for c in range(depth):
        ctx_ref[c * rows : (c + 1) * rows, :] = by_chunk[c]
        out = near_ref if c < half else far_ref
        at = (c % half) * rows
        out[at : at + rows, :] = mm_nt(by_chunk[c], w_ref[:, 3 * width :]).astype(BF)


def attn_out_terms(got, attn_w, me):
    depth = len(got)
    rows, width = got[0].shape
    model = attn_w.shape[0]
    tokens = depth * rows
    return vmem_call(
        functools.partial(attn_out_kernel, depth, width),
        [sds((tokens, width), BF)] + [sds((tokens // 2, model), BF)] * 2,
        *got,
        attn_w,
        index=me,
        scratch=[pltpu.VMEM((depth, rows, width), BF)],
        flops=2 * tokens * width * model,
    )


def join_kernel(chips, *refs):
    terms = refs[:chips]
    rows_ref, mask_ref, gain_ref = refs[chips : chips + 3]
    hidden_ref, normed_ref = refs[chips + 3 :]
    hidden = rows_ref[...] + mask_ref[:, :1] * sum_refs(terms)
    hidden_ref[...] = hidden
    normed_ref[...] = rms_forward(hidden, gain_ref[1:2, :])[2]


def join_rows(terms, rows_in, mask, gains):
    shape = rows_in.shape
    return vmem_call(
        functools.partial(join_kernel, len(terms)),
        [sds(shape, F32), sds(shape, BF)],
        *terms,
        rows_in,
        mask,
        gains,
    )


def norm_back_kernel(chips, _, *refs):
    terms = refs[:chips]
    rows_ref, grad_ref, mask_ref, gain_ref = refs[chips : chips + 4]
    out_ref, masked_ref, gain_out_ref = refs[chips + 4 :]
    grad_normed = sum_refs(terms)
    gain = gain_ref[1:2, :]
    unit_rows, inv_rms, _ = rms_forward(rows_ref[...], gain)
    grad = grad_ref[...] + rms_backward(grad_normed, unit_rows, inv_rms, gain)
    out_ref[...] = grad
    masked_ref[...] = (mask_ref[:, :1] * grad).astype(BF)
    gain_out_ref[...] = jnp.sum(grad_normed * unit_rows, axis=0, keepdims=True)


def norm_back(terms, rows, grad_rows, mask, gains, index):
    shape = rows.shape
    return vmem_call(
        functools.partial(norm_back_kernel, len(terms)),
        [sds(shape, F32), sds(shape, BF), sds((1, shape[1]), F32)],
        *terms,
        rows,
        grad_rows,
        mask,
        gains,
        index=index,
    )


def finish_kernel(depth, chips, me_ref, *refs):
    terms, ffn_terms = refs[:chips], refs[chips : 2 * chips]
    totals, refs = refs[2 * chips : 2 * chips + 2], refs[2 * chips + 2 :]
    rows_ref, grad_ref, hidden_ref, mask_ref, gain_ref = refs[:5]
    outs, (output, input_grad) = refs[5:-2], refs[-2:]
    gain = gain_ref[0:1, :]
    unit_rows, inv_rms, _ = rms_forward(rows_ref[...], gain)
    grad = rms_backward(sum_refs(terms), unit_rows, inv_rms, gain)
    output[...] = (hidden_ref[...] + mask_ref[:, :1] * sum_refs(ffn_terms)).astype(BF)
    input_grad[...] = (grad_ref[...] + grad).astype(BF)
    total = totals[0][...] + totals[1][...]
    high = total.astype(BF)
    low = (total - high.astype(F32)).astype(BF)
    share, model = outs[0].shape[1:]
    count = total.shape[0]
    for t, ref in enumerate(outs):
        at = pl.ds(pl.multiple_of((me_ref[0] ^ t) * share, share), share)
        ref[0] = output[at, :]
        ref[1] = input_grad[at, :]
        ref[2] = jnp.zeros((share, model), BF)
        ref[2, :count, :] = high
        ref[2, 8 : 8 + count, :] = low


def finish_rows(terms, ffn_terms, totals, rows, grad_rows, hidden, mask, gains, me, depth):
    tokens, model = rows.shape
    return vmem_call(
        functools.partial(finish_kernel, depth, len(terms)),
        [sds((3, tokens // depth, model), BF)] * depth,
        *terms,
        *ffn_terms,
        *totals,
        rows,
        grad_rows,
        hidden,
        mask,
        gains,
        index=me,
        scratch=[pltpu.VMEM((tokens, model), BF)] * 2,
        vmem=56,
    )


def by_position_kernel(depth, me_ref, *refs):
    rows_ref, total_ref = refs[depth:]
    count = total_ref.shape[0]
    parts = []
    for t in range(depth):
        rows_ref[me_ref[0] ^ t] = refs[t][:2]
        high, low = refs[t][2, :count, :], refs[t][2, 8 : 8 + count, :]
        parts.append(high.astype(F32) + low.astype(F32))
    total_ref[...] = tree_sum(parts)


def by_position(got, me, count):
    depth = len(got)
    _, share, model = got[0].shape
    return vmem_call(
        functools.partial(by_position_kernel, depth),
        [sds((depth, 2, share, model), BF), sds((count, model), F32)],
        *got,
        index=me,
    )


def whole_frames_kernel(parts, me_ref, *refs):
    share = refs[0].shape[2]
    for t in range(parts):
        at = pl.ds(pl.multiple_of((me_ref[0] ^ t) * share, share), share)
        for p in range(refs[0].shape[0]):
            for j in range(2):
                refs[parts + j][p, at, :] = refs[t][p, j]


def whole_frames(got, me):
    depth, _, share, model = got[0].shape
    return vmem_call(
        functools.partial(whole_frames_kernel, len(got)),
        [sds((depth, len(got) * share, model), BF)] * 2,
        *got,
        index=me,
    )


def ffn_tile(x, g, w_ref, hidden):
    gate_up = mm(x, w_ref[:, : 2 * hidden])
    gate_pre = gate_up[:, :hidden]
    up_proj = gate_up[:, hidden:]
    sig = jax.nn.sigmoid(gate_pre)
    acts = (gate_pre * sig * up_proj).astype(BF)
    grad_act = mm(g, w_ref[:, 2 * hidden :])
    grad_gate = (grad_act * up_proj * sig * (1.0 + gate_pre * (1.0 - sig))).astype(BF)
    grad_up = (grad_act * gate_pre * sig).astype(BF)
    return acts, grad_gate, grad_up


def ffn_kernel(x_ref, g_ref, w_ref, acts_ref, grads_ref, near_ref, far_ref):
    hidden = w_ref.shape[1] // 3
    half = near_ref.shape[0]
    for j, out_ref in enumerate((near_ref, far_ref)):
        at = slice(j * half, (j + 1) * half)
        acts, grad_gate, grad_up = ffn_tile(x_ref[at, :], g_ref[at, :], w_ref, hidden)
        acts_ref[at, :] = acts
        grads_ref[at, :hidden] = grad_gate
        grads_ref[at, hidden:] = grad_up
        out_ref[...] = mm_nt(grads_ref[at, :], w_ref[:, : 2 * hidden]).astype(BF)


def ffn_block(normed, grad_ffn, ffn_w):
    tokens, model = normed.shape
    hidden = ffn_w.shape[1] // 3
    return vmem_call(
        ffn_kernel,
        [sds((tokens, hidden), BF), sds((tokens, 2 * hidden), BF)]
        + [sds((tokens // 2, model), BF)] * 2,
        normed,
        grad_ffn,
        ffn_w,
        flops=10 * tokens * hidden * model,
    )


def weight_grad_kernel(count, *refs):
    out_ref, square_ref = refs[2 * count :]
    total = jnp.zeros((1, 128), F32)
    lane = 0
    for i in range(count):
        left, right = refs[2 * i], refs[2 * i + 1]
        width = right.shape[1]
        grads = mm_tn(left[...], right[...])
        out_ref[:, lane : lane + width] = grads.astype(BF)
        squares = jnp.sum(grads * grads, axis=0, keepdims=True)
        for j in range(0, width, 128):
            total = total + squares[:, j : j + 128]
        lane += width

    @pl.when(pl.program_id(0) == 0)
    def _():
        square_ref[...] = total

    @pl.when(pl.program_id(0) > 0)
    def _():
        square_ref[...] += total


def weight_grads(*pairs):
    owners = axis_total(OWNERS)
    tokens, model = pairs[0][0].shape
    widths = [last - first for _, _, first, last in pairs]
    width = sum(widths)
    if lax.axis_size("rf") > 1 or any(w % 128 for w in widths):
        grads = [mm_tn(left, right[:, first:last]) for left, right, first, last in pairs]
        grads = jnp.concatenate(grads, 1)
        if lax.axis_size("rf") > 1:
            grads = grads.reshape(lax.axis_size("pz"), lax.axis_size("rf"), -1, width)
            grads = lax.psum_scatter(grads, "rf", scatter_dimension=1)
        squares = jnp.sum((grads * grads).reshape(-1, 128), axis=0, keepdims=True)
        return grads.astype(BF).reshape(owners, -1, width), squares
    step = 512
    in_specs = []
    for (_, _, first, _), w in zip(pairs, widths):
        in_specs.append(pl.BlockSpec((tokens, step), lambda i: (0, i)))
        in_specs.append(pl.BlockSpec((tokens, w), lambda i, at=first // w: (0, at)))
    out, squares = pl.pallas_call(
        functools.partial(weight_grad_kernel, len(pairs)),
        out_shape=[sds((model, width), BF), sds((1, 128), F32)],
        grid=(model // step,),
        in_specs=in_specs,
        out_specs=[
            pl.BlockSpec((step, width), lambda i: (i, 0)),
            pl.BlockSpec((1, 128), lambda i: (0, 0)),
        ],
        compiler_params=pltpu.CompilerParams(vmem_limit_bytes=VMEM_LIMIT),
        cost_estimate=pl.CostEstimate(
            flops=2 * tokens * model * width,
            bytes_accessed=2 * (tokens * (2 * model + width) + model * width),
            transcendentals=0,
        ),
        name="weight_grads",
    )(*[v for left, right, _, _ in pairs for v in (left, right)])
    return out.reshape(owners, -1, width), squares


def context_kernel(depth, width, *refs):
    me_ref = refs[0]
    parts = len(refs) - 4 - depth
    pieces = refs[1 : 1 + parts]
    w_ref = refs[1 + parts]
    rows_ref = refs[2 + parts]
    outs = refs[3 + parts : 3 + parts + depth]
    by_chunk = refs[-1]
    stack_kernel(*pieces, rows_ref)
    rows = by_chunk.shape[1]
    for c in range(depth):
        by_chunk[c] = mm(rows_ref[c * rows : (c + 1) * rows, :], w_ref[:, 3 * width :]).astype(BF)
    for t in range(depth):
        outs[t][...] = by_chunk[me_ref[0] ^ t]


def context_grads(pieces, attn_w, width, me, depth):
    tokens = sum(p.shape[0] for p in pieces)
    rows = tokens // depth
    out = vmem_call(
        functools.partial(context_kernel, depth, width),
        [sds((tokens, attn_w.shape[0]), BF)] + [sds((rows, width), BF)] * depth,
        *pieces,
        attn_w,
        index=me,
        scratch=[pltpu.VMEM((depth, rows, width), BF)],
        flops=2 * tokens * width * attn_w.shape[0],
    )
    return out[0], out[1:]


def qkv_back_kernel(depth, width, me_ref, *refs):
    got = refs[:depth]
    w_ref, normed_ref, gain_ref, rows_ref, near_ref, far_ref, gain_out_ref, by_chunk = refs[depth:]
    for t in range(depth):
        by_chunk[me_ref[0] ^ t] = got[t][...]
    rows = by_chunk.shape[1]
    half = depth // 2
    total = jnp.zeros(gain_out_ref.shape, F32)
    for c in range(depth):
        here = slice(c * rows, (c + 1) * rows)
        rows_ref[here, :] = by_chunk[c]
        out = near_ref if c < half else far_ref
        at = (c % half) * rows
        terms = mm_nt(by_chunk[c], w_ref[:, : 3 * width])
        out[at : at + rows, :] = terms.astype(BF)
        total = total + jnp.sum(terms * normed_ref[here, :].astype(F32), axis=0, keepdims=True)
    gain_out_ref[...] = total / gain_ref[0:1, :]


def qkv_back(got, attn_w, normed, gains, width, me):
    depth = len(got)
    rows = got[0].shape[0]
    tokens = depth * rows
    model = attn_w.shape[0]
    return vmem_call(
        functools.partial(qkv_back_kernel, depth, width),
        [sds((tokens, 3 * width), BF)]
        + [sds((tokens // 2, model), BF)] * 2
        + [sds((1, model), F32)],
        *got,
        attn_w,
        normed,
        gains,
        index=me,
        scratch=[pltpu.VMEM((depth, rows, 3 * width), BF)],
        flops=6 * tokens * width * model,
    )


def attn_grads_kernel(depth, width, me_ref, *refs):
    got = refs[:depth]
    w_ref, normed_ref, gain_ref, gain2_ref, square_ref = refs[depth : depth + 5]
    near_ref, far_ref, chunk_ref, total_ref, by_chunk, grads = refs[depth + 5 :]
    for t in range(depth):
        by_chunk[me_ref[0] ^ t] = got[t][...]
    rows = by_chunk.shape[1]
    half = depth // 2
    total = jnp.zeros(gain2_ref.shape, F32)
    for c in range(depth):
        here = slice(c * rows, (c + 1) * rows)
        grads[here, :] = by_chunk[c]
        out = near_ref if c < half else far_ref
        at = (c % half) * rows
        terms = mm_nt(by_chunk[c], w_ref[:, : 3 * width])
        out[at : at + rows, :] = terms.astype(BF)
        total = total + jnp.sum(terms * normed_ref[here, :].astype(F32), axis=0, keepdims=True)
    total_ref[0:1, :] = total / gain_ref[0:1, :]
    total_ref[1:2, :] = gain2_ref[...]
    chunk = mm_tn(normed_ref[...], grads[...])
    chunk_ref[...] = chunk.astype(BF)
    column = jnp.sum(chunk * chunk, axis=0, keepdims=True)
    squares = square_ref[...]
    for j in range(0, 3 * width, 128):
        squares = squares + column[:, j : j + 128]
    total_ref[2:3, :] = jnp.zeros(gain2_ref.shape, F32)
    total_ref[2:3, :128] = squares


def attn_grads(got, attn_w, normed, gains, gain_part2, squares, me):
    depth = len(got)
    rows, wide = got[0].shape
    width = wide // 3
    tokens = depth * rows
    model = attn_w.shape[0]
    if lax.axis_size("rf") > 1 or width % 128:
        grads, near, far, gain_part1 = qkv_back(got, attn_w, normed, gains, width, me)
        chunks, more = weight_grads((normed, grads, 0, wide))
        squares = jnp.pad(squares + more, ((0, 0), (0, model - 128)))
        return near, far, chunks, jnp.concatenate([gain_part1, gain_part2, squares], 0)
    near, far, chunks, total = vmem_call(
        functools.partial(attn_grads_kernel, depth, width),
        [sds((tokens // 2, model), BF)] * 2 + [sds((model, wide), BF), sds((3, model), F32)],
        *got,
        attn_w,
        normed,
        gains,
        gain_part2,
        squares,
        index=me,
        scratch=[pltpu.VMEM((depth, rows, wide), BF), pltpu.VMEM((tokens, wide), BF)],
        flops=12 * tokens * width * model,
        vmem=56,
    )
    return near, far, chunks.reshape(axis_total(OWNERS), -1, wide), total


OWNERS = ("pz", "rs")


def lanes_view(array):
    rows, kinds, depth, cols = array.shape
    split = array.reshape(rows, kinds, depth, cols // 128, 128)
    return split.transpose(0, 1, 3, 2, 4).reshape(-1, 128)


def lanes_back(view, shape):
    rows, kinds, depth, cols = shape
    split = view.reshape(rows, kinds, cols // 128, depth, 128)
    return split.transpose(0, 1, 3, 2, 4).reshape(shape)


def tiles_of(dims, pieces):
    kinds, tiles, depth, parts = dims
    per = tiles // parts
    for number, piece in enumerate(pieces):
        lane = 0
        for k, first, count in piece:
            if k is None:
                lane += 128 * count
                continue
            for t in range(first, first + count):
                for part in range(parts):
                    for p in range(depth):
                        at = (k * tiles + part * per + t) * depth + p
                        yield at, p * parts + part, number, lane
                lane += 128


def widths_of(pieces):
    return [128 * sum(count for _, _, count in piece) for piece in pieces]


def whole_message(kinds, cols):
    return [[(k, 0, cols // 128) for k in range(kinds)]]


def split_kernel(dims, pieces, w_ref, *out_refs):
    kinds, tiles, depth, _ = dims
    rows = out_refs[0].shape[1]
    for at, chunk, number, lane in tiles_of(dims, pieces):
        values = w_ref[pl.ds(at, rows, stride=kinds * tiles * depth), :]
        out_refs[number][chunk, :, lane : lane + 128] = values.astype(BF)


def in_blocks(kernel, grid, in_specs, out_shape, out_specs, args, vmem, scalars=(), scratch=(), **more):
    n_in, n_out, n_scalar = len(in_specs), len(out_specs), len(scalars)

    def run(*refs):
        fixed = refs[:n_scalar]
        arrays = refs[n_scalar : n_scalar + n_in + n_out]
        held = refs[n_scalar + n_in + n_out :]
        pltpu.emit_pipeline(
            lambda *blocks: kernel(*fixed, *blocks, *held),
            grid=grid,
            in_specs=in_specs,
            out_specs=out_specs,
        )(*arrays)

    return pl.pallas_call(
        run,
        out_shape=out_shape,
        in_specs=[pl.BlockSpec(memory_space=pltpu.SMEM)] * n_scalar
        + [pl.BlockSpec(memory_space=pltpu.HBM)] * n_in,
        out_specs=[pl.BlockSpec(memory_space=pltpu.HBM)] * n_out,
        scratch_shapes=list(scratch),
        compiler_params=pltpu.CompilerParams(vmem_limit_bytes=vmem << 20),
        **more,
    )(*scalars, *args)


def split_weights(weights, vmem, pieces=None):
    rows, kinds, depth, cols = weights.shape
    parts = lax.axis_size("rs")
    if (cols // parts) % 128 or rows % 16:
        low = weights.astype(BF).reshape(rows, kinds, depth, parts, cols // parts)
        return [low.transpose(2, 3, 0, 1, 4).reshape(depth * parts, rows, -1)]
    pieces = pieces or whole_message(kinds, cols // parts)
    tiles = cols // 128
    step = math.gcd(rows, 32)
    chunks = depth * parts
    return in_blocks(
        functools.partial(split_kernel, (kinds, tiles, depth, parts), pieces),
        (rows // step,),
        [pl.BlockSpec((step * kinds * tiles * depth, 128), lambda i: (i, 0))],
        [sds((chunks, rows, w), BF) for w in widths_of(pieces)],
        [pl.BlockSpec((chunks, step, w), lambda i: (0, i, 0)) for w in widths_of(pieces)],
        [lanes_view(weights)],
        vmem=vmem,
        cost_estimate=pl.CostEstimate(
            flops=weights.size, bytes_accessed=6 * weights.size, transcendentals=0
        ),
        name="split_weights",
    )


def to_planes(low):
    full = lax.all_to_all(low, OWNERS, 0, 0, tiled=True)
    if lax.axis_size("rf") > 1:
        full = full.reshape((lax.axis_size("pz"), lax.axis_size("rs")) + full.shape[1:])
        full = lax.all_gather(full, "rf", axis=1)
    return full.reshape(-1, full.shape[-1])


def to_owners(chunks):
    return lax.all_to_all(chunks, OWNERS, 0, 0, tiled=True)


def adamw_update(weights, first, second, grads, clip_factor, decay_rate, step_rate):
    clipped = clip_factor * grads
    first_new = BETA_ONE * first + (1.0 - BETA_ONE) * clipped
    second_new = BETA_TWO * second + (1.0 - BETA_TWO) * clipped * clipped
    first_hat = first_new * (1.0 / (1.0 - BETA_ONE**STEP))
    second_hat = second_new * (1.0 / (1.0 - BETA_TWO**STEP))
    new_weights = weights - step_rate * (
        first_hat / (jnp.sqrt(second_hat) + ADAM_EPS) + decay_rate * weights
    )
    return (new_weights, first_new, second_new)


def norm_of(total):
    sums = jnp.sum(total[:2] * total[:2], axis=0, keepdims=True) + total[2:3]
    return jnp.sqrt(jnp.sum(sums, axis=1, keepdims=True))


def adamw_kernel(dims, pieces, steps, stages, total_from, *refs):
    kinds, tiles, depth, _ = dims
    n = len(pieces)
    g_refs, state, refs = refs[:n], refs[n : n + 3], refs[n + 3 :]
    stage_refs, new_refs, staged_refs = refs[:stages], refs[stages : stages + 3], refs[stages + 3 :]
    staged_refs, refs = staged_refs[:stages], staged_refs[stages:]
    g_held, refs = refs[:n], refs[n:]
    here = len(refs) == 7
    state_held, refs = (state, refs) if here else (refs[:3], refs[3:])
    new_held, grads, total_ref, in_sems, out_sems = refs[:3], *refs[3:]
    rows, units, _ = grads.shape
    count = rows * units
    places = {at: (number, chunk, lane) for at, chunk, number, lane in tiles_of(dims, pieces)}

    def fetches(i):
        some = pl.ds(pl.multiple_of(i * rows, rows), rows)
        pairs = [(g.at[:, some, :], held.at[:, some, :]) for g, held in zip(g_refs, g_held)]
        if not here:
            some = pl.ds(pl.multiple_of(i * count, count), count)
            pairs += [(v.at[some, :], held.at[some, :]) for v, held in zip(state, state_held)]
        return [pltpu.make_async_copy(*pair, in_sems.at[i, j]) for j, pair in enumerate(pairs)]

    def stores(i):
        some = pl.ds(pl.multiple_of(i * count, count), count)
        pairs = [(held.at[some, :], new.at[some, :]) for held, new in zip(new_held, new_refs)]
        return [pltpu.make_async_copy(*pair, out_sems.at[i, j]) for j, pair in enumerate(pairs)]

    staging = [
        pltpu.make_async_copy(source, to, out_sems.at[steps, j])
        for j, (source, to) in enumerate(zip(stage_refs, staged_refs))
    ]

    summed = pltpu.make_async_copy(total_from, total_ref, out_sems.at[steps, stages])
    summed.start()

    @pl.loop(0, steps)
    def _(i):
        for copy in fetches(i):
            copy.start()

    for copy in staging:
        copy.start()
    summed.wait()
    clip = CLIP_NORM / jnp.maximum(norm_of(total_ref[...]), CLIP_NORM)

    @pl.loop(0, steps)
    def _(i):
        for copy in fetches(i):
            copy.wait()
        some = pl.ds(pl.multiple_of(i * rows, rows), rows)
        for first in range(0, units, 8):
            tile = [
                g_held[number][chunk, some, lane : lane + 128].astype(F32)
                for number, chunk, lane in (places[at] for at in range(first, first + 8))
            ]
            grads[:, first : first + 8, :] = jnp.swapaxes(jnp.stack(tile), 0, 1)

        @pl.loop(0, rows)
        def _(row):
            at = pl.ds(pl.multiple_of(i * count + row * units, units), units)
            new = adamw_update(
                *(held[at, :] for held in state_held), grads[row], clip, WEIGHT_DECAY, LEARN_RATE
            )
            for held, values in zip(new_held, new):
                held[at, :] = values

        for copy in stores(i):
            copy.start()

    @pl.loop(0, steps)
    def _(i):
        for copy in stores(i):
            copy.wait()

    for copy in staging:
        copy.wait()


def adamw_owned(state, chunks, total, shape, pieces=None, stage=(), here=False):
    rows, kinds, depth, cols = shape
    parts = lax.axis_size("rs")
    pieces = pieces or whole_message(kinds, cols // parts)
    units = kinds * cols // 128 * depth
    step = math.gcd(rows, 16)
    steps = rows // step
    anywhere = pl.BlockSpec(memory_space=pl.ANY)
    inside = pl.BlockSpec(memory_space=pltpu.VMEM)
    view = state[0].shape
    out = pl.pallas_call(
        functools.partial(
            adamw_kernel, (kinds, cols // 128, depth, parts), pieces, steps, len(stage)
        ),
        out_shape=[sds(view, F32)] * 3 + [sds(v.shape, F32) for v in stage],
        in_specs=[anywhere] * (1 + len(chunks))
        + [inside if here else anywhere] * 3
        + [anywhere] * len(stage),
        out_specs=[anywhere] * 3 + [inside] * len(stage),
        scratch_shapes=[pltpu.VMEM(v.shape, BF) for v in chunks]
        + [pltpu.VMEM(view, F32)] * (3 if here else 6)
        + [pltpu.VMEM((step, units, 128), F32), pltpu.VMEM(total.shape, F32)]
        + [pltpu.SemaphoreType.DMA((steps, len(chunks) + 3))]
        + [pltpu.SemaphoreType.DMA((steps + 1, 4))],
        compiler_params=pltpu.CompilerParams(vmem_limit_bytes=(20 if here else 52) << 20),
        cost_estimate=pl.CostEstimate(
            flops=20 * math.prod(shape), bytes_accessed=26 * math.prod(shape), transcendentals=0
        ),
        name="adamw",
    )(total, *chunks, *state, *stage)
    return out[:3], out[3:]


def gains_kernel(total_ref, w_ref, m_ref, v_ref, norm_ref, *new_refs):
    norm = norm_of(total_ref[...])
    norm_ref[...] = norm
    clip = CLIP_NORM / jnp.maximum(norm, CLIP_NORM)
    new = adamw_update(
        w_ref[...], m_ref[...], v_ref[...], total_ref[0:2, :], clip, 0.0, GAIN_RATE
    )
    for ref, values in zip(new_refs, new):
        ref[...] = values


def update_gains(total, state):
    return vmem_call(
        gains_kernel, [sds((1, 1), F32)] + [sds(v.shape, F32) for v in state], total, *state
    )


def body(
    inputs,
    depth_counts,
    out_grad,
    attn_weight,
    attn_first,
    attn_second,
    ffn_weight,
    ffn_first,
    ffn_second,
    norm_gains,
    gain_first,
    gain_second,
):
    depth, frames, model = inputs.shape
    mp_axes = ("mx", "mc")
    share = frames // axis_total(mp_axes)

    me = lax.axis_index("pz")
    positions = ("pz",)
    per = ffn_weight.shape[3] // lax.axis_size("rs") // 128
    packed = pack_rows(inputs, out_grad, depth_counts, me, linear_index(mp_axes), share)
    packed = swap_parts(packed, positions)
    attn_low = split_weights(attn_weight, 48)[0]
    rows_in, rows_grad, mask, normed1_rows, masked = unpack_rows(packed, norm_gains, me)
    attn_w = to_planes(after(attn_low, mask))
    ffn_low = split_weights(ffn_weight, 48)[0]
    width = attn_w.shape[1] // 4
    normed1_pieces = gather_pieces(normed1_rows)
    grad_ffn = stack_rows(gather_pieces(masked))

    normed1, qkv = project(normed1_pieces, attn_w, width, me, depth)
    qkv = swap_parts(qkv, positions)
    context = swap_parts(attend_pieces(qkv, after(me.reshape(1), ffn_low)), positions)
    ffn_w = to_planes(after(ffn_low, *context[1:]))
    context, near, far = attn_out_terms(context, attn_w, me)
    hidden_in, normed2_rows = join_rows(scatter_pieces(near, far), rows_in, mask, norm_gains)
    normed2 = stack_rows(gather_pieces(normed2_rows))

    acts, gate_up_grads, near, far = ffn_block(normed2, grad_ffn, ffn_w)
    terms = scatter_pieces(near, far)
    hidden = acts.shape[1]
    pieces = [[(0, 0, per), (1, 0, per)], [(2, 0, per), (None, 0, width // 128)]]
    chunks_a, squares_a = weight_grads((normed2, gate_up_grads, 0, 2 * hidden))
    owned_a = to_owners(chunks_a)
    ffn_terms = mm_nt(acts, ffn_w[:, 2 * hidden :]).astype(BF)

    grad_hidden, masked, gain_part2 = norm_back(
        terms, hidden_in, rows_grad, mask, norm_gains, after(me.reshape(1), ffn_terms)
    )
    grad_attn, grad_context = context_grads(gather_pieces(masked), attn_w, width, me, depth)
    grad_context = swap_parts(grad_context, positions)
    grad_qkv = swap_parts(attend_back_pieces(qkv, grad_context, me), positions)
    half = ffn_terms.shape[0] // 2
    ffn_terms = scatter_pieces(ffn_terms[:half], ffn_terms[half:])
    chunks_b, squares_b = weight_grads((grad_ffn, acts, 0, hidden), (grad_attn, context, 0, width))
    owned_b = to_owners(after(chunks_b, *grad_qkv[1:], *ffn_terms[1:]))
    near, far, attn_chunks, total = attn_grads(
        grad_qkv,
        attn_w,
        normed1,
        norm_gains,
        gain_part2,
        squares_a + squares_b,
        after(me.reshape(1), owned_a),
    )
    terms = scatter_pieces(near, far)

    if lax.axis_size("rf") > 1:
        total = lax.psum(total, "rf")
    total = all_sum(total, mp_axes)
    totals = [total] + [hop(total, ("rs",), t) for t in range(1, lax.axis_size("rs"))]
    if len(totals) != 2:
        totals = [tree_sum(totals), jnp.zeros_like(total)]
    back = finish_rows(
        terms, ffn_terms, totals, rows_in, grad_hidden, hidden_in, mask, norm_gains, me, depth
    )

    back, total = by_position(swap_parts(back, positions), me, total.shape[0])
    attn_owned = to_owners(after(attn_chunks, total))
    back = swap_parts([back] * axis_total(mp_axes), mp_axes)
    output, input_grad = whole_frames(back, linear_index(mp_axes))

    ffn_state = [lanes_view(v) for v in (ffn_weight, ffn_first, ffn_second)]
    attn_state = [lanes_view(v) for v in (attn_weight, attn_first, attn_second)]
    ffn_new, _ = adamw_owned(ffn_state, [owned_a, owned_b], total, ffn_weight.shape, pieces)
    grad_norm, *gain_new = update_gains(total, [norm_gains, gain_first, gain_second])
    if width % 128:
        grads = jnp.concatenate([attn_owned, owned_b[:, :, hidden:]], -1)
        grads = grads.reshape(depth, lax.axis_size("rs"), -1, 4, width)
        grads = grads.transpose(2, 3, 0, 1, 4).reshape(attn_weight.shape).astype(F32)
        clip_factor = CLIP_NORM / jnp.maximum(grad_norm[0, 0], CLIP_NORM)
        attn_new = adamw_update(
            attn_weight, attn_first, attn_second, grads, clip_factor, WEIGHT_DECAY, LEARN_RATE
        )
    else:
        tiles = width // 128
        attn_pieces = [[(k, 0, tiles) for k in range(3)], [(None, 0, per), (3, 0, tiles)]]
        attn_new, _ = adamw_owned(
            attn_state,
            [attn_owned, owned_b],
            after(total, ffn_new[0], output),
            attn_weight.shape,
            attn_pieces,
        )
        attn_new = tuple(lanes_back(v, attn_weight.shape) for v in attn_new)
    ffn_new = tuple(lanes_back(v, ffn_weight.shape) for v in ffn_new)

    return (output, input_grad, grad_norm[0, 0]) + attn_new + ffn_new + tuple(gain_new)


def solution(mesh):
    dp = mesh.shape["dp"]
    mp = mesh.shape["mp"]

    def run(*args):
        depth, _, model = args[0].shape
        heads = args[3].shape[3] // mp // HD
        parts = math.gcd(dp // depth, heads)
        fine = Mesh(
            mesh.devices.reshape(depth, dp // depth // parts, parts, mp // 2, 2),
            ("pz", "rf", "rs", "mx", "mc"),
        )
        rows = ("pz", "rf", "rs")
        cols = ("mx", "mc")
        acts = P(None, rows, None)
        weight = P(rows, None, None, cols)
        return jax.shard_map(
            body,
            mesh=fine,
            in_specs=(acts, P(rows), acts) + (weight,) * 6 + (P(),) * 3,
            out_specs=(acts, acts, P()) + (weight,) * 6 + (P(),) * 3,
            check_vma=False,
        )(*args)

    return run
```

```python
import functools
import math

import jax
import jax.numpy as jnp
from jax import lax
from jax.experimental import pallas as pl
from jax.experimental.pallas import tpu as pltpu
from jax.sharding import Mesh, PartitionSpec as P

HD = 64
STEP = 5
NORM_EPS = 1e-05
BETA_ONE = 0.5
BETA_TWO = 0.5
LEARN_RATE = 0.02
GAIN_RATE = 0.4
WEIGHT_DECAY = 0.1
ADAM_EPS = 1e-08
CLIP_NORM = 1.0

VMEM_LIMIT = 28 << 20

BF = jnp.bfloat16
F32 = jnp.float32


def axis_total(axes):
    return math.prod(lax.axis_size(a) for a in axes)


def linear_index(axes):
    index = 0
    for a in axes:
        index = index * lax.axis_size(a) + lax.axis_index(a)
    return index


def hop(value, axes, step):
    n = axis_total(axes)
    return lax.ppermute(value, axes, [(i, i ^ step) for i in range(n)])


def take(stack, index):
    return lax.dynamic_index_in_dim(stack, index, 0, keepdims=False)


def put(stack, value, index):
    return lax.dynamic_update_index_in_dim(stack, value, index, 0)


def gather_parts(parts, me):
    full = jnp.zeros((len(parts),) + parts[0].shape, parts[0].dtype)
    for s, part in enumerate(parts):
        full = put(full, part, me ^ s)
    return full


def all_to_all(stack, axes):
    n = axis_total(axes)
    me = linear_index(axes)
    parts = [take(stack, me)]
    for s in range(1, n):
        parts.append(hop(take(stack, me ^ s), axes, s))
    return gather_parts(parts, me)


def all_gather(value, axes):
    n = axis_total(axes)
    me = linear_index(axes)
    return gather_parts([value] + [hop(value, axes, s) for s in range(1, n)], me)


def tree_sum(parts):
    while len(parts) > 1:
        parts = [a + b for a, b in zip(parts[::2], parts[1::2])]
    return parts[0]


def all_sum(value, axes):
    n = axis_total(axes)
    return tree_sum([value] + [hop(value, axes, s) for s in range(1, n)])


CHIPS = ("rs", "mx")
CORES = ("mc",)


def rms_forward(values, gain):
    inv_rms = lax.rsqrt(jnp.mean(values * values, axis=-1, keepdims=True) + NORM_EPS)
    unit_rows = values * inv_rms
    return unit_rows, inv_rms, (unit_rows * gain).astype(BF)


def rms_backward(grad_normed, unit_rows, inv_rms, gain):
    scaled = grad_normed * gain
    return inv_rms * (scaled - unit_rows * jnp.mean(scaled * unit_rows, axis=-1, keepdims=True))


def mm(a, b):
    return jnp.dot(a, b, preferred_element_type=F32)


def mm_nt(a, b):
    return lax.dot_general(a, b, (((1,), (1,)), ((), ())), preferred_element_type=F32)


def mm_tn(a, b):
    return lax.dot_general(a, b, (((0,), (0,)), ((), ())), preferred_element_type=F32)


def head_sums(products):
    width = products.shape[-1]
    head_in = lax.broadcasted_iota(jnp.int32, (width, width), 0) // HD
    head_out = lax.broadcasted_iota(jnp.int32, (width, width), 1) // HD
    ones = jnp.where(head_in == head_out, 1.0, 0.0).astype(BF)
    high = products.astype(BF)
    low = (products - high.astype(F32)).astype(BF)
    return mm(high, ones) + mm(low, ones)


def attend(query, key, value):
    depth = len(query)
    q32, k32, v32 = ([v.astype(F32) for v in rows] for rows in (query, key, value))
    pairs = [(p, q) for p in range(depth) for q in range(p + 1)]
    rows = query[0].shape[0]
    sums = head_sums(jnp.concatenate([q32[p] * k32[q] for p, q in pairs], 0)) * HD ** (-0.5)
    scores = {pq: sums[i * rows : (i + 1) * rows] for i, pq in enumerate(pairs)}
    probs = {}
    context = []
    for p in range(depth):
        top = scores[p, 0]
        for q in range(1, p + 1):
            top = jnp.maximum(top, scores[p, q])
        terms = [jnp.exp(scores[p, q] - top) for q in range(p + 1)]
        scale = 1.0 / sum(terms[1:], terms[0])
        acc = 0.0
        for q in range(p + 1):
            probs[p, q] = terms[q] * scale
            acc = acc + probs[p, q].astype(BF).astype(F32) * v32[q]
        context.append(acc.astype(BF))
    return context, probs


def attend_back(query, key, value, probs, grad_context):
    depth = len(query)
    q32, k32, v32, g32 = ([v.astype(F32) for v in r] for r in (query, key, value, grad_context))
    pairs = [(p, q) for p in range(depth) for q in range(p + 1)]
    rows = query[0].shape[0]
    sums = head_sums(jnp.concatenate([g32[p] * v32[q] for p, q in pairs], 0))
    grad_probs = {pq: sums[i * rows : (i + 1) * rows] for i, pq in enumerate(pairs)}
    grad_scores = {}
    for p in range(depth):
        inner = sum(probs[p, q] * grad_probs[p, q] for q in range(p + 1))
        for q in range(p + 1):
            low = (probs[p, q] * (grad_probs[p, q] - inner)).astype(BF)
            grad_scores[p, q] = low.astype(F32)
    scale = HD ** (-0.5)
    grad_query, grad_key, grad_value = [], [], []
    for p in range(depth):
        later = range(p, depth)
        grad_query.append(
            (scale * sum(grad_scores[p, q] * k32[q] for q in range(p + 1))).astype(BF)
        )
        grad_key.append((scale * sum(grad_scores[o, p] * q32[o] for o in later)).astype(BF))
        grad_value.append(
            sum(probs[o, p].astype(BF).astype(F32) * g32[o] for o in later).astype(BF)
        )
    return grad_query, grad_key, grad_value


def vmem_call(kernel, outs, *args, index=None, scratch=(), flops=0, vmem=None):
    size = sum(v.size * v.dtype.itemsize for v in args)
    size += sum(math.prod(v.shape) * v.dtype.itemsize for v in outs)
    first = () if index is None else (jnp.reshape(index, (-1,)).astype(jnp.int32),)
    array = pl.BlockSpec() if vmem else pl.BlockSpec(memory_space=pltpu.VMEM)
    return pl.pallas_call(
        kernel,
        out_shape=list(outs),
        in_specs=[pl.BlockSpec(memory_space=pltpu.SMEM)] * len(first) + [array] * len(args),
        out_specs=[array] * len(outs),
        scratch_shapes=list(scratch),
        compiler_params=pltpu.CompilerParams(
            vmem_limit_bytes=vmem << 20 if vmem else VMEM_LIMIT
        ),
        cost_estimate=pl.CostEstimate(flops=flops, bytes_accessed=size, transcendentals=0),
        name=getattr(kernel, "func", kernel).__name__,
    )(*first, *args)


def sds(shape, dtype):
    return jax.ShapeDtypeStruct(shape, dtype)


def pass_kernel(*refs):
    pass


def after(value, *others):
    anywhere = pl.BlockSpec(memory_space=pl.ANY)
    return pl.pallas_call(
        pass_kernel,
        out_shape=sds(value.shape, value.dtype),
        in_specs=[anywhere] * (1 + len(others)),
        out_specs=anywhere,
        input_output_aliases={0: 0},
        name="after",
    )(value, *others)


def swap_parts(parts, axes):
    return [parts[0]] + [hop(part, axes, t) for t, part in enumerate(parts) if t]


def stack_kernel(*refs):
    at = 0
    for ref in refs[:-1]:
        rows = ref.shape[0]
        refs[-1][at : at + rows, :] = ref[...]
        at += rows


def stack_rows(parts):
    shape = (sum(p.shape[0] for p in parts), parts[0].shape[1])
    return vmem_call(stack_kernel, [sds(shape, parts[0].dtype)], *parts)[0]


def gather_pieces(rows):
    near = [rows] + [hop(rows, CHIPS, t) for t in range(1, axis_total(CHIPS))]
    return near + [hop(stack_rows(near), CORES, 1)]


def pair_kernel(near_ref, far_ref, *out_refs):
    rows = out_refs[0].shape[0]
    for t, ref in enumerate(out_refs):
        at = slice(t * rows, (t + 1) * rows)
        ref[...] = (near_ref[at, :].astype(F32) + far_ref[at, :].astype(F32)).astype(BF)


def scatter_pieces(near, far):
    chips = axis_total(CHIPS)
    got = hop(far, CORES, 1)
    rows = near.shape[0] // chips
    pair = vmem_call(pair_kernel, [sds((rows, near.shape[1]), BF)] * chips, near, got)
    return swap_parts(pair, CHIPS)


def sum_refs(refs):
    return tree_sum([ref[...].astype(F32) for ref in refs])


def pack_rows(inputs, out_grad, depth_counts, me, mine, share):
    depth = inputs.shape[0]
    counts = lax.dynamic_slice_in_dim(depth_counts, mine * share, share, 0)
    live = (jnp.arange(depth)[:, None] < counts[None, :]).astype(BF)
    live = jnp.broadcast_to(live[:, None, :, None], (depth, 2, share, 128))
    rows = [lax.dynamic_slice_in_dim(v, mine * share, share, 1) for v in (inputs, out_grad)]
    sent = jnp.concatenate([jnp.stack(rows, 1), live], -1)
    return [take(sent, me ^ t) for t in range(depth)]


def unpack_kernel(depth, me_ref, *refs):
    got = refs[:depth]
    gain_ref, rows_ref, grad_ref, mask_ref, normed_ref, masked_ref = refs[depth:]
    share, wide = got[0].shape[1:]
    model = rows_ref.shape[1]
    for t in range(depth):
        at = pl.ds(pl.multiple_of((me_ref[0] ^ t) * share, share), share)
        rows_ref[at, :] = got[t][0, :, :model].astype(F32)
        grad_ref[at, :] = got[t][1, :, :model].astype(F32)
        mask_ref[at, :] = got[t][0, :, model:].astype(F32)
    normed_ref[...] = rms_forward(rows_ref[...], gain_ref[0:1, :])[2]
    masked_ref[...] = (mask_ref[:, :1] * grad_ref[...]).astype(BF)


def unpack_rows(got, gains, me):
    depth = len(got)
    share, wide = got[0].shape[1:]
    shape = (depth * share, wide - 128)
    return vmem_call(
        functools.partial(unpack_kernel, depth),
        [sds(shape, F32), sds(shape, F32), sds((shape[0], 128), F32), sds(shape, BF), sds(shape, BF)],
        *got,
        gains,
        index=me,
    )


def project_kernel(width, parts, *refs):
    me_ref = refs[0]
    pieces = refs[1 : 1 + parts]
    w_ref = refs[1 + parts]
    normed_ref = refs[2 + parts]
    out_refs = refs[3 + parts : -1]
    all_ref = refs[-1]
    stack_kernel(*pieces, normed_ref)
    depth, rows, _ = all_ref.shape
    weights = w_ref[:, : 3 * width]
    for c in range(depth):
        all_ref[c] = mm(normed_ref[c * rows : (c + 1) * rows, :], weights).astype(BF)
    for t, ref in enumerate(out_refs):
        ref[...] = all_ref[me_ref[0] ^ t]


def project(pieces, attn_w, width, me, depth):
    tokens = sum(p.shape[0] for p in pieces)
    rows = tokens // depth
    out = vmem_call(
        functools.partial(project_kernel, width, len(pieces)),
        [sds((tokens, attn_w.shape[0]), BF)] + [sds((rows, 3 * width), BF)] * depth,
        *pieces,
        attn_w,
        index=me,
        scratch=[pltpu.VMEM((depth, rows, 3 * width), BF)],
        flops=6 * tokens * width * attn_w.shape[0],
    )
    return out[0], out[1:]


def attend_kernel(depth, me_ref, *refs):
    got = refs[:depth]
    outs = refs[depth : 2 * depth]
    qkv, ctx = refs[2 * depth :]
    width = ctx.shape[-1]
    for t in range(depth):
        qkv[me_ref[0] ^ t] = got[t][...]
    q, k, v = ([qkv[p, :, j * width : (j + 1) * width] for p in range(depth)] for j in range(3))
    context, _ = attend(q, k, v)
    for p in range(depth):
        ctx[p] = context[p]
    for t in range(depth):
        outs[t][...] = ctx[me_ref[0] ^ t]


def attend_pieces(got, me):
    depth = len(got)
    rows, wide = got[0].shape
    return vmem_call(
        functools.partial(attend_kernel, depth),
        [sds((rows, wide // 3), BF)] * depth,
        *got,
        index=me,
        scratch=[pltpu.VMEM((depth, rows, wide), BF), pltpu.VMEM((depth, rows, wide // 3), BF)],
        flops=depth * rows * wide * 60,
    )


def attend_back_kernel(depth, me_ref, *refs):
    got = refs[:depth]
    got_context = refs[depth : 2 * depth]
    outs = refs[2 * depth : 3 * depth]
    qkv, ctx = refs[3 * depth :]
    width = ctx.shape[-1]
    for t in range(depth):
        qkv[me_ref[0] ^ t] = got[t][...]
        ctx[me_ref[0] ^ t] = got_context[t][...]
    q, k, v = ([qkv[p, :, j * width : (j + 1) * width] for p in range(depth)] for j in range(3))
    _, probs = attend(q, k, v)
    grads = attend_back(q, k, v, probs, [ctx[p] for p in range(depth)])
    for p in range(depth):
        for j in range(3):
            qkv[p, :, j * width : (j + 1) * width] = grads[j][p]
    for t in range(depth):
        outs[t][...] = qkv[me_ref[0] ^ t]


def attend_back_pieces(got, got_context, me):
    depth = len(got)
    rows, wide = got[0].shape
    return vmem_call(
        functools.partial(attend_back_kernel, depth),
        [sds((rows, wide), BF)] * depth,
        *got,
        *got_context,
        index=me,
        scratch=[pltpu.VMEM((depth, rows, wide), BF), pltpu.VMEM((depth, rows, wide // 3), BF)],
        flops=depth * rows * wide * 100,
    )


def attn_out_kernel(depth, width, me_ref, *refs):
    got = refs[:depth]
    w_ref = refs[depth]
    ctx_ref, near_ref, far_ref = refs[depth + 1 : depth + 4]
    by_chunk = refs[depth + 4]
    for t in range(depth):
        by_chunk[me_ref[0] ^ t] = got[t][...]
    rows = by_chunk.shape[1]
    half = depth // 2
    for c in range(depth):
        ctx_ref[c * rows : (c + 1) * rows, :] = by_chunk[c]
        out = near_ref if c < half else far_ref
        at = (c % half) * rows
        out[at : at + rows, :] = mm_nt(by_chunk[c], w_ref[:, 3 * width :]).astype(BF)


def attn_out_terms(got, attn_w, me):
    depth = len(got)
    rows, width = got[0].shape
    model = attn_w.shape[0]
    tokens = depth * rows
    return vmem_call(
        functools.partial(attn_out_kernel, depth, width),
        [sds((tokens, width), BF)] + [sds((tokens // 2, model), BF)] * 2,
        *got,
        attn_w,
        index=me,
        scratch=[pltpu.VMEM((depth, rows, width), BF)],
        flops=2 * tokens * width * model,
    )


def join_kernel(chips, *refs):
    terms = refs[:chips]
    rows_ref, mask_ref, gain_ref = refs[chips : chips + 3]
    hidden_ref, normed_ref = refs[chips + 3 :]
    hidden = rows_ref[...] + mask_ref[:, :1] * sum_refs(terms)
    hidden_ref[...] = hidden
    normed_ref[...] = rms_forward(hidden, gain_ref[1:2, :])[2]


def join_rows(terms, rows_in, mask, gains):
    shape = rows_in.shape
    return vmem_call(
        functools.partial(join_kernel, len(terms)),
        [sds(shape, F32), sds(shape, BF)],
        *terms,
        rows_in,
        mask,
        gains,
    )


def norm_back_kernel(chips, _, *refs):
    terms = refs[:chips]
    rows_ref, grad_ref, mask_ref, gain_ref = refs[chips : chips + 4]
    out_ref, masked_ref, gain_out_ref = refs[chips + 4 :]
    grad_normed = sum_refs(terms)
    gain = gain_ref[1:2, :]
    unit_rows, inv_rms, _ = rms_forward(rows_ref[...], gain)
    grad = grad_ref[...] + rms_backward(grad_normed, unit_rows, inv_rms, gain)
    out_ref[...] = grad
    masked_ref[...] = (mask_ref[:, :1] * grad).astype(BF)
    gain_out_ref[...] = jnp.sum(grad_normed * unit_rows, axis=0, keepdims=True)


def norm_back(terms, rows, grad_rows, mask, gains, index):
    shape = rows.shape
    return vmem_call(
        functools.partial(norm_back_kernel, len(terms)),
        [sds(shape, F32), sds(shape, BF), sds((1, shape[1]), F32)],
        *terms,
        rows,
        grad_rows,
        mask,
        gains,
        index=index,
    )


def finish_kernel(depth, chips, me_ref, *refs):
    terms, ffn_terms = refs[:chips], refs[chips : 2 * chips]
    totals, refs = refs[2 * chips : 2 * chips + 2], refs[2 * chips + 2 :]
    rows_ref, grad_ref, hidden_ref, mask_ref, gain_ref = refs[:5]
    outs, (output, input_grad) = refs[5:-2], refs[-2:]
    gain = gain_ref[0:1, :]
    unit_rows, inv_rms, _ = rms_forward(rows_ref[...], gain)
    grad = rms_backward(sum_refs(terms), unit_rows, inv_rms, gain)
    output[...] = (hidden_ref[...] + mask_ref[:, :1] * sum_refs(ffn_terms)).astype(BF)
    input_grad[...] = (grad_ref[...] + grad).astype(BF)
    total = totals[0][...] + totals[1][...]
    high = total.astype(BF)
    low = (total - high.astype(F32)).astype(BF)
    share, model = outs[0].shape[1:]
    count = total.shape[0]
    for t, ref in enumerate(outs):
        at = pl.ds(pl.multiple_of((me_ref[0] ^ t) * share, share), share)
        ref[0] = output[at, :]
        ref[1] = input_grad[at, :]
        ref[2] = jnp.zeros((share, model), BF)
        ref[2, :count, :] = high
        ref[2, 8 : 8 + count, :] = low


def finish_rows(terms, ffn_terms, totals, rows, grad_rows, hidden, mask, gains, me, depth):
    tokens, model = rows.shape
    return vmem_call(
        functools.partial(finish_kernel, depth, len(terms)),
        [sds((3, tokens // depth, model), BF)] * depth,
        *terms,
        *ffn_terms,
        *totals,
        rows,
        grad_rows,
        hidden,
        mask,
        gains,
        index=me,
        scratch=[pltpu.VMEM((tokens, model), BF)] * 2,
        vmem=56,
    )


def by_position_kernel(depth, me_ref, *refs):
    rows_ref, total_ref = refs[depth:]
    count = total_ref.shape[0]
    parts = []
    for t in range(depth):
        rows_ref[me_ref[0] ^ t] = refs[t][:2]
        high, low = refs[t][2, :count, :], refs[t][2, 8 : 8 + count, :]
        parts.append(high.astype(F32) + low.astype(F32))
    total_ref[...] = tree_sum(parts)


def by_position(got, me, count):
    depth = len(got)
    _, share, model = got[0].shape
    return vmem_call(
        functools.partial(by_position_kernel, depth),
        [sds((depth, 2, share, model), BF), sds((count, model), F32)],
        *got,
        index=me,
    )


def whole_frames_kernel(parts, me_ref, *refs):
    share = refs[0].shape[2]
    for t in range(parts):
        at = pl.ds(pl.multiple_of((me_ref[0] ^ t) * share, share), share)
        for p in range(refs[0].shape[0]):
            for j in range(2):
                refs[parts + j][p, at, :] = refs[t][p, j]


def whole_frames(got, me):
    depth, _, share, model = got[0].shape
    return vmem_call(
        functools.partial(whole_frames_kernel, len(got)),
        [sds((depth, len(got) * share, model), BF)] * 2,
        *got,
        index=me,
    )


def ffn_tile(x, g, w_ref, hidden):
    gate_up = mm(x, w_ref[:, : 2 * hidden])
    gate_pre = gate_up[:, :hidden]
    up_proj = gate_up[:, hidden:]
    sig = jax.nn.sigmoid(gate_pre)
    acts = (gate_pre * sig * up_proj).astype(BF)
    grad_act = mm(g, w_ref[:, 2 * hidden :])
    grad_gate = (grad_act * up_proj * sig * (1.0 + gate_pre * (1.0 - sig))).astype(BF)
    grad_up = (grad_act * gate_pre * sig).astype(BF)
    return acts, grad_gate, grad_up


def ffn_kernel(x_ref, g_ref, w_ref, acts_ref, grads_ref, near_ref, far_ref):
    hidden = w_ref.shape[1] // 3
    half = near_ref.shape[0]
    for j, out_ref in enumerate((near_ref, far_ref)):
        at = slice(j * half, (j + 1) * half)
        acts, grad_gate, grad_up = ffn_tile(x_ref[at, :], g_ref[at, :], w_ref, hidden)
        acts_ref[at, :] = acts
        grads_ref[at, :hidden] = grad_gate
        grads_ref[at, hidden:] = grad_up
        out_ref[...] = mm_nt(grads_ref[at, :], w_ref[:, : 2 * hidden]).astype(BF)


def ffn_block(normed, grad_ffn, ffn_w):
    tokens, model = normed.shape
    hidden = ffn_w.shape[1] // 3
    return vmem_call(
        ffn_kernel,
        [sds((tokens, hidden), BF), sds((tokens, 2 * hidden), BF)]
        + [sds((tokens // 2, model), BF)] * 2,
        normed,
        grad_ffn,
        ffn_w,
        flops=10 * tokens * hidden * model,
    )


def weight_grad_kernel(count, *refs):
    out_ref, square_ref = refs[2 * count :]
    total = jnp.zeros((1, 128), F32)
    lane = 0
    for i in range(count):
        left, right = refs[2 * i], refs[2 * i + 1]
        width = right.shape[1]
        grads = mm_tn(left[...], right[...])
        out_ref[:, lane : lane + width] = grads.astype(BF)
        squares = jnp.sum(grads * grads, axis=0, keepdims=True)
        for j in range(0, width, 128):
            total = total + squares[:, j : j + 128]
        lane += width

    @pl.when(pl.program_id(0) == 0)
    def _():
        square_ref[...] = total

    @pl.when(pl.program_id(0) > 0)
    def _():
        square_ref[...] += total


def weight_grads(*pairs):
    owners = axis_total(OWNERS)
    tokens, model = pairs[0][0].shape
    widths = [last - first for _, _, first, last in pairs]
    width = sum(widths)
    if lax.axis_size("rf") > 1 or any(w % 128 for w in widths):
        grads = [mm_tn(left, right[:, first:last]) for left, right, first, last in pairs]
        grads = jnp.concatenate(grads, 1)
        if lax.axis_size("rf") > 1:
            grads = grads.reshape(lax.axis_size("pz"), lax.axis_size("rf"), -1, width)
            grads = lax.psum_scatter(grads, "rf", scatter_dimension=1)
        squares = jnp.sum((grads * grads).reshape(-1, 128), axis=0, keepdims=True)
        return grads.astype(BF).reshape(owners, -1, width), squares
    step = 512
    in_specs = []
    for (_, _, first, _), w in zip(pairs, widths):
        in_specs.append(pl.BlockSpec((tokens, step), lambda i: (0, i)))
        in_specs.append(pl.BlockSpec((tokens, w), lambda i, at=first // w: (0, at)))
    out, squares = pl.pallas_call(
        functools.partial(weight_grad_kernel, len(pairs)),
        out_shape=[sds((model, width), BF), sds((1, 128), F32)],
        grid=(model // step,),
        in_specs=in_specs,
        out_specs=[
            pl.BlockSpec((step, width), lambda i: (i, 0)),
            pl.BlockSpec((1, 128), lambda i: (0, 0)),
        ],
        compiler_params=pltpu.CompilerParams(vmem_limit_bytes=VMEM_LIMIT),
        cost_estimate=pl.CostEstimate(
            flops=2 * tokens * model * width,
            bytes_accessed=2 * (tokens * (2 * model + width) + model * width),
            transcendentals=0,
        ),
        name="weight_grads",
    )(*[v for left, right, _, _ in pairs for v in (left, right)])
    return out.reshape(owners, -1, width), squares


def context_kernel(depth, width, *refs):
    me_ref = refs[0]
    parts = len(refs) - 4 - depth
    pieces = refs[1 : 1 + parts]
    w_ref = refs[1 + parts]
    rows_ref = refs[2 + parts]
    outs = refs[3 + parts : 3 + parts + depth]
    by_chunk = refs[-1]
    stack_kernel(*pieces, rows_ref)
    rows = by_chunk.shape[1]
    for c in range(depth):
        by_chunk[c] = mm(rows_ref[c * rows : (c + 1) * rows, :], w_ref[:, 3 * width :]).astype(BF)
    for t in range(depth):
        outs[t][...] = by_chunk[me_ref[0] ^ t]


def context_grads(pieces, attn_w, width, me, depth):
    tokens = sum(p.shape[0] for p in pieces)
    rows = tokens // depth
    out = vmem_call(
        functools.partial(context_kernel, depth, width),
        [sds((tokens, attn_w.shape[0]), BF)] + [sds((rows, width), BF)] * depth,
        *pieces,
        attn_w,
        index=me,
        scratch=[pltpu.VMEM((depth, rows, width), BF)],
        flops=2 * tokens * width * attn_w.shape[0],
    )
    return out[0], out[1:]


def qkv_back_kernel(depth, width, me_ref, *refs):
    got = refs[:depth]
    w_ref, normed_ref, gain_ref, rows_ref, near_ref, far_ref, gain_out_ref, by_chunk = refs[depth:]
    for t in range(depth):
        by_chunk[me_ref[0] ^ t] = got[t][...]
    rows = by_chunk.shape[1]
    half = depth // 2
    total = jnp.zeros(gain_out_ref.shape, F32)
    for c in range(depth):
        here = slice(c * rows, (c + 1) * rows)
        rows_ref[here, :] = by_chunk[c]
        out = near_ref if c < half else far_ref
        at = (c % half) * rows
        terms = mm_nt(by_chunk[c], w_ref[:, : 3 * width])
        out[at : at + rows, :] = terms.astype(BF)
        total = total + jnp.sum(terms * normed_ref[here, :].astype(F32), axis=0, keepdims=True)
    gain_out_ref[...] = total / gain_ref[0:1, :]


def qkv_back(got, attn_w, normed, gains, width, me):
    depth = len(got)
    rows = got[0].shape[0]
    tokens = depth * rows
    model = attn_w.shape[0]
    return vmem_call(
        functools.partial(qkv_back_kernel, depth, width),
        [sds((tokens, 3 * width), BF)]
        + [sds((tokens // 2, model), BF)] * 2
        + [sds((1, model), F32)],
        *got,
        attn_w,
        normed,
        gains,
        index=me,
        scratch=[pltpu.VMEM((depth, rows, 3 * width), BF)],
        flops=6 * tokens * width * model,
    )


def attn_grads_kernel(depth, width, me_ref, *refs):
    got = refs[:depth]
    w_ref, normed_ref, gain_ref, gain2_ref, square_ref = refs[depth : depth + 5]
    near_ref, far_ref, chunk_ref, total_ref, by_chunk, grads = refs[depth + 5 :]
    for t in range(depth):
        by_chunk[me_ref[0] ^ t] = got[t][...]
    rows = by_chunk.shape[1]
    half = depth // 2
    total = jnp.zeros(gain2_ref.shape, F32)
    for c in range(depth):
        here = slice(c * rows, (c + 1) * rows)
        grads[here, :] = by_chunk[c]
        out = near_ref if c < half else far_ref
        at = (c % half) * rows
        terms = mm_nt(by_chunk[c], w_ref[:, : 3 * width])
        out[at : at + rows, :] = terms.astype(BF)
        total = total + jnp.sum(terms * normed_ref[here, :].astype(F32), axis=0, keepdims=True)
    total_ref[0:1, :] = total / gain_ref[0:1, :]
    total_ref[1:2, :] = gain2_ref[...]
    chunk = mm_tn(normed_ref[...], grads[...])
    chunk_ref[...] = chunk.astype(BF)
    column = jnp.sum(chunk * chunk, axis=0, keepdims=True)
    squares = square_ref[...]
    for j in range(0, 3 * width, 128):
        squares = squares + column[:, j : j + 128]
    total_ref[2:3, :] = jnp.zeros(gain2_ref.shape, F32)
    total_ref[2:3, :128] = squares


def attn_grads(got, attn_w, normed, gains, gain_part2, squares, me):
    depth = len(got)
    rows, wide = got[0].shape
    width = wide // 3
    tokens = depth * rows
    model = attn_w.shape[0]
    if lax.axis_size("rf") > 1 or width % 128:
        grads, near, far, gain_part1 = qkv_back(got, attn_w, normed, gains, width, me)
        chunks, more = weight_grads((normed, grads, 0, wide))
        squares = jnp.pad(squares + more, ((0, 0), (0, model - 128)))
        return near, far, chunks, jnp.concatenate([gain_part1, gain_part2, squares], 0)
    near, far, chunks, total = vmem_call(
        functools.partial(attn_grads_kernel, depth, width),
        [sds((tokens // 2, model), BF)] * 2 + [sds((model, wide), BF), sds((3, model), F32)],
        *got,
        attn_w,
        normed,
        gains,
        gain_part2,
        squares,
        index=me,
        scratch=[pltpu.VMEM((depth, rows, wide), BF), pltpu.VMEM((tokens, wide), BF)],
        flops=12 * tokens * width * model,
        vmem=56,
    )
    return near, far, chunks.reshape(axis_total(OWNERS), -1, wide), total


OWNERS = ("pz", "rs")


def lanes_view(array):
    rows, kinds, depth, cols = array.shape
    split = array.reshape(rows, kinds, depth, cols // 128, 128)
    return split.transpose(0, 1, 3, 2, 4).reshape(-1, 128)


def lanes_back(view, shape):
    rows, kinds, depth, cols = shape
    split = view.reshape(rows, kinds, cols // 128, depth, 128)
    return split.transpose(0, 1, 3, 2, 4).reshape(shape)


def tiles_of(dims, pieces):
    kinds, tiles, depth, parts = dims
    per = tiles // parts
    for number, piece in enumerate(pieces):
        lane = 0
        for k, first, count in piece:
            if k is None:
                lane += 128 * count
                continue
            for t in range(first, first + count):
                for part in range(parts):
                    for p in range(depth):
                        at = (k * tiles + part * per + t) * depth + p
                        yield at, p * parts + part, number, lane
                lane += 128


def widths_of(pieces):
    return [128 * sum(count for _, _, count in piece) for piece in pieces]


def whole_message(kinds, cols):
    return [[(k, 0, cols // 128) for k in range(kinds)]]


def split_kernel(dims, pieces, w_ref, *out_refs):
    kinds, tiles, depth, _ = dims
    rows = out_refs[0].shape[1]
    for at, chunk, number, lane in tiles_of(dims, pieces):
        values = w_ref[pl.ds(at, rows, stride=kinds * tiles * depth), :]
        out_refs[number][chunk, :, lane : lane + 128] = values.astype(BF)


def in_blocks(kernel, grid, in_specs, out_shape, out_specs, args, vmem, scalars=(), scratch=(), **more):
    n_in, n_out, n_scalar = len(in_specs), len(out_specs), len(scalars)

    def run(*refs):
        fixed = refs[:n_scalar]
        arrays = refs[n_scalar : n_scalar + n_in + n_out]
        held = refs[n_scalar + n_in + n_out :]
        pltpu.emit_pipeline(
            lambda *blocks: kernel(*fixed, *blocks, *held),
            grid=grid,
            in_specs=in_specs,
            out_specs=out_specs,
        )(*arrays)

    return pl.pallas_call(
        run,
        out_shape=out_shape,
        in_specs=[pl.BlockSpec(memory_space=pltpu.SMEM)] * n_scalar
        + [pl.BlockSpec(memory_space=pltpu.HBM)] * n_in,
        out_specs=[pl.BlockSpec(memory_space=pltpu.HBM)] * n_out,
        scratch_shapes=list(scratch),
        compiler_params=pltpu.CompilerParams(vmem_limit_bytes=vmem << 20),
        **more,
    )(*scalars, *args)


def split_weights(weights, vmem, pieces=None):
    rows, kinds, depth, cols = weights.shape
    parts = lax.axis_size("rs")
    if (cols // parts) % 128 or rows % 16:
        low = weights.astype(BF).reshape(rows, kinds, depth, parts, cols // parts)
        return [low.transpose(2, 3, 0, 1, 4).reshape(depth * parts, rows, -1)]
    pieces = pieces or whole_message(kinds, cols // parts)
    tiles = cols // 128
    step = math.gcd(rows, 32)
    chunks = depth * parts
    return in_blocks(
        functools.partial(split_kernel, (kinds, tiles, depth, parts), pieces),
        (rows // step,),
        [pl.BlockSpec((step * kinds * tiles * depth, 128), lambda i: (i, 0))],
        [sds((chunks, rows, w), BF) for w in widths_of(pieces)],
        [pl.BlockSpec((chunks, step, w), lambda i: (0, i, 0)) for w in widths_of(pieces)],
        [lanes_view(weights)],
        vmem=vmem,
        cost_estimate=pl.CostEstimate(
            flops=weights.size, bytes_accessed=6 * weights.size, transcendentals=0
        ),
        name="split_weights",
    )


def to_planes(low):
    full = lax.all_to_all(low, OWNERS, 0, 0, tiled=True)
    if lax.axis_size("rf") > 1:
        full = full.reshape((lax.axis_size("pz"), lax.axis_size("rs")) + full.shape[1:])
        full = lax.all_gather(full, "rf", axis=1)
    return full.reshape(-1, full.shape[-1])


def to_owners(chunks):
    return lax.all_to_all(chunks, OWNERS, 0, 0, tiled=True)


def adamw_update(weights, first, second, grads, clip_factor, decay_rate, step_rate):
    clipped = clip_factor * grads
    first_new = BETA_ONE * first + (1.0 - BETA_ONE) * clipped
    second_new = BETA_TWO * second + (1.0 - BETA_TWO) * clipped * clipped
    first_hat = first_new * (1.0 / (1.0 - BETA_ONE**STEP))
    second_hat = second_new * (1.0 / (1.0 - BETA_TWO**STEP))
    new_weights = weights - step_rate * (
        first_hat / (jnp.sqrt(second_hat) + ADAM_EPS) + decay_rate * weights
    )
    return (new_weights, first_new, second_new)


def norm_of(total):
    sums = jnp.sum(total[:2] * total[:2], axis=0, keepdims=True) + total[2:3]
    return jnp.sqrt(jnp.sum(sums, axis=1, keepdims=True))


def adamw_kernel(dims, pieces, steps, stages, total_from, *refs):
    kinds, tiles, depth, _ = dims
    n = len(pieces)
    g_refs, state, refs = refs[:n], refs[n : n + 3], refs[n + 3 :]
    stage_refs, new_refs, staged_refs = refs[:stages], refs[stages : stages + 3], refs[stages + 3 :]
    staged_refs, refs = staged_refs[:stages], staged_refs[stages:]
    g_held, refs = refs[:n], refs[n:]
    here = len(refs) == 7
    state_held, refs = (state, refs) if here else (refs[:3], refs[3:])
    new_held, grads, total_ref, in_sems, out_sems = refs[:3], *refs[3:]
    rows, units, _ = grads.shape
    count = rows * units
    places = {at: (number, chunk, lane) for at, chunk, number, lane in tiles_of(dims, pieces)}

    def fetches(i):
        some = pl.ds(pl.multiple_of(i * rows, rows), rows)
        pairs = [(g.at[:, some, :], held.at[:, some, :]) for g, held in zip(g_refs, g_held)]
        if not here:
            some = pl.ds(pl.multiple_of(i * count, count), count)
            pairs += [(v.at[some, :], held.at[some, :]) for v, held in zip(state, state_held)]
        return [pltpu.make_async_copy(*pair, in_sems.at[i, j]) for j, pair in enumerate(pairs)]

    def stores(i):
        some = pl.ds(pl.multiple_of(i * count, count), count)
        pairs = [(held.at[some, :], new.at[some, :]) for held, new in zip(new_held, new_refs)]
        return [pltpu.make_async_copy(*pair, out_sems.at[i, j]) for j, pair in enumerate(pairs)]

    staging = [
        pltpu.make_async_copy(source, to, out_sems.at[steps, j])
        for j, (source, to) in enumerate(zip(stage_refs, staged_refs))
    ]

    summed = pltpu.make_async_copy(total_from, total_ref, out_sems.at[steps, stages])
    summed.start()

    @pl.loop(0, steps)
    def _(i):
        for copy in fetches(i):
            copy.start()

    for copy in staging:
        copy.start()
    summed.wait()
    clip = CLIP_NORM / jnp.maximum(norm_of(total_ref[...]), CLIP_NORM)

    @pl.loop(0, steps)
    def _(i):
        for copy in fetches(i):
            copy.wait()
        some = pl.ds(pl.multiple_of(i * rows, rows), rows)
        for first in range(0, units, 8):
            tile = [
                g_held[number][chunk, some, lane : lane + 128].astype(F32)
                for number, chunk, lane in (places[at] for at in range(first, first + 8))
            ]
            grads[:, first : first + 8, :] = jnp.swapaxes(jnp.stack(tile), 0, 1)

        @pl.loop(0, rows)
        def _(row):
            at = pl.ds(pl.multiple_of(i * count + row * units, units), units)
            new = adamw_update(
                *(held[at, :] for held in state_held), grads[row], clip, WEIGHT_DECAY, LEARN_RATE
            )
            for held, values in zip(new_held, new):
                held[at, :] = values

        for copy in stores(i):
            copy.start()

    @pl.loop(0, steps)
    def _(i):
        for copy in stores(i):
            copy.wait()

    for copy in staging:
        copy.wait()


def adamw_owned(state, chunks, total, shape, pieces=None, stage=(), here=False):
    rows, kinds, depth, cols = shape
    parts = lax.axis_size("rs")
    pieces = pieces or whole_message(kinds, cols // parts)
    units = kinds * cols // 128 * depth
    step = math.gcd(rows, 16)
    steps = rows // step
    anywhere = pl.BlockSpec(memory_space=pl.ANY)
    inside = pl.BlockSpec(memory_space=pltpu.VMEM)
    view = state[0].shape
    out = pl.pallas_call(
        functools.partial(
            adamw_kernel, (kinds, cols // 128, depth, parts), pieces, steps, len(stage)
        ),
        out_shape=[sds(view, F32)] * 3 + [sds(v.shape, F32) for v in stage],
        in_specs=[anywhere] * (1 + len(chunks))
        + [inside if here else anywhere] * 3
        + [anywhere] * len(stage),
        out_specs=[anywhere] * 3 + [inside] * len(stage),
        scratch_shapes=[pltpu.VMEM(v.shape, BF) for v in chunks]
        + [pltpu.VMEM(view, F32)] * (3 if here else 6)
        + [pltpu.VMEM((step, units, 128), F32), pltpu.VMEM(total.shape, F32)]
        + [pltpu.SemaphoreType.DMA((steps, len(chunks) + 3))]
        + [pltpu.SemaphoreType.DMA((steps + 1, 4))],
        compiler_params=pltpu.CompilerParams(vmem_limit_bytes=(20 if here else 52) << 20),
        cost_estimate=pl.CostEstimate(
            flops=20 * math.prod(shape), bytes_accessed=26 * math.prod(shape), transcendentals=0
        ),
        name="adamw",
    )(total, *chunks, *state, *stage)
    return out[:3], out[3:]


def gains_kernel(total_ref, w_ref, m_ref, v_ref, norm_ref, *new_refs):
    norm = norm_of(total_ref[...])
    norm_ref[...] = norm
    clip = CLIP_NORM / jnp.maximum(norm, CLIP_NORM)
    new = adamw_update(
        w_ref[...], m_ref[...], v_ref[...], total_ref[0:2, :], clip, 0.0, GAIN_RATE
    )
    for ref, values in zip(new_refs, new):
        ref[...] = values


def update_gains(total, state):
    return vmem_call(
        gains_kernel, [sds((1, 1), F32)] + [sds(v.shape, F32) for v in state], total, *state
    )


def body(
    inputs,
    depth_counts,
    out_grad,
    attn_weight,
    attn_first,
    attn_second,
    ffn_weight,
    ffn_first,
    ffn_second,
    norm_gains,
    gain_first,
    gain_second,
):
    depth, frames, model = inputs.shape
    mp_axes = ("mx", "mc")
    share = frames // axis_total(mp_axes)

    me = lax.axis_index("pz")
    positions = ("pz",)
    per = ffn_weight.shape[3] // lax.axis_size("rs") // 128
    packed = pack_rows(inputs, out_grad, depth_counts, me, linear_index(mp_axes), share)
    packed = swap_parts(packed, positions)
    attn_low = split_weights(attn_weight, 48)[0]
    rows_in, rows_grad, mask, normed1_rows, masked = unpack_rows(packed, norm_gains, me)
    attn_w = to_planes(after(attn_low, mask))
    ffn_low = split_weights(ffn_weight, 48)[0]
    width = attn_w.shape[1] // 4
    normed1_pieces = gather_pieces(normed1_rows)
    grad_ffn = stack_rows(gather_pieces(masked))

    normed1, qkv = project(normed1_pieces, attn_w, width, me, depth)
    qkv = swap_parts(qkv, positions)
    context = swap_parts(attend_pieces(qkv, after(me.reshape(1), ffn_low)), positions)
    ffn_w = to_planes(after(ffn_low, *context[1:]))
    context, near, far = attn_out_terms(context, attn_w, me)
    hidden_in, normed2_rows = join_rows(scatter_pieces(near, far), rows_in, mask, norm_gains)
    normed2 = stack_rows(gather_pieces(normed2_rows))

    acts, gate_up_grads, near, far = ffn_block(normed2, grad_ffn, ffn_w)
    terms = scatter_pieces(near, far)
    hidden = acts.shape[1]
    pieces = [[(0, 0, per), (1, 0, per)], [(2, 0, per), (None, 0, width // 128)]]
    chunks_a, squares_a = weight_grads((normed2, gate_up_grads, 0, 2 * hidden))
    owned_a = to_owners(chunks_a)
    ffn_terms = mm_nt(acts, ffn_w[:, 2 * hidden :]).astype(BF)

    grad_hidden, masked, gain_part2 = norm_back(
        terms, hidden_in, rows_grad, mask, norm_gains, after(me.reshape(1), ffn_terms)
    )
    grad_attn, grad_context = context_grads(gather_pieces(masked), attn_w, width, me, depth)
    grad_context = swap_parts(grad_context, positions)
    grad_qkv = swap_parts(attend_back_pieces(qkv, grad_context, me), positions)
    half = ffn_terms.shape[0] // 2
    ffn_terms = scatter_pieces(ffn_terms[:half], ffn_terms[half:])
    chunks_b, squares_b = weight_grads((grad_ffn, acts, 0, hidden), (grad_attn, context, 0, width))
    owned_b = to_owners(after(chunks_b, *grad_qkv[1:], *ffn_terms[1:]))
    near, far, attn_chunks, total = attn_grads(
        grad_qkv,
        attn_w,
        normed1,
        norm_gains,
        gain_part2,
        squares_a + squares_b,
        after(me.reshape(1), owned_a),
    )
    terms = scatter_pieces(near, far)

    if lax.axis_size("rf") > 1:
        total = lax.psum(total, "rf")
    total = all_sum(total, mp_axes)
    totals = [total] + [hop(total, ("rs",), t) for t in range(1, lax.axis_size("rs"))]
    if len(totals) != 2:
        totals = [tree_sum(totals), jnp.zeros_like(total)]
    back = finish_rows(
        terms, ffn_terms, totals, rows_in, grad_hidden, hidden_in, mask, norm_gains, me, depth
    )

    back, total = by_position(swap_parts(back, positions), me, total.shape[0])
    attn_owned = to_owners(after(attn_chunks, total))
    back = swap_parts([back] * axis_total(mp_axes), mp_axes)
    output, input_grad = whole_frames(back, linear_index(mp_axes))

    ffn_state = [lanes_view(v) for v in (ffn_weight, ffn_first, ffn_second)]
    attn_state = [lanes_view(v) for v in (attn_weight, attn_first, attn_second)]
    ffn_new, _ = adamw_owned(ffn_state, [owned_a, owned_b], total, ffn_weight.shape, pieces)
    grad_norm, *gain_new = update_gains(total, [norm_gains, gain_first, gain_second])
    if width % 128:
        grads = jnp.concatenate([attn_owned, owned_b[:, :, hidden:]], -1)
        grads = grads.reshape(depth, lax.axis_size("rs"), -1, 4, width)
        grads = grads.transpose(2, 3, 0, 1, 4).reshape(attn_weight.shape).astype(F32)
        clip_factor = CLIP_NORM / jnp.maximum(grad_norm[0, 0], CLIP_NORM)
        attn_new = adamw_update(
            attn_weight, attn_first, attn_second, grads, clip_factor, WEIGHT_DECAY, LEARN_RATE
        )
    else:
        tiles = width // 128
        attn_pieces = [[(k, 0, tiles) for k in range(3)], [(None, 0, per), (3, 0, tiles)]]
        attn_new, _ = adamw_owned(
            attn_state,
            [attn_owned, owned_b],
            after(total, ffn_new[0], output),
            attn_weight.shape,
            attn_pieces,
        )
        attn_new = tuple(lanes_back(v, attn_weight.shape) for v in attn_new)
    ffn_new = tuple(lanes_back(v, ffn_weight.shape) for v in ffn_new)

    return (output, input_grad, grad_norm[0, 0]) + attn_new + ffn_new + tuple(gain_new)


def solution(mesh):
    dp = mesh.shape["dp"]
    mp = mesh.shape["mp"]

    def run(*args):
        depth, _, model = args[0].shape
        heads = args[3].shape[3] // mp // HD
        parts = math.gcd(dp // depth, heads)
        fine = Mesh(
            mesh.devices.reshape(depth, dp // depth // parts, parts, mp // 2, 2),
            ("pz", "rf", "rs", "mx", "mc"),
        )
        rows = ("pz", "rf", "rs")
        cols = ("mx", "mc")
        acts = P(None, rows, None)
        weight = P(rows, None, None, cols)
        return jax.shard_map(
            body,
            mesh=fine,
            in_specs=(acts, P(rows), acts) + (weight,) * 6 + (P(),) * 3,
            out_specs=(acts, acts, P()) + (weight,) * 6 + (P(),) * 3,
            check_vma=False,
        )(*args)

    return run
```
